32 devices in a mesh: segment: 2 (over core), seq: 16 (over z, y, x).
Axes of the slice: x: 2, y: 2, z: 4, core: 2. Of those that a mesh axis runs over, the one named last changes fastest.
Arguments:
- activations: bfloat16 [2, 4096, 768], P('segment', 'seq'), may hold values from -6 to 6
- short_filters: bfloat16 [2, 128, 768], replicated, may hold values from -0.5 to 0.5
- long_filters: float32 [2, 4096, 768], P('segment', 'seq'), may hold values from -4 to 4
- skip_gain: float32 [2, 768], replicated, may hold values from -1 to 1
Outputs:
- sections: bfloat16 [2, 4096, 768], P('segment', 'seq')
The draws below stay inside these ranges and needn't reach their ends.
All inputs are finite; a program needn't handle non-finite values.
Results may differ from the reference program's by a relative error of at most 0.012.
Values may be sent and summed in bfloat16 or wider, within the bound.
No kernel may reach another device: no remote copies, remote signals or barrier semaphores. Data moves between devices by JAX's collectives and lax.ppermute only.
A program may use at most 64 MiB of HBM per device.

```python
import math
import jax
import jax.numpy as jnp
from jax import lax

D = 768
COLS = 256
SHORT = 128
SECTIONS = 2
L = 4096
FFT_LEN = 8192
ROWS = 32


def draw_long_filters(key, part):
    rate_key = jax.random.fold_in(key, 11)
    noise_key = jax.random.fold_in(key, 23)
    rates = jnp.exp(jax.random.uniform(rate_key, (SECTIONS, 1, D), jnp.float32, math.log(0.25), math.log(64.0)))
    positions = jnp.arange(L, dtype=jnp.float32)[None, :, None] / L
    envelope = jnp.exp(-rates * positions)
    noise = jnp.clip(jax.random.normal(noise_key, (SECTIONS, L, D), jnp.float32), -4.0, 4.0)
    return noise * envelope


def block_scale(key, shape, cuts, low, top_value):
    def one(dim, shards_of):
        heights = jax.random.uniform(jax.random.fold_in(jax.random.fold_in(key, 6), dim), (shards_of,), jnp.float32, low / len(cuts), top_value / len(cuts))
        return jnp.repeat(jnp.exp(heights), shape[dim] // shards_of).reshape((-1,) + (1,) * (len(shape) - dim - 1))

    gain = one(*cuts[0])
    for cut in cuts[1:]:
        gain = gain * one(*cut)
    return gain


def bell_draw(stream_key, extent, width, bound, shards=(), held_as=jnp.bfloat16):
    gain = block_scale(stream_key, extent, shards, -0.22, 0.18) if shards else 1.0
    drawn = jax.random.normal(stream_key, extent, jnp.float32) * width * gain
    return jnp.minimum(jnp.maximum(drawn, -bound), bound).astype(held_as)


def setup_inputs(seed: int = 0) -> dict:
    splits = jax.random.split(jax.random.key(seed), 5)
    activations = bell_draw(splits[0], (SECTIONS, L, D), 1.0, 6.0, ((0, 2), (1, 16)))
    short_filters = bell_draw(splits[1], (SECTIONS, SHORT, D), SHORT ** -0.5, 0.5)
    long_filters = draw_long_filters(jax.random.fold_in(splits[4], 71), 0)
    skip_gain = jnp.clip(jax.random.uniform(splits[3], (SECTIONS, D), jnp.float32, -1.0, 1.0), -1.0, 1.0)
    return {"activations": activations, "short_filters": short_filters, "long_filters": long_filters, "skip_gain": skip_gain}


def row_table(grid_rows):
    real_rows = grid_rows // 2
    phases = (jnp.arange(grid_rows, dtype=jnp.int32)[:, None] * jnp.arange(real_rows, dtype=jnp.int32)[None, :] % grid_rows).astype(jnp.float32) * (2.0 * math.pi / grid_rows)
    return jnp.stack([jnp.cos(phases), -jnp.sin(phases)]).astype(jnp.bfloat16)

def back_row_table(grid_rows):
    real_rows = grid_rows // 2
    phases = (jnp.arange(real_rows, dtype=jnp.int32)[:, None] * jnp.arange(grid_rows, dtype=jnp.int32)[None, :] % grid_rows).astype(jnp.float32) * (2.0 * math.pi / grid_rows)
    return jnp.stack([jnp.cos(phases), -jnp.sin(phases)], axis=1).astype(jnp.bfloat16)

def column_table(width_cols, direction):
    phases = (jnp.arange(width_cols, dtype=jnp.int32)[:, None] * jnp.arange(width_cols, dtype=jnp.int32)[None, :] % width_cols).astype(jnp.float32) * (2.0 * math.pi / width_cols)
    cosine = jnp.cos(phases)
    sine_part = direction * jnp.sin(phases)
    return jnp.stack([jnp.stack([cosine, -sine_part], axis=1), jnp.stack([sine_part, cosine], axis=1)]).astype(jnp.bfloat16)

def twiddle(freq_index, col_index, fft_len):
    phases = (freq_index[:, None] * col_index[None, :] % fft_len).astype(jnp.float32) * (2.0 * math.pi / fft_len)
    return (jnp.cos(phases)[:, :, None], jnp.sin(phases)[:, :, None])

def complex_times(left, right):
    return jnp.stack([left[0] * right[0] - left[1] * right[1], left[0] * right[1] + left[1] * right[0]])

def short_conv(padded, tap_block):
    kernel = tap_block[::-1].astype(jnp.float32)[:, None, :]
    result = lax.conv_general_dilated(padded.astype(jnp.float32)[None], kernel, (1,), 'VALID', dimension_numbers=('NWC', 'WIO', 'NWC'), feature_group_count=tap_block.shape[1], precision=lax.Precision.HIGHEST)
    return result[0].astype(jnp.bfloat16)

def whole_forward(signal):
    token_grid = signal.reshape(ROWS // 2, COLS, signal.shape[1])
    first_pass = jnp.einsum('pka,abw->pkbw', row_table(ROWS).astype(jnp.float32), token_grid.astype(jnp.float32), precision=lax.Precision.HIGHEST)
    cosine, sine_part = twiddle(jnp.arange(ROWS, dtype=jnp.int32), jnp.arange(COLS, dtype=jnp.int32), FFT_LEN)
    turned = jnp.stack([first_pass[0] * cosine + first_pass[1] * sine_part, first_pass[1] * cosine - first_pass[0] * sine_part]).astype(jnp.bfloat16)
    return jnp.einsum('qdpb,pkbw->qkdw', column_table(COLS, -1.0).astype(jnp.float32), turned.astype(jnp.float32), precision=lax.Precision.HIGHEST)

def whole_inverse(product):
    back_cols = jnp.einsum('qdpb,pkbw->qkdw', column_table(COLS, 1.0).astype(jnp.float32), product.astype(jnp.float32), precision=lax.Precision.HIGHEST)
    cosine, sine_part = twiddle(jnp.arange(ROWS, dtype=jnp.int32), jnp.arange(COLS, dtype=jnp.int32), FFT_LEN)
    turned = jnp.stack([back_cols[0] * cosine - back_cols[1] * sine_part, back_cols[0] * sine_part + back_cols[1] * cosine]).astype(jnp.bfloat16)
    rows_out = jnp.einsum('apk,pkbw->abw', back_row_table(ROWS).astype(jnp.float32), turned.astype(jnp.float32), precision=lax.Precision.HIGHEST)
    scale = 1.0 / (FFT_LEN * math.sqrt(L))
    return (rows_out * scale).astype(jnp.bfloat16).reshape(L, product.shape[3])

def section_whole(signal, tap_block, filter_block, gain_block):
    padded = jnp.concatenate([jnp.zeros((SHORT - 1, signal.shape[1]), jnp.bfloat16), signal], axis=0)
    filtered_short = short_conv(padded, tap_block)
    spectrum = whole_forward(filter_block.astype(jnp.bfloat16))
    signal_spec = whole_forward(filtered_short)
    product = complex_times(signal_spec, spectrum).astype(jnp.bfloat16)
    filtered_long = whole_inverse(product)
    return (filtered_long.astype(jnp.float32) + gain_block[None, :] * filtered_short.astype(jnp.float32)).astype(jnp.bfloat16)

def reference(activations, short_filters, long_filters, skip_gain):
    block_width = math.gcd(D, 64)
    block_count = D // block_width

    def to_blocks(array):
        return jnp.moveaxis(array.reshape(array.shape[:-1] + (block_count, block_width)), -2, 0)

    def from_blocks(array):
        return jnp.moveaxis(array, 0, -2).reshape(array.shape[1:-1] + (D,))

    def run_whole(section_index, signal):

        def process(pieces):
            return section_whole(pieces[0], pieces[1], pieces[2], pieces[3])
        outputs = lax.map(process, (to_blocks(signal), to_blocks(short_filters[section_index]), to_blocks(long_filters[section_index]), to_blocks(skip_gain[section_index])))
        return from_blocks(outputs)
    first_out = run_whole(0, activations[0])
    gated = (first_out.astype(jnp.float32) * activations[1].astype(jnp.float32)).astype(jnp.bfloat16)
    second_out = run_whole(1, gated)
    return jnp.stack([first_out, second_out])
```

```python
import functools
import math

import jax
import jax.numpy as jnp
import numpy as np
from jax import lax
from jax.experimental import pallas as pl
from jax.experimental.pallas import tpu as pltpu
from jax.sharding import PartitionSpec as P

BOTH = ("segment", "seq")
LANES = 8


def tables(real_rows, cols):
    grid_rows = 2 * real_rows + 1
    length = grid_rows * cols
    freqs = real_rows + 1
    padded = freqs + freqs % 2
    k = np.arange(freqs)
    rows = 2.0 * math.pi * ((k[:, None] * np.arange(real_rows)[None, :]) % grid_rows) / grid_rows
    first = np.zeros((2, padded, real_rows))
    first[0, :freqs], first[1, :freqs] = np.cos(rows), -np.sin(rows)
    eye = np.eye(LANES)
    forward_rows = np.kron(first.reshape(2 * padded, real_rows), eye)
    back_rows = np.kron(first.reshape(2 * padded, real_rows).T, eye)
    b = np.arange(cols)
    turn = np.zeros((2, padded, cols))
    angle = 2.0 * math.pi * (k[:, None] * b[None, :]) / length
    turn[0, :freqs], turn[1, :freqs] = np.cos(angle), np.sin(angle)
    turn = np.repeat(turn, LANES, axis=1)
    grid = 2.0 * math.pi * ((b[:, None] * b[None, :]) % cols) / cols
    c, s = np.cos(grid), np.sin(grid)
    forward_cols = np.block([[c, -s], [s, c]])
    back_cols = np.block([[c, s], [-s, c]])
    bf = jnp.bfloat16
    return (
        jnp.asarray(forward_rows, bf),
        jnp.asarray(back_rows, bf),
        jnp.asarray(turn, jnp.float32),
        jnp.asarray(forward_cols, bf),
        jnp.asarray(back_cols, bf),
    )


def dot(a, b):
    return jnp.dot(a, b, preferred_element_type=jnp.float32)


def send_kernel(width, act_ref, filt_ref, out_ref):
    act = act_ref[0].astype(jnp.float32).T
    filt = filt_ref[0].T
    for d in range(out_ref.shape[0]):
        part = slice(d * width, (d + 1) * width)
        out_ref[d] = jnp.concatenate([act[part], filt[part]], axis=0).astype(jnp.bfloat16)


def final_kernel(in_ref, out_ref):
    blocks = in_ref[...].astype(jnp.float32)
    n, double, half = blocks.shape
    width = double // 2
    low = blocks[:, :width].reshape(n * width, half)
    high = blocks[:, width:].reshape(n * width, half)
    out_ref[0] = jnp.concatenate([low, high], axis=1).T.astype(jnp.bfloat16)


def main_kernel(
    width, owned, place_ref, in_ref, taps_ref, gain_ref, fr_ref, br_ref, turn_ref, fc_ref, bc_ref, out_ref
):
    sections = taps_ref.shape[0]
    rows = in_ref.shape[0] // sections
    cols = in_ref.shape[2]
    groups = width // LANES
    cosine, sine = turn_ref[0], turn_ref[1]
    high = cosine.shape[0]
    length = (2 * rows + 1) * cols
    bf = jnp.bfloat16
    channels = taps_ref.shape[2]
    mine = lax.broadcasted_iota(jnp.int32, (width, channels), 0)
    them = lax.broadcasted_iota(jnp.int32, (width, channels), 1)
    pick = jnp.where((them == mine + place_ref[0] * owned) & (mine < owned), 1.0, 0.0)
    all_cos = jnp.concatenate([cosine] * groups, axis=0)
    all_sin = jnp.concatenate([sine] * groups, axis=0)
    weight = jnp.where(
        lax.broadcasted_iota(jnp.int32, (high, 1), 0) < LANES, 1.0 / length, 2.0 / length
    )
    all_weight = jnp.concatenate([weight] * groups, axis=0)

    def forward(grid):
        reals, imags = [], []
        for g in range(groups):
            block = grid[:, g * LANES : (g + 1) * LANES].reshape(rows * LANES, cols).astype(bf)
            spread = dot(fr_ref[...], block)
            reals.append(spread[:high])
            imags.append(spread[high:])
        real = jnp.concatenate(reals, axis=0)
        imag = jnp.concatenate(imags, axis=0)
        turned = jnp.concatenate(
            [real * all_cos + imag * all_sin, imag * all_cos - real * all_sin], axis=1
        ).astype(bf)
        return dot(turned, fc_ref[...])

    def times(left, right):
        lr, li = left[:, :cols], left[:, cols:]
        rr, ri = right[:, :cols], right[:, cols:]
        return jnp.concatenate([lr * rr - li * ri, lr * ri + li * rr], axis=1)

    def back(product):
        flat = dot(product.astype(bf), bc_ref[...])
        real, imag = flat[:, :cols], flat[:, cols:]
        turned_real = (real * all_cos - imag * all_sin).astype(bf)
        turned_imag = (real * all_sin + imag * all_cos).astype(bf)
        pieces = []
        for g in range(groups):
            part = slice(g * high, (g + 1) * high)
            both = jnp.concatenate([turned_real[part], turned_imag[part]], axis=0)
            pieces.append(dot(br_ref[...], both).reshape(rows, LANES, cols))
        return jnp.concatenate(pieces, axis=1)

    combined = []
    for s in range(sections):
        chunk = in_ref[s * rows : (s + 1) * rows].astype(jnp.float32)
        long_spec = forward(chunk[:, width:])
        taps = lax.dot_general(
            pick.astype(bf), taps_ref[s], (((1,), (1,)), ((), ())), preferred_element_type=jnp.float32
        )
        short = jnp.concatenate(
            [taps, jnp.zeros((width, cols - taps.shape[1]), jnp.float32)], axis=1
        )
        gain = jnp.sum(pick * gain_ref[s : s + 1, :], axis=1, keepdims=True)
        copies = high // LANES
        short_rows = jnp.concatenate(
            [short[g * LANES : (g + 1) * LANES] for g in range(groups) for _ in range(copies)], axis=0
        )
        gain_rows = jnp.concatenate(
            [gain[g * LANES : (g + 1) * LANES] for g in range(groups) for _ in range(copies)], axis=0
        )
        short_turned = jnp.concatenate(
            [short_rows * all_cos, -(short_rows * all_sin)], axis=1
        ).astype(bf)
        short_spec = dot(short_turned, fc_ref[...]) * all_weight
        scale = 1.0 / math.sqrt(rows * cols)
        shifted = jnp.concatenate(
            [long_spec[:, :cols] * scale + gain_rows, long_spec[:, cols:] * scale], axis=1
        )
        combined.append(times(short_spec, shifted))

    signal = in_ref[0:rows].astype(jnp.float32)[:, :width]
    for s in range(sections):
        result = back(times(forward(signal), combined[s]))
        half = cols // 2
        packed = jnp.concatenate([result[:, :, :half], result[:, :, half:]], axis=1).astype(bf)
        out_ref[s * rows : (s + 1) * rows] = packed
        if s + 1 < sections:
            gate = in_ref[(s + 1) * rows : (s + 2) * rows].astype(jnp.float32)[:, :width]
            signal = result.astype(bf).astype(jnp.float32) * gate


def body(activations, short_filters, long_filters, skip_gain):
    sections = short_filters.shape[0]
    tokens, channels = activations.shape[1:]
    devices = lax.axis_size(BOTH)
    seq_devices = lax.axis_size("seq")
    owned = channels // devices
    width = -(-owned // LANES) * LANES
    cols = tokens

    def widen(array):
        split = array.reshape(array.shape[:2] + (devices, owned))
        split = jnp.pad(split, ((0, 0), (0, 0), (0, 0), (0, width - owned)))
        return split.reshape(array.shape[:2] + (devices * width,))

    acts, filters = activations, long_filters
    if width != owned:
        acts, filters = widen(acts), widen(filters)
    limit = pltpu.CompilerParams(vmem_limit_bytes=56 * 1024 * 1024)
    outgoing = pl.pallas_call(
        functools.partial(send_kernel, width),
        out_shape=jax.ShapeDtypeStruct((devices, 2 * width, cols), jnp.bfloat16),
        compiler_params=limit,
    )(acts, filters)
    arrived = lax.all_to_all(outgoing, BOTH, split_axis=0, concat_axis=0, tiled=True)
    place = lax.axis_index(BOTH).astype(jnp.int32).reshape(1)
    vmem = pl.BlockSpec(memory_space=pltpu.VMEM)
    results = pl.pallas_call(
        functools.partial(main_kernel, width, owned),
        out_shape=jax.ShapeDtypeStruct((devices, 2 * width, cols // 2), jnp.bfloat16),
        in_specs=[pl.BlockSpec(memory_space=pltpu.SMEM)] + [vmem] * 8,
        out_specs=vmem,
        compiler_params=limit,
    )(place, arrived, short_filters, skip_gain, *tables(seq_devices, cols))
    returned = lax.all_to_all(results, BOTH, split_axis=0, concat_axis=0, tiled=True)
    final = pl.pallas_call(
        final_kernel,
        out_shape=jax.ShapeDtypeStruct((1, cols, devices * width), jnp.bfloat16),
        compiler_params=limit,
    )(returned)
    if width != owned:
        final = final.reshape(1, cols, devices, width)[..., :owned].reshape(1, cols, channels)
    return final


def solution(mesh):
    return jax.shard_map(
        body,
        mesh=mesh,
        in_specs=(P("segment", "seq", None), P(), P("segment", "seq", None), P()),
        out_specs=P("segment", "seq", None),
        check_vma=False,
    )
```

```python
import functools
import math

import jax
import jax.numpy as jnp
import numpy as np
from jax import lax
from jax.experimental import pallas as pl
from jax.experimental.pallas import tpu as pltpu
from jax.sharding import PartitionSpec as P

BOTH = ("segment", "seq")
LANES = 8
MIB = 1024 * 1024


def tables(real_rows, cols):
    grid_rows = 2 * real_rows + 1
    length = grid_rows * cols
    freqs = real_rows + 1
    k = np.arange(freqs)
    rows = 2.0 * math.pi * ((k[:, None] * np.arange(real_rows)[None, :]) % grid_rows) / grid_rows
    first = np.stack([np.cos(rows), -np.sin(rows)])
    eye = np.eye(LANES)
    forward_rows = np.kron(first.reshape(2 * freqs, real_rows), eye)
    back_rows = np.kron(first[:, 1:].reshape(2 * real_rows, real_rows).T, eye)
    b = np.arange(cols)
    angle = 2.0 * math.pi * (k[:, None] * b[None, :]) / length
    turn = np.repeat(np.stack([np.cos(angle), np.sin(angle)]), LANES, axis=1)
    grid = 2.0 * math.pi * ((b[:, None] * b[None, :]) % cols) / cols
    c, s = np.cos(grid), np.sin(grid)
    forward_cols = np.block([[c, -s], [s, c]])
    back_cols = np.block([[c, s], [-s, c]])
    bf = jnp.bfloat16
    return (
        jnp.asarray(forward_rows, bf),
        jnp.asarray(back_rows, bf),
        jnp.asarray(turn, jnp.float32),
        jnp.asarray(forward_cols, bf),
        jnp.asarray(back_cols, bf),
    )


def dot(a, b):
    return jnp.dot(a, b, preferred_element_type=jnp.float32)


def dot_rows(a, b):
    return lax.dot_general(a, b, (((1,), (1,)), ((), ())), preferred_element_type=jnp.float32)


def identity(size):
    down = lax.broadcasted_iota(jnp.int32, (size, size), 0)
    across = lax.broadcasted_iota(jnp.int32, (size, size), 1)
    return jnp.where(down == across, 1.0, 0.0).astype(jnp.bfloat16)


def send_kernel(width, act_ref, filt_ref, out_ref):
    channels = act_ref.shape[2]
    step = math.gcd(channels, 256)
    eye = identity(step)
    acts, filts = [], []
    for start in range(0, channels, step):
        part = slice(start, start + step)
        acts.append(dot_rows(eye, act_ref[0, :, part]))
        filts.append(dot_rows(eye, filt_ref[0, :, part].astype(jnp.bfloat16)))
    act = jnp.concatenate(acts, axis=0)
    filt = jnp.concatenate(filts, axis=0)
    for d in range(channels // width):
        part = slice(d * width, (d + 1) * width)
        both = jnp.concatenate([act[part], filt[part]], axis=0).astype(jnp.bfloat16)
        out_ref[2 * d * width : 2 * (d + 1) * width] = both


def final_kernel(in_ref, out_ref):
    channels, tokens = in_ref.shape
    step = math.gcd(channels, 256)
    eye = identity(tokens)
    for start in range(0, channels, step):
        part = slice(start, start + step)
        out_ref[0, :, part] = dot_rows(eye, in_ref[part]).astype(jnp.bfloat16)


def short_kernel(width, owned, rows, place_ref, taps_ref, gain_ref, turn_ref, fc_ref, spec_ref, shift_ref):
    sections, count, channels = taps_ref.shape
    high, cols = turn_ref.shape[1:]
    groups = width // LANES
    copies = high // LANES
    length = (2 * rows + 1) * cols
    scale = 1.0 / math.sqrt(rows * cols)
    bf = jnp.bfloat16
    mine = lax.broadcasted_iota(jnp.int32, (width, channels), 0)
    them = lax.broadcasted_iota(jnp.int32, (width, channels), 1)
    pick = jnp.where((them == mine + place_ref[0] * owned) & (mine < owned), 1.0, 0.0)
    row = lax.broadcasted_iota(jnp.int32, (high, 1), 0)
    weight = jnp.where(row < LANES, scale / length, 2.0 * scale / length)
    for s in range(sections):
        taps = dot_rows(pick.astype(bf), taps_ref[s])
        short = jnp.concatenate([taps, jnp.zeros((width, cols - count), jnp.float32)], axis=1)
        gain = jnp.sum(pick * gain_ref[s : s + 1, :], axis=1, keepdims=True) * (1.0 / scale)
        wide = jnp.broadcast_to(gain, (width, 128))
        for g in range(groups):
            own = slice(g * LANES, (g + 1) * LANES)
            part = slice(g * high, (g + 1) * high)
            spread = jnp.concatenate([short[own]] * copies, axis=0)
            turned = jnp.concatenate([spread * turn_ref[0], -(spread * turn_ref[1])], axis=1).astype(bf)
            spec_ref[s, part] = dot(turned, fc_ref[...]) * weight
            shift_ref[s, part] = jnp.concatenate([wide[own]] * copies, axis=0)


def main_kernel(
    width, sections, in_ref, spec_ref, shift_ref, fr_ref, br_ref, turn_ref, fc_ref, bc_ref, out_ref
):
    total, cols = in_ref.shape
    rows = total // (2 * width * sections)
    groups = width // LANES
    high = turn_ref.shape[1]
    span = groups * high
    bf = jnp.bfloat16
    all_cos = jnp.concatenate([turn_ref[0]] * groups, axis=0)
    all_sin = jnp.concatenate([turn_ref[1]] * groups, axis=0)

    def chunk(s):
        part = in_ref[s * rows * 2 * width : (s + 1) * rows * 2 * width]
        return part.astype(jnp.float32).reshape(rows, 2 * width, cols)

    def forward(grids):
        turned = []
        for grid in grids:
            for g in range(groups):
                block = grid[:, g * LANES : (g + 1) * LANES].reshape(rows * LANES, cols).astype(bf)
                spread = dot(fr_ref[...], block)
                real, imag = spread[:high], spread[high:]
                cosine, sine = turn_ref[0], turn_ref[1]
                turned.append(
                    jnp.concatenate(
                        [real * cosine + imag * sine, imag * cosine - real * sine], axis=1
                    )
                )
        return dot(jnp.concatenate(turned, axis=0).astype(bf), fc_ref[...])

    def times(left, right):
        lr, li = left[:, :cols], left[:, cols:]
        rr, ri = right
        return jnp.concatenate([lr * rr - li * ri, lr * ri + li * rr], axis=1).astype(bf)

    def back(product):
        flat = dot(product, bc_ref[...])
        real, imag = flat[:, :cols], flat[:, cols:]
        turned_real = real * all_cos - imag * all_sin
        turned_imag = real * all_sin + imag * all_cos
        pieces = []
        for g in range(groups):
            start = g * high
            part = slice(start + LANES, start + high)
            both = jnp.concatenate([turned_real[part], turned_imag[part]], axis=0).astype(bf)
            piece = dot(br_ref[...], both).reshape(rows, LANES, cols)
            pieces.append(piece + turned_real[start : start + LANES][None])
        return jnp.concatenate(pieces, axis=1)

    def combine(s, spec):
        shift = jnp.concatenate([shift_ref[s]] * (cols // 128), axis=1)
        lr, li = spec[:, :cols] + shift, spec[:, cols:]
        rr, ri = spec_ref[s, :, :cols], spec_ref[s, :, cols:]
        return lr * rr - li * ri, lr * ri + li * rr

    chunks = [chunk(s) for s in range(sections)]
    specs = forward([chunks[0][:, :width]] + [part[:, width:] for part in chunks])
    signal_spec = specs[:span]
    for s in range(sections):
        mixed = combine(s, specs[(s + 1) * span : (s + 2) * span])
        result = back(times(signal_spec, mixed))
        rounded = result.reshape(rows * width, cols).astype(bf)
        out_ref[s * rows * width : (s + 1) * rows * width] = rounded
        if s + 1 < sections:
            gated = rounded.astype(jnp.float32).reshape(rows, width, cols) * chunks[s + 1][:, :width]
            signal_spec = forward([gated])


def body(activations, short_filters, long_filters, skip_gain):
    sections = short_filters.shape[0]
    tokens, channels = activations.shape[1:]
    devices = lax.axis_size(BOTH)
    seq_devices = lax.axis_size("seq")
    owned = channels // devices
    width = -(-owned // LANES) * LANES
    cols = tokens
    laid = devices * width

    def widen(array):
        split = array.reshape(array.shape[:2] + (devices, owned))
        split = jnp.pad(split, ((0, 0), (0, 0), (0, 0), (0, width - owned)))
        return split.reshape(array.shape[:2] + (laid,))

    def exchanged(array, height):
        chunks = array.reshape(devices, height, cols)
        moved = lax.all_to_all(chunks, BOTH, split_axis=0, concat_axis=0, tiled=True)
        return moved.reshape(devices * height, cols)

    def grant(size):
        return pltpu.CompilerParams(vmem_limit_bytes=int(size))

    acts, filters = activations, long_filters
    if width != owned:
        acts, filters = widen(acts), widen(filters)
    forward_rows, back_rows, turn, forward_cols, back_cols = tables(seq_devices, cols)
    vmem = pl.BlockSpec(memory_space=pltpu.VMEM)
    area = laid * cols
    span = (seq_devices + 1) * width
    table_bytes = 4 * (forward_rows.size + turn.size + forward_cols.size)
    outgoing = pl.pallas_call(
        functools.partial(send_kernel, width),
        out_shape=jax.ShapeDtypeStruct((2 * laid, cols), jnp.bfloat16),
        compiler_params=grant(4 * MIB + 24 * area),
    )(acts, filters)
    arrived = exchanged(outgoing, 2 * width)
    place = lax.axis_index(BOTH).astype(jnp.int32).reshape(1)
    short_spec, shift = pl.pallas_call(
        functools.partial(short_kernel, width, owned, seq_devices),
        out_shape=(
            jax.ShapeDtypeStruct((sections, span, 2 * cols), jnp.float32),
            jax.ShapeDtypeStruct((sections, span, 128), jnp.float32),
        ),
        in_specs=[pl.BlockSpec(memory_space=pltpu.SMEM)] + [vmem] * 4,
        out_specs=(vmem, vmem),
        compiler_params=grant(4 * MIB + 16 * sections * span * cols + table_bytes),
        cost_estimate=pl.CostEstimate(
            flops=8 * sections * span * cols * cols, bytes_accessed=8 * MIB, transcendentals=0
        ),
    )(place, short_filters, skip_gain, turn, forward_cols)
    results = pl.pallas_call(
        functools.partial(main_kernel, width, sections),
        out_shape=jax.ShapeDtypeStruct((laid, cols), jnp.bfloat16),
        in_specs=[vmem] * 8,
        out_specs=vmem,
        compiler_params=grant(8 * MIB + 64 * span * cols + 2 * table_bytes),
    )(arrived, short_spec, shift, forward_rows, back_rows, turn, forward_cols, back_cols)
    returned = exchanged(results, width)
    final = pl.pallas_call(
        final_kernel,
        out_shape=jax.ShapeDtypeStruct((1, cols, laid), jnp.bfloat16),
        compiler_params=grant(4 * MIB + 16 * area),
    )(returned)
    if width != owned:
        final = final.reshape(1, cols, devices, width)[..., :owned].reshape(1, cols, channels)
    return final


def solution(mesh):
    return jax.shard_map(
        body,
        mesh=mesh,
        in_specs=(P("segment", "seq", None), P(), P("segment", "seq", None), P()),
        out_specs=P("segment", "seq", None),
        check_vma=False,
    )
```

```python
import functools
import math

import jax
import jax.numpy as jnp
import numpy as np
from jax import lax
from jax.experimental import pallas as pl
from jax.experimental.pallas import tpu as pltpu
from jax.sharding import PartitionSpec as P

BOTH = ("segment", "seq")
LANES = 8
MIB = 1024 * 1024


def tables(real_rows, cols):
    grid_rows = 2 * real_rows + 1
    length = grid_rows * cols
    freqs = real_rows + 1
    k = np.arange(freqs)
    rows = 2.0 * math.pi * ((k[:, None] * np.arange(real_rows)[None, :]) % grid_rows) / grid_rows
    first = np.stack([np.cos(rows), -np.sin(rows)]).reshape(2 * freqs, real_rows)
    row_part = np.kron(first, np.eye(LANES))
    b = np.arange(cols)
    angle = 2.0 * math.pi * (k[:, None] * b[None, :]) / length
    turn = np.repeat(np.concatenate([np.cos(angle), np.sin(angle)], axis=1), LANES, axis=0)
    grid = 2.0 * math.pi * ((b[:, None] * b[None, :]) % cols) / cols
    c, s = np.cos(grid), np.sin(grid)
    parts = [np.block([[c, -s], [s, c]]), np.block([[c, s], [-s, c]]), row_part]
    lanes = max(part.shape[1] for part in parts)
    stacked = np.concatenate([np.pad(p, ((0, 0), (0, lanes - p.shape[1]))) for p in parts])
    return jnp.asarray(stacked, jnp.bfloat16), jnp.asarray(turn, jnp.float32)


def dot(a, b):
    return jnp.dot(a, b, preferred_element_type=jnp.float32)


def dot_rows(a, b):
    return lax.dot_general(a, b, (((1,), (1,)), ((), ())), preferred_element_type=jnp.float32)


def identity(size):
    down = lax.broadcasted_iota(jnp.int32, (size, size), 0)
    across = lax.broadcasted_iota(jnp.int32, (size, size), 1)
    return jnp.where(down == across, 1.0, 0.0).astype(jnp.bfloat16)


def send_steps(width, channels):
    step = math.lcm(width, 128)
    while 2 * step <= 512 and channels % (2 * step) == 0:
        step = 2 * step
    return step, channels // step


def send_kernel(width, act_ref, filt_ref, out_ref, act_held, filt_held, out_held, in_sem, out_sem):
    step, count = send_steps(width, act_ref.shape[2])
    arriving = []
    for n in range(count):
        part = pl.ds(n * step, step)
        pair = (
            pltpu.make_async_copy(filt_ref.at[0, :, part], filt_held.at[:, part], in_sem.at[2 * n]),
            pltpu.make_async_copy(act_ref.at[0, :, part], act_held.at[:, part], in_sem.at[2 * n + 1]),
        )
        for copy in pair:
            copy.start()
        arriving.append(pair)
    eye = identity(128)
    leaving = []
    for n in range(count):
        for copy in arriving[n]:
            copy.wait()
        acts, filts = [], []
        for start in range(n * step, (n + 1) * step, 128):
            part = slice(start, start + 128)
            acts.append(dot_rows(eye, act_held[:, part]))
            filts.append(dot_rows(eye, filt_held[:, part].astype(jnp.bfloat16)))
        act = jnp.concatenate(acts, axis=0)
        filt = jnp.concatenate(filts, axis=0)
        pieces = []
        for d in range(step // width):
            part = slice(d * width, (d + 1) * width)
            pieces += [act[part], filt[part]]
        whole = slice(2 * n * step, 2 * (n + 1) * step)
        out_held[whole] = jnp.concatenate(pieces, axis=0).astype(jnp.bfloat16)
        copy = pltpu.make_async_copy(out_held.at[whole], out_ref.at[whole], out_sem.at[n])
        copy.start()
        leaving.append(copy)
    for copy in leaving:
        copy.wait()


def final_kernel(in_ref, out_ref):
    channels, tokens = in_ref.shape
    step = math.gcd(channels, 256)
    eye = identity(tokens)
    for start in range(0, channels, step):
        part = slice(start, start + step)
        out_ref[0, :, part] = dot_rows(eye, in_ref[part]).astype(jnp.bfloat16)


def short_kernel(width, owned, rows, place_ref, taps_ref, gain_ref, turn_ref, table_ref, out_ref):
    sections, count, channels = taps_ref.shape
    high = turn_ref.shape[0]
    cols = turn_ref.shape[1] // 2
    groups = width // LANES
    copies = high // LANES
    span = groups * high
    length = (2 * rows + 1) * cols
    scale = 1.0 / math.sqrt(rows * cols)
    bf = jnp.bfloat16
    mine = lax.broadcasted_iota(jnp.int32, (width, channels), 0)
    them = lax.broadcasted_iota(jnp.int32, (width, channels), 1)
    pick = jnp.where((them == mine + place_ref[0] * owned) & (mine < owned), 1.0, 0.0)
    row = lax.broadcasted_iota(jnp.int32, (high, 1), 0)
    weight = jnp.where(row < LANES, scale / length, 2.0 * scale / length)
    cosine, sine = turn_ref[:, :cols], turn_ref[:, cols:]
    out_ref[sections * span : sections * span + high] = turn_ref[...]
    for s in range(sections):
        taps = dot_rows(pick.astype(bf), taps_ref[s])
        short = jnp.concatenate([taps, jnp.zeros((width, cols - count), jnp.float32)], axis=1)
        gain = jnp.sum(pick * gain_ref[s : s + 1, :], axis=1, keepdims=True) * (1.0 / scale)
        at = sections * span + high + s * width
        out_ref[at : at + width] = jnp.broadcast_to(gain, (width, 2 * cols))
        for g in range(groups):
            own = slice(g * LANES, (g + 1) * LANES)
            spread = jnp.concatenate([short[own]] * copies, axis=0)
            turned = jnp.concatenate([spread * cosine, -(spread * sine)], axis=1).astype(bf)
            at = s * span + g * high
            out_ref[at : at + high] = dot(turned, table_ref[: 2 * cols, : 2 * cols]) * weight


def main_kernel(width, sections, in_ref, short_ref, table_ref, out_ref):
    total, cols = in_ref.shape
    rows = total // (2 * width * sections)
    groups = width // LANES
    high = (rows + 1) * LANES
    span = groups * high
    bf = jnp.bfloat16
    turns = slice(sections * span, sections * span + high)
    cosine, sine = short_ref[turns, :cols], short_ref[turns, cols:]
    all_cos = jnp.concatenate([cosine] * groups, axis=0)
    all_sin = jnp.concatenate([sine] * groups, axis=0)
    forward_cols = table_ref[: 2 * cols, : 2 * cols]
    back_cols = table_ref[2 * cols : 4 * cols, : 2 * cols]
    forward_rows = table_ref[4 * cols : 4 * cols + 2 * high, : rows * LANES]
    wide_rows = forward_rows.astype(jnp.float32)
    some_rows = jnp.concatenate([wide_rows[LANES:high], wide_rows[high + LANES :]], axis=0)
    back_rows = dot_rows(identity(rows * LANES), some_rows.astype(bf)).astype(bf)

    def chunk(s):
        part = in_ref[s * rows * 2 * width : (s + 1) * rows * 2 * width]
        return part.astype(jnp.float32).reshape(rows, 2 * width, cols)

    def forward(grids):
        turned = []
        for grid in grids:
            for g in range(groups):
                block = grid[:, g * LANES : (g + 1) * LANES].reshape(rows * LANES, cols).astype(bf)
                spread = dot(forward_rows, block)
                real, imag = spread[:high], spread[high:]
                turned.append(
                    jnp.concatenate(
                        [real * cosine + imag * sine, imag * cosine - real * sine], axis=1
                    )
                )
        return dot(jnp.concatenate(turned, axis=0).astype(bf), forward_cols)

    def times(left, right):
        lr, li = left[:, :cols], left[:, cols:]
        rr, ri = right
        return jnp.concatenate([lr * rr - li * ri, lr * ri + li * rr], axis=1).astype(bf)

    def back(product):
        flat = dot(product, back_cols)
        real, imag = flat[:, :cols], flat[:, cols:]
        turned_real = real * all_cos - imag * all_sin
        turned_imag = real * all_sin + imag * all_cos
        pieces = []
        for g in range(groups):
            start = g * high
            part = slice(start + LANES, start + high)
            both = jnp.concatenate([turned_real[part], turned_imag[part]], axis=0).astype(bf)
            piece = dot(back_rows, both).reshape(rows, LANES, cols)
            pieces.append(piece + turned_real[start : start + LANES][None])
        return jnp.concatenate(pieces, axis=1)

    def combine(s, spec):
        at = sections * span + high + s * width
        gains = short_ref[at : at + width, :cols]
        shift = jnp.concatenate(
            [gains[g * LANES : (g + 1) * LANES] for g in range(groups) for _ in range(rows + 1)], axis=0
        )
        own = slice(s * span, (s + 1) * span)
        lr, li = spec[:, :cols] + shift, spec[:, cols:]
        rr, ri = short_ref[own, :cols], short_ref[own, cols:]
        return lr * rr - li * ri, lr * ri + li * rr

    chunks = [chunk(s) for s in range(sections)]
    specs = forward([chunks[0][:, :width]] + [part[:, width:] for part in chunks])
    signal_spec = specs[:span]
    for s in range(sections):
        mixed = combine(s, specs[(s + 1) * span : (s + 2) * span])
        result = back(times(signal_spec, mixed))
        rounded = result.reshape(rows * width, cols).astype(bf)
        out_ref[s * rows * width : (s + 1) * rows * width] = rounded
        if s + 1 < sections:
            gated = rounded.astype(jnp.float32).reshape(rows, width, cols) * chunks[s + 1][:, :width]
            signal_spec = forward([gated])


def body(activations, short_filters, long_filters, skip_gain):
    sections = short_filters.shape[0]
    tokens, channels = activations.shape[1:]
    devices = lax.axis_size(BOTH)
    seq_devices = lax.axis_size("seq")
    owned = channels // devices
    width = -(-owned // LANES) * LANES
    cols = tokens
    laid = devices * width

    def widen(array):
        split = array.reshape(array.shape[:2] + (devices, owned))
        split = jnp.pad(split, ((0, 0), (0, 0), (0, 0), (0, width - owned)))
        return split.reshape(array.shape[:2] + (laid,))

    def exchanged(array, height):
        chunks = array.reshape(devices, height, cols)
        moved = lax.all_to_all(chunks, BOTH, split_axis=0, concat_axis=0, tiled=True)
        return moved.reshape(devices * height, cols)

    def grant(size):
        return pltpu.CompilerParams(vmem_limit_bytes=int(size))

    acts, filters = activations, long_filters
    if width != owned:
        acts, filters = widen(acts), widen(filters)
    table, turn = tables(seq_devices, cols)
    vmem = pl.BlockSpec(memory_space=pltpu.VMEM)
    hbm = pl.BlockSpec(memory_space=pltpu.HBM)
    area = laid * cols
    span = (seq_devices + 1) * width
    steps = send_steps(width, laid)[1]
    outgoing = pl.pallas_call(
        functools.partial(send_kernel, width),
        out_shape=jax.ShapeDtypeStruct((2 * laid, cols), jnp.bfloat16),
        in_specs=[hbm, hbm],
        out_specs=hbm,
        scratch_shapes=[
            pltpu.VMEM((cols, laid), jnp.bfloat16),
            pltpu.VMEM((cols, laid), jnp.float32),
            pltpu.VMEM((2 * laid, cols), jnp.bfloat16),
            pltpu.SemaphoreType.DMA((2 * steps,)),
            pltpu.SemaphoreType.DMA((steps,)),
        ],
        compiler_params=grant(56 * MIB),
    )(acts, filters)
    arrived = exchanged(outgoing, 2 * width)
    place = lax.axis_index(BOTH).astype(jnp.int32).reshape(1)
    held = sections * (span + width) + turn.shape[0]
    short_spec = pl.pallas_call(
        functools.partial(short_kernel, width, owned, seq_devices),
        out_shape=jax.ShapeDtypeStruct((held, 2 * cols), jnp.float32),
        in_specs=[pl.BlockSpec(memory_space=pltpu.SMEM)] + [vmem] * 4,
        out_specs=vmem,
        compiler_params=grant(4 * MIB + 8 * held * cols + 4 * table.size + 4 * turn.size),
        cost_estimate=pl.CostEstimate(
            flops=8 * sections * span * cols * cols, bytes_accessed=8 * MIB, transcendentals=0
        ),
    )(place, short_filters, skip_gain, turn, table)
    results = pl.pallas_call(
        functools.partial(main_kernel, width, sections),
        out_shape=jax.ShapeDtypeStruct((laid, cols), jnp.bfloat16),
        in_specs=[vmem] * 3,
        out_specs=vmem,
        compiler_params=grant(8 * MIB + 64 * span * cols + 4 * table.size),
    )(arrived, short_spec, table)
    returned = exchanged(results, width)
    final = pl.pallas_call(
        final_kernel,
        out_shape=jax.ShapeDtypeStruct((1, cols, laid), jnp.bfloat16),
        compiler_params=grant(4 * MIB + 16 * area),
    )(returned)
    if width != owned:
        final = final.reshape(1, cols, devices, width)[..., :owned].reshape(1, cols, channels)
    return final


def solution(mesh):
    return jax.shard_map(
        body,
        mesh=mesh,
        in_specs=(P("segment", "seq", None), P(), P("segment", "seq", None), P()),
        out_specs=P("segment", "seq", None),
        check_vma=False,
    )
```

```python
import functools
import math

import jax
import jax.numpy as jnp
import numpy as np
from jax import lax
from jax.experimental import pallas as pl
from jax.experimental.pallas import tpu as pltpu
from jax.sharding import PartitionSpec as P

BOTH = ("segment", "seq")
LANES = 8
MIB = 1024 * 1024


def tables(real_rows, cols):
    grid_rows = 2 * real_rows + 1
    length = grid_rows * cols
    freqs = real_rows + 1
    k = np.arange(freqs)
    rows = 2.0 * math.pi * ((k[:, None] * np.arange(real_rows)[None, :]) % grid_rows) / grid_rows
    first = np.stack([np.cos(rows), -np.sin(rows)]).reshape(2 * freqs, real_rows)
    row_part = np.kron(first, np.eye(LANES))
    b = np.arange(cols)
    angle = 2.0 * math.pi * (k[:, None] * b[None, :]) / length
    turn = np.repeat(np.concatenate([np.cos(angle), np.sin(angle)], axis=1), LANES, axis=0)
    grid = 2.0 * math.pi * ((b[:, None] * b[None, :]) % cols) / cols
    c, s = np.cos(grid), np.sin(grid)
    parts = [np.block([[c, -s], [s, c]]), np.block([[c, s], [-s, c]]), row_part]
    lanes = max(part.shape[1] for part in parts)
    stacked = np.concatenate([np.pad(p, ((0, 0), (0, lanes - p.shape[1]))) for p in parts])
    return jnp.asarray(stacked, jnp.bfloat16), jnp.asarray(turn, jnp.float32)


def dot(a, b):
    return jnp.dot(a, b, preferred_element_type=jnp.float32)


def dot_rows(a, b):
    return lax.dot_general(a, b, (((1,), (1,)), ((), ())), preferred_element_type=jnp.float32)


def identity(size):
    down = lax.broadcasted_iota(jnp.int32, (size, size), 0)
    across = lax.broadcasted_iota(jnp.int32, (size, size), 1)
    return jnp.where(down == across, 1.0, 0.0).astype(jnp.bfloat16)


def send_steps(width, channels):
    step = math.lcm(width, 128)
    while 2 * step <= 512 and channels % (2 * step) == 0:
        step = 2 * step
    return step, channels // step


def send_kernel(width, act_ref, filt_ref, out_ref, act_held, filt_held, out_held, in_sem, out_sem):
    step, count = send_steps(width, act_ref.shape[2])
    arriving = []
    for n in range(count):
        part = pl.ds(n * step, step)
        pair = (
            pltpu.make_async_copy(filt_ref.at[0, :, part], filt_held.at[:, part], in_sem.at[2 * n]),
            pltpu.make_async_copy(act_ref.at[0, :, part], act_held.at[:, part], in_sem.at[2 * n + 1]),
        )
        for copy in pair:
            copy.start()
        arriving.append(pair)
    eye = identity(128)
    leaving = []
    for n in range(count):
        for copy in arriving[n]:
            copy.wait()
        acts, filts = [], []
        for start in range(n * step, (n + 1) * step, 128):
            part = slice(start, start + 128)
            acts.append(dot_rows(eye, act_held[:, part]))
            filts.append(dot_rows(eye, filt_held[:, part].astype(jnp.bfloat16)))
        act = jnp.concatenate(acts, axis=0)
        filt = jnp.concatenate(filts, axis=0)
        pieces = []
        for d in range(step // width):
            part = slice(d * width, (d + 1) * width)
            pieces += [act[part], filt[part]]
        whole = slice(2 * n * step, 2 * (n + 1) * step)
        out_held[whole] = jnp.concatenate(pieces, axis=0).astype(jnp.bfloat16)
        copy = pltpu.make_async_copy(out_held.at[whole], out_ref.at[whole], out_sem.at[n])
        copy.start()
        leaving.append(copy)
    for copy in leaving:
        copy.wait()


def final_kernel(in_ref, out_ref):
    channels, tokens = in_ref.shape
    step = math.gcd(channels, 256)
    eye = identity(tokens)
    for start in range(0, channels, step):
        part = slice(start, start + step)
        out_ref[0, :, part] = dot_rows(eye, in_ref[part]).astype(jnp.bfloat16)


def short_kernel(width, owned, rows, place_ref, taps_ref, gain_ref, turn_ref, table_ref, out_ref):
    sections, count, channels = taps_ref.shape
    high = turn_ref.shape[0]
    cols = turn_ref.shape[1] // 2
    groups = width // LANES
    copies = high // LANES
    span = groups * high
    length = (2 * rows + 1) * cols
    scale = 1.0 / math.sqrt(rows * cols)
    bf = jnp.bfloat16
    mine = lax.broadcasted_iota(jnp.int32, (width, channels), 0)
    them = lax.broadcasted_iota(jnp.int32, (width, channels), 1)
    pick = jnp.where((them == mine + place_ref[0] * owned) & (mine < owned), 1.0, 0.0)
    row = lax.broadcasted_iota(jnp.int32, (high, 1), 0)
    weight = jnp.where(row < LANES, scale / length, 2.0 * scale / length)
    cosine, sine = turn_ref[:, :cols], turn_ref[:, cols:]
    out_ref[sections * span : sections * span + high] = turn_ref[...]
    for s in range(sections):
        taps = dot_rows(pick.astype(bf), taps_ref[s])
        short = jnp.concatenate([taps, jnp.zeros((width, cols - count), jnp.float32)], axis=1)
        gain = jnp.sum(pick * gain_ref[s : s + 1, :], axis=1, keepdims=True) * (1.0 / scale)
        at = sections * span + high + s * width
        out_ref[at : at + width] = jnp.broadcast_to(gain, (width, 2 * cols))
        for g in range(groups):
            own = slice(g * LANES, (g + 1) * LANES)
            spread = jnp.concatenate([short[own]] * copies, axis=0)
            turned = jnp.concatenate([spread * cosine, -(spread * sine)], axis=1).astype(bf)
            at = s * span + g * high
            out_ref[at : at + high] = dot(turned, table_ref[: 2 * cols, : 2 * cols]) * weight


def main_kernel(width, sections, in_ref, short_ref, table_ref, out_ref):
    total, cols = in_ref.shape
    rows = total // (2 * width * sections)
    groups = width // LANES
    high = (rows + 1) * LANES
    span = groups * high
    bf = jnp.bfloat16
    turns = slice(sections * span, sections * span + high)
    cosine, sine = short_ref[turns, :cols], short_ref[turns, cols:]
    all_cos = jnp.concatenate([cosine] * groups, axis=0)
    all_sin = jnp.concatenate([sine] * groups, axis=0)
    forward_cols = table_ref[: 2 * cols, : 2 * cols]
    back_cols = table_ref[2 * cols : 4 * cols, : 2 * cols]
    forward_rows = table_ref[4 * cols : 4 * cols + 2 * high, : rows * LANES]
    wide_rows = forward_rows.astype(jnp.float32)
    some_rows = jnp.concatenate([wide_rows[LANES:high], wide_rows[high + LANES :]], axis=0)
    back_rows = dot_rows(identity(rows * LANES), some_rows.astype(bf)).astype(bf)

    def chunk(s):
        part = in_ref[s * rows * 2 * width : (s + 1) * rows * 2 * width]
        return part.astype(jnp.float32).reshape(rows, 2 * width, cols)

    def forward(grids):
        turned = []
        for grid in grids:
            for g in range(groups):
                block = grid[:, g * LANES : (g + 1) * LANES].reshape(rows * LANES, cols).astype(bf)
                spread = dot(forward_rows, block)
                real, imag = spread[:high], spread[high:]
                turned.append(
                    jnp.concatenate(
                        [real * cosine + imag * sine, imag * cosine - real * sine], axis=1
                    )
                )
        return dot(jnp.concatenate(turned, axis=0).astype(bf), forward_cols)

    def times(left, right):
        lr, li = left[:, :cols], left[:, cols:]
        rr, ri = right
        return jnp.concatenate([lr * rr - li * ri, lr * ri + li * rr], axis=1).astype(bf)

    def back(product):
        flat = dot(product, back_cols)
        real, imag = flat[:, :cols], flat[:, cols:]
        turned_real = real * all_cos - imag * all_sin
        turned_imag = real * all_sin + imag * all_cos
        pieces = []
        for g in range(groups):
            start = g * high
            part = slice(start + LANES, start + high)
            both = jnp.concatenate([turned_real[part], turned_imag[part]], axis=0).astype(bf)
            piece = dot(back_rows, both).reshape(rows, LANES, cols)
            pieces.append(piece + turned_real[start : start + LANES][None])
        return jnp.concatenate(pieces, axis=1)

    def combine(s, spec):
        at = sections * span + high + s * width
        gains = short_ref[at : at + width, :cols]
        shift = jnp.concatenate(
            [gains[g * LANES : (g + 1) * LANES] for g in range(groups) for _ in range(rows + 1)], axis=0
        )
        own = slice(s * span, (s + 1) * span)
        lr, li = spec[:, :cols] + shift, spec[:, cols:]
        rr, ri = short_ref[own, :cols], short_ref[own, cols:]
        return lr * rr - li * ri, lr * ri + li * rr

    chunks = [chunk(s) for s in range(sections)]
    specs = forward([chunks[0][:, :width]] + [part[:, width:] for part in chunks])
    signal_spec = specs[:span]
    for s in range(sections):
        mixed = combine(s, specs[(s + 1) * span : (s + 2) * span])
        result = back(times(signal_spec, mixed))
        rounded = result.reshape(rows * width, cols).astype(bf)
        out_ref[s * rows * width : (s + 1) * rows * width] = rounded
        if s + 1 < sections:
            gated = rounded.astype(jnp.float32).reshape(rows, width, cols) * chunks[s + 1][:, :width]
            signal_spec = forward([gated])


def body(activations, short_filters, long_filters, skip_gain):
    sections = short_filters.shape[0]
    tokens, channels = activations.shape[1:]
    devices = lax.axis_size(BOTH)
    seq_devices = lax.axis_size("seq")
    owned = channels // devices
    width = -(-owned // LANES) * LANES
    cols = tokens
    laid = devices * width

    def widen(array):
        split = array.reshape(array.shape[:2] + (devices, owned))
        split = jnp.pad(split, ((0, 0), (0, 0), (0, 0), (0, width - owned)))
        return split.reshape(array.shape[:2] + (laid,))

    def exchanged(array, height):
        chunks = array.reshape(devices, height, cols)
        moved = lax.all_to_all(chunks, BOTH, split_axis=0, concat_axis=0, tiled=True)
        return moved.reshape(devices * height, cols)

    def grant(size):
        return pltpu.CompilerParams(vmem_limit_bytes=int(size))

    acts, filters = activations, long_filters
    if width != owned:
        acts, filters = widen(acts), widen(filters)
    table, turn = tables(seq_devices, cols)
    vmem = pl.BlockSpec(memory_space=pltpu.VMEM)
    hbm = pl.BlockSpec(memory_space=pltpu.HBM)
    area = laid * cols
    span = (seq_devices + 1) * width
    steps = send_steps(width, laid)[1]
    outgoing = pl.pallas_call(
        functools.partial(send_kernel, width),
        out_shape=jax.ShapeDtypeStruct((2 * laid, cols), jnp.bfloat16),
        in_specs=[hbm, hbm],
        out_specs=hbm,
        scratch_shapes=[
            pltpu.VMEM((cols, laid), jnp.bfloat16),
            pltpu.VMEM((cols, laid), jnp.float32),
            pltpu.VMEM((2 * laid, cols), jnp.bfloat16),
            pltpu.SemaphoreType.DMA((2 * steps,)),
            pltpu.SemaphoreType.DMA((steps,)),
        ],
        compiler_params=grant(56 * MIB),
    )(acts, filters)
    arrived = exchanged(outgoing, 2 * width)
    place = lax.axis_index(BOTH).astype(jnp.int32).reshape(1)
    held = sections * (span + width) + turn.shape[0]
    short_spec = pl.pallas_call(
        functools.partial(short_kernel, width, owned, seq_devices),
        out_shape=jax.ShapeDtypeStruct((held, 2 * cols), jnp.float32),
        in_specs=[pl.BlockSpec(memory_space=pltpu.SMEM)] + [vmem] * 4,
        out_specs=vmem,
        compiler_params=grant(2 * MIB + 8 * held * cols + 2 * table.size + 4 * turn.size),
        cost_estimate=pl.CostEstimate(
            flops=8 * sections * span * cols * cols, bytes_accessed=8 * MIB, transcendentals=0
        ),
    )(place, short_filters, skip_gain, turn, table)
    results = pl.pallas_call(
        functools.partial(main_kernel, width, sections),
        out_shape=jax.ShapeDtypeStruct((laid, cols), jnp.bfloat16),
        in_specs=[vmem] * 3,
        out_specs=vmem,
        compiler_params=grant(MIB + 6 * area + 8 * held * cols + 2 * table.size + 32 * span * cols),
    )(arrived, short_spec, table)
    returned = exchanged(results, width)
    final = pl.pallas_call(
        final_kernel,
        out_shape=jax.ShapeDtypeStruct((1, cols, laid), jnp.bfloat16),
        compiler_params=grant(4 * MIB + 16 * area),
    )(returned)
    if width != owned:
        final = final.reshape(1, cols, devices, width)[..., :owned].reshape(1, cols, channels)
    return final


def solution(mesh):
    return jax.shard_map(
        body,
        mesh=mesh,
        in_specs=(P("segment", "seq", None), P(), P("segment", "seq", None), P()),
        out_specs=P("segment", "seq", None),
        check_vma=False,
    )
```

```python
import functools
import math

import jax
import jax.numpy as jnp
import numpy as np
from jax import lax
from jax.experimental import pallas as pl
from jax.experimental.pallas import tpu as pltpu
from jax.sharding import PartitionSpec as P

BOTH = ("segment", "seq")
LANES = 8
MIB = 1024 * 1024


def tables(real_rows, cols):
    grid_rows = 2 * real_rows + 1
    length = grid_rows * cols
    freqs = real_rows + 1
    k = np.arange(freqs)
    rows = 2.0 * math.pi * ((k[:, None] * np.arange(real_rows)[None, :]) % grid_rows) / grid_rows
    first = np.stack([np.cos(rows), -np.sin(rows)]).reshape(2 * freqs, real_rows)
    row_part = np.kron(first, np.eye(LANES))
    b = np.arange(cols)
    angle = 2.0 * math.pi * (k[:, None] * b[None, :]) / length
    turn = np.concatenate([np.cos(angle), np.sin(angle)], axis=1)
    turn = np.pad(turn, ((0, -freqs % LANES), (0, 0)))
    grid = 2.0 * math.pi * ((b[:, None] * b[None, :]) % cols) / cols
    c, s = np.cos(grid), np.sin(grid)
    parts = [np.block([[c, -s], [s, c]]), row_part]
    lanes = max(part.shape[1] for part in parts)
    stacked = np.concatenate([np.pad(p, ((0, 0), (0, lanes - p.shape[1]))) for p in parts])
    return jnp.asarray(stacked, jnp.bfloat16), jnp.asarray(turn, jnp.float32)


def dot(a, b):
    return jnp.dot(a, b, preferred_element_type=jnp.float32)


def dot_rows(a, b):
    return lax.dot_general(a, b, (((1,), (1,)), ((), ())), preferred_element_type=jnp.float32)


def repeated(rows, count):
    return jnp.concatenate(
        [jnp.broadcast_to(rows[k : k + 1], (LANES, rows.shape[1])) for k in range(count)], axis=0
    )


def identity(size):
    down = lax.broadcasted_iota(jnp.int32, (size, size), 0)
    across = lax.broadcasted_iota(jnp.int32, (size, size), 1)
    return jnp.where(down == across, 1.0, 0.0).astype(jnp.bfloat16)


def send_steps(width, channels):
    step = math.lcm(width, 128)
    while 2 * step <= 512 and channels % (2 * step) == 0:
        step = 2 * step
    return step, channels // step


def send_kernel(width, act_ref, filt_ref, out_ref, act_held, filt_held, out_held, in_sem, out_sem):
    step, count = send_steps(width, act_ref.shape[2])
    arriving = []
    for n in range(count):
        part = pl.ds(n * step, step)
        pair = (
            pltpu.make_async_copy(filt_ref.at[0, :, part], filt_held.at[:, part], in_sem.at[2 * n]),
            pltpu.make_async_copy(act_ref.at[0, :, part], act_held.at[:, part], in_sem.at[2 * n + 1]),
        )
        for copy in pair:
            copy.start()
        arriving.append(pair)
    eye = identity(128)
    leaving = []
    for n in range(count):
        for copy in arriving[n]:
            copy.wait()
        acts, filts = [], []
        for start in range(n * step, (n + 1) * step, 128):
            part = slice(start, start + 128)
            acts.append(dot_rows(eye, act_held[:, part]))
            filts.append(dot_rows(eye, filt_held[:, part].astype(jnp.bfloat16)))
        act = jnp.concatenate(acts, axis=0)
        filt = jnp.concatenate(filts, axis=0)
        pieces = []
        for d in range(step // width):
            part = slice(d * width, (d + 1) * width)
            pieces += [act[part], filt[part]]
        whole = slice(2 * n * step, 2 * (n + 1) * step)
        out_held[whole] = jnp.concatenate(pieces, axis=0).astype(jnp.bfloat16)
        copy = pltpu.make_async_copy(out_held.at[whole], out_ref.at[whole], out_sem.at[n])
        copy.start()
        leaving.append(copy)
    for copy in leaving:
        copy.wait()


def final_kernel(in_ref, out_ref):
    channels, tokens = in_ref.shape
    step = math.gcd(channels, 256)
    eye = identity(tokens)
    for start in range(0, channels, step):
        part = slice(start, start + step)
        out_ref[0, :, part] = dot_rows(eye, in_ref[part]).astype(jnp.bfloat16)


def short_kernel(width, owned, rows, place_ref, taps_ref, gain_ref, turn_ref, table_ref, out_ref):
    sections, count, channels = taps_ref.shape
    copies = rows + 1
    high = copies * LANES
    held, cols = turn_ref.shape[0], turn_ref.shape[1] // 2
    groups = width // LANES
    span = groups * high
    length = (2 * rows + 1) * cols
    scale = 1.0 / math.sqrt(rows * cols)
    bf = jnp.bfloat16
    mine = lax.broadcasted_iota(jnp.int32, (width, channels), 0)
    them = lax.broadcasted_iota(jnp.int32, (width, channels), 1)
    pick = jnp.where((them == mine + place_ref[0] * owned) & (mine < owned), 1.0, 0.0)
    row = lax.broadcasted_iota(jnp.int32, (high, 1), 0)
    weight = jnp.where(row < LANES, scale / length, 2.0 * scale / length)
    turn = turn_ref[...]
    both = repeated(turn, copies)
    cosine, sine = both[:, :cols], both[:, cols:]
    out_ref[sections * span : sections * span + held] = turn
    for s in range(sections):
        taps = dot_rows(pick.astype(bf), taps_ref[s])
        short = jnp.concatenate([taps, jnp.zeros((width, cols - count), jnp.float32)], axis=1)
        gain = jnp.sum(pick * gain_ref[s : s + 1, :], axis=1, keepdims=True) * (1.0 / scale)
        at = sections * span + held + s * width
        out_ref[at : at + width] = jnp.broadcast_to(gain, (width, 2 * cols))
        for g in range(groups):
            own = slice(g * LANES, (g + 1) * LANES)
            spread = jnp.concatenate([short[own]] * copies, axis=0)
            turned = jnp.concatenate([spread * cosine, -(spread * sine)], axis=1).astype(bf)
            at = s * span + g * high
            out_ref[at : at + high] = dot(turned, table_ref[: 2 * cols, : 2 * cols]) * weight


def main_kernel(width, sections, in_ref, short_ref, table_ref, out_ref):
    total, cols = in_ref.shape
    rows = total // (2 * width * sections)
    groups = width // LANES
    high = (rows + 1) * LANES
    span = groups * high
    bf = jnp.bfloat16
    held = -(-(rows + 1) // LANES) * LANES
    turn = repeated(short_ref[sections * span : sections * span + held], rows + 1)
    cosine, sine = turn[:, :cols], turn[:, cols:]
    all_cos = jnp.concatenate([cosine] * groups, axis=0)
    all_sin = jnp.concatenate([sine] * groups, axis=0)
    forward_cols = table_ref[: 2 * cols, : 2 * cols]
    level, minus = table_ref[:cols, :cols], table_ref[:cols, cols : 2 * cols]
    plus = table_ref[cols : 2 * cols, :cols]
    back_cols = jnp.concatenate(
        [jnp.concatenate([level, plus], axis=1), jnp.concatenate([minus, level], axis=1)], axis=0
    )
    forward_rows = table_ref[2 * cols : 2 * cols + 2 * high, : rows * LANES]
    wide_rows = forward_rows.astype(jnp.float32)
    some_rows = jnp.concatenate([wide_rows[LANES:high], wide_rows[high + LANES :]], axis=0)
    back_rows = dot_rows(identity(rows * LANES), some_rows.astype(bf)).astype(bf)

    def chunk(s):
        part = in_ref[s * rows * 2 * width : (s + 1) * rows * 2 * width]
        return part.astype(jnp.float32).reshape(rows, 2 * width, cols)

    def forward(grids):
        turned = []
        for grid in grids:
            for g in range(groups):
                block = grid[:, g * LANES : (g + 1) * LANES].reshape(rows * LANES, cols).astype(bf)
                spread = dot(forward_rows, block)
                real, imag = spread[:high], spread[high:]
                turned.append(
                    jnp.concatenate(
                        [real * cosine + imag * sine, imag * cosine - real * sine], axis=1
                    )
                )
        return dot(jnp.concatenate(turned, axis=0).astype(bf), forward_cols)

    def times(left, right):
        lr, li = left[:, :cols], left[:, cols:]
        rr, ri = right
        return jnp.concatenate([lr * rr - li * ri, lr * ri + li * rr], axis=1).astype(bf)

    def back(product):
        flat = dot(product, back_cols)
        real, imag = flat[:, :cols], flat[:, cols:]
        turned_real = real * all_cos - imag * all_sin
        turned_imag = real * all_sin + imag * all_cos
        pieces = []
        for g in range(groups):
            start = g * high
            part = slice(start + LANES, start + high)
            both = jnp.concatenate([turned_real[part], turned_imag[part]], axis=0).astype(bf)
            piece = dot(back_rows, both).reshape(rows, LANES, cols)
            pieces.append(piece + turned_real[start : start + LANES][None])
        return jnp.concatenate(pieces, axis=1)

    def combine(s, spec):
        at = sections * span + held + s * width
        gains = short_ref[at : at + width, :cols]
        shift = jnp.concatenate(
            [gains[g * LANES : (g + 1) * LANES] for g in range(groups) for _ in range(rows + 1)], axis=0
        )
        own = slice(s * span, (s + 1) * span)
        lr, li = spec[:, :cols] + shift, spec[:, cols:]
        rr, ri = short_ref[own, :cols], short_ref[own, cols:]
        return lr * rr - li * ri, lr * ri + li * rr

    chunks = [chunk(s) for s in range(sections)]
    specs = forward([chunks[0][:, :width]] + [part[:, width:] for part in chunks])
    signal_spec = specs[:span]
    for s in range(sections):
        mixed = combine(s, specs[(s + 1) * span : (s + 2) * span])
        result = back(times(signal_spec, mixed))
        rounded = result.reshape(rows * width, cols).astype(bf)
        out_ref[s * rows * width : (s + 1) * rows * width] = rounded
        if s + 1 < sections:
            gated = rounded.astype(jnp.float32).reshape(rows, width, cols) * chunks[s + 1][:, :width]
            signal_spec = forward([gated])


def body(activations, short_filters, long_filters, skip_gain):
    sections = short_filters.shape[0]
    tokens, channels = activations.shape[1:]
    devices = lax.axis_size(BOTH)
    seq_devices = lax.axis_size("seq")
    owned = channels // devices
    width = -(-owned // LANES) * LANES
    cols = tokens
    laid = devices * width

    def widen(array):
        split = array.reshape(array.shape[:2] + (devices, owned))
        split = jnp.pad(split, ((0, 0), (0, 0), (0, 0), (0, width - owned)))
        return split.reshape(array.shape[:2] + (laid,))

    def exchanged(array, height):
        chunks = array.reshape(devices, height, cols)
        moved = lax.all_to_all(chunks, BOTH, split_axis=0, concat_axis=0, tiled=True)
        return moved.reshape(devices * height, cols)

    def grant(size):
        return pltpu.CompilerParams(vmem_limit_bytes=int(size))

    acts, filters = activations, long_filters
    if width != owned:
        acts, filters = widen(acts), widen(filters)
    table, turn = tables(seq_devices, cols)
    vmem = pl.BlockSpec(memory_space=pltpu.VMEM)
    hbm = pl.BlockSpec(memory_space=pltpu.HBM)
    area = laid * cols
    span = (seq_devices + 1) * width
    steps = send_steps(width, laid)[1]
    outgoing = pl.pallas_call(
        functools.partial(send_kernel, width),
        out_shape=jax.ShapeDtypeStruct((2 * laid, cols), jnp.bfloat16),
        in_specs=[hbm, hbm],
        out_specs=hbm,
        scratch_shapes=[
            pltpu.VMEM((cols, laid), jnp.bfloat16),
            pltpu.VMEM((cols, laid), jnp.float32),
            pltpu.VMEM((2 * laid, cols), jnp.bfloat16),
            pltpu.SemaphoreType.DMA((2 * steps,)),
            pltpu.SemaphoreType.DMA((steps,)),
        ],
        compiler_params=grant(56 * MIB),
    )(acts, filters)
    arrived = exchanged(outgoing, 2 * width)
    place = lax.axis_index(BOTH).astype(jnp.int32).reshape(1)
    held = sections * (span + width) + turn.shape[0]
    short_spec = pl.pallas_call(
        functools.partial(short_kernel, width, owned, seq_devices),
        out_shape=jax.ShapeDtypeStruct((held, 2 * cols), jnp.float32),
        in_specs=[pl.BlockSpec(memory_space=pltpu.SMEM)] + [vmem] * 4,
        out_specs=vmem,
        compiler_params=grant(2 * MIB + 8 * held * cols + 2 * table.size + 4 * turn.size),
        cost_estimate=pl.CostEstimate(
            flops=8 * sections * span * cols * cols, bytes_accessed=8 * MIB, transcendentals=0
        ),
    )(place, short_filters, skip_gain, turn, table)
    results = pl.pallas_call(
        functools.partial(main_kernel, width, sections),
        out_shape=jax.ShapeDtypeStruct((laid, cols), jnp.bfloat16),
        in_specs=[vmem] * 3,
        out_specs=vmem,
        compiler_params=grant(MIB + 6 * area + 8 * held * cols + 2 * table.size + 32 * span * cols),
    )(arrived, short_spec, table)
    returned = exchanged(results, width)
    final = pl.pallas_call(
        final_kernel,
        out_shape=jax.ShapeDtypeStruct((1, cols, laid), jnp.bfloat16),
        compiler_params=grant(4 * MIB + 16 * area),
    )(returned)
    if width != owned:
        final = final.reshape(1, cols, devices, width)[..., :owned].reshape(1, cols, channels)
    return final


def solution(mesh):
    return jax.shard_map(
        body,
        mesh=mesh,
        in_specs=(P("segment", "seq", None), P(), P("segment", "seq", None), P()),
        out_specs=P("segment", "seq", None),
        check_vma=False,
    )
```

```python
import functools
import math

import jax
import jax.numpy as jnp
import numpy as np
from jax import lax
from jax.experimental import pallas as pl
from jax.experimental.pallas import tpu as pltpu
from jax.sharding import PartitionSpec as P

BOTH = ("segment", "seq")
LANES = 8
MIB = 1024 * 1024


def tables(real_rows, cols):
    grid_rows = 2 * real_rows + 1
    length = grid_rows * cols
    freqs = real_rows + 1
    k = np.arange(freqs)
    rows = 2.0 * math.pi * ((k[:, None] * np.arange(real_rows)[None, :]) % grid_rows) / grid_rows
    first = np.stack([np.cos(rows), -np.sin(rows)]).reshape(2 * freqs, real_rows)
    row_part = np.kron(first, np.eye(LANES))
    b = np.arange(cols)
    angle = 2.0 * math.pi * (k[:, None] * b[None, :]) / length
    turn = np.concatenate([np.cos(angle), np.sin(angle)], axis=1)
    turn = np.pad(turn, ((0, -freqs % LANES), (0, 0)))
    grid = 2.0 * math.pi * ((b[:, None] * b[None, :]) % cols) / cols
    c, s = np.cos(grid), np.sin(grid)
    parts = [np.block([[c, -s], [s, c]]), row_part]
    lanes = max(part.shape[1] for part in parts)
    stacked = np.concatenate([np.pad(p, ((0, 0), (0, lanes - p.shape[1]))) for p in parts])
    return jnp.asarray(stacked, jnp.bfloat16), jnp.asarray(turn, jnp.float32)


def dot(a, b):
    return jnp.dot(a, b, preferred_element_type=jnp.float32)


def dot_rows(a, b):
    return lax.dot_general(a, b, (((1,), (1,)), ((), ())), preferred_element_type=jnp.float32)


def repeated(rows, count):
    return jnp.concatenate(
        [jnp.broadcast_to(rows[k : k + 1], (LANES, rows.shape[1])) for k in range(count)], axis=0
    )


def identity(size):
    down = lax.broadcasted_iota(jnp.int32, (size, size), 0)
    across = lax.broadcasted_iota(jnp.int32, (size, size), 1)
    return jnp.where(down == across, 1.0, 0.0).astype(jnp.bfloat16)


def send_steps(width, channels):
    step = math.lcm(width, 128)
    while 2 * step <= 512 and channels % (2 * step) == 0:
        step = 2 * step
    return step, channels // step


def send_kernel(
    width,
    owned,
    place_ref,
    act_ref,
    filt_ref,
    taps_ref,
    gain_ref,
    out_ref,
    own_ref,
    act_held,
    filt_held,
    taps_held,
    gain_held,
    in_sem,
    own_sem,
):
    step, count = send_steps(width, act_ref.shape[2])
    sections, length, channels = taps_ref.shape
    mine_first = (
        pltpu.make_async_copy(taps_ref, taps_held, own_sem.at[0]),
        pltpu.make_async_copy(gain_ref, gain_held, own_sem.at[1]),
    )
    for copy in mine_first:
        copy.start()
    arriving = []
    for n in range(count):
        part = pl.ds(n * step, step)
        pair = (
            pltpu.make_async_copy(filt_ref.at[0, :, part], filt_held.at[:, part], in_sem.at[2 * n]),
            pltpu.make_async_copy(act_ref.at[0, :, part], act_held.at[:, part], in_sem.at[2 * n + 1]),
        )
        for copy in pair:
            copy.start()
        arriving.append(pair)
    eye = identity(128)
    mine = lax.broadcasted_iota(jnp.int32, (width, channels), 0)
    them = lax.broadcasted_iota(jnp.int32, (width, channels), 1)
    pick = jnp.where((them == mine + place_ref[0] * owned) & (mine < owned), 1.0, 0.0)
    for copy in mine_first:
        copy.wait()
    for s in range(sections):
        gain = jnp.sum(pick * gain_held[s : s + 1, :], axis=1, keepdims=True)
        own_ref[s * width : (s + 1) * width, :length] = dot_rows(pick.astype(jnp.bfloat16), taps_held[s])
        own_ref[s * width : (s + 1) * width, length:] = jnp.broadcast_to(gain, (width, 128))
    for n in range(count):
        for copy in arriving[n]:
            copy.wait()
        acts, filts = [], []
        for start in range(n * step, (n + 1) * step, 128):
            part = slice(start, start + 128)
            acts.append(dot_rows(eye, act_held[:, part]))
            filts.append(dot_rows(eye, filt_held[:, part].astype(jnp.bfloat16)))
        act = jnp.concatenate(acts, axis=0)
        filt = jnp.concatenate(filts, axis=0)
        pieces = []
        for d in range(step // width):
            part = slice(d * width, (d + 1) * width)
            pieces += [act[part], filt[part]]
        whole = slice(2 * n * step, 2 * (n + 1) * step)
        out_ref[whole] = jnp.concatenate(pieces, axis=0).astype(jnp.bfloat16)


def final_kernel(in_ref, out_ref):
    channels, tokens = in_ref.shape
    step = math.gcd(channels, 256)
    eye = identity(tokens)
    for start in range(0, channels, step):
        part = slice(start, start + step)
        out_ref[0, :, part] = dot_rows(eye, in_ref[part]).astype(jnp.bfloat16)


def main_kernel(width, sections, in_ref, own_ref, turn_ref, table_ref, out_ref):
    total, cols = in_ref.shape
    rows = total // (2 * width * sections)
    groups = width // LANES
    high = (rows + 1) * LANES
    span = groups * high
    bf = jnp.bfloat16
    copies = rows + 1
    length = own_ref.shape[1] - 128
    scale = 1.0 / math.sqrt(rows * cols)
    whole = (2 * rows + 1) * cols
    turn = repeated(turn_ref[...], copies)
    cosine, sine = turn[:, :cols], turn[:, cols:]
    all_cos = jnp.concatenate([cosine] * groups, axis=0)
    all_sin = jnp.concatenate([sine] * groups, axis=0)
    forward_cols = table_ref[: 2 * cols, : 2 * cols]
    level, minus = table_ref[:cols, :cols], table_ref[:cols, cols : 2 * cols]
    plus = table_ref[cols : 2 * cols, :cols]
    back_cols = jnp.concatenate(
        [jnp.concatenate([level, plus], axis=1), jnp.concatenate([minus, level], axis=1)], axis=0
    )
    forward_rows = table_ref[2 * cols : 2 * cols + 2 * high, : rows * LANES]
    wide_rows = forward_rows.astype(jnp.float32)
    some_rows = jnp.concatenate([wide_rows[LANES:high], wide_rows[high + LANES :]], axis=0)
    back_rows = dot_rows(identity(rows * LANES), some_rows.astype(bf)).astype(bf)

    def chunk(s):
        part = in_ref[s * rows * 2 * width : (s + 1) * rows * 2 * width]
        return part.astype(jnp.float32).reshape(rows, 2 * width, cols)

    def forward(grids):
        turned = []
        for grid in grids:
            for g in range(groups):
                block = grid[:, g * LANES : (g + 1) * LANES].reshape(rows * LANES, cols).astype(bf)
                spread = dot(forward_rows, block)
                real, imag = spread[:high], spread[high:]
                turned.append(
                    jnp.concatenate(
                        [real * cosine + imag * sine, imag * cosine - real * sine], axis=1
                    )
                )
        return dot(jnp.concatenate(turned, axis=0).astype(bf), forward_cols)

    def times(left, right):
        lr, li = left[:, :cols], left[:, cols:]
        rr, ri = right
        return jnp.concatenate([lr * rr - li * ri, lr * ri + li * rr], axis=1).astype(bf)

    def back(product):
        flat = dot(product, back_cols)
        real, imag = flat[:, :cols], flat[:, cols:]
        turned_real = real * all_cos - imag * all_sin
        turned_imag = real * all_sin + imag * all_cos
        pieces = []
        for g in range(groups):
            start = g * high
            part = slice(start + LANES, start + high)
            both = jnp.concatenate([turned_real[part], turned_imag[part]], axis=0).astype(bf)
            piece = dot(back_rows, both).reshape(rows, LANES, cols)
            pieces.append(piece + turned_real[start : start + LANES][None])
        return jnp.concatenate(pieces, axis=1)

    def short_specs():
        turned = []
        for s in range(sections):
            for g in range(groups):
                start = s * width + g * LANES
                taps = jnp.concatenate([own_ref[start : start + LANES, :length]] * copies, axis=0)
                turned.append(
                    jnp.concatenate([taps * cosine[:, :length], -(taps * sine[:, :length])], axis=1)
                )
        columns = jnp.concatenate([table_ref[:length, : 2 * cols], table_ref[cols : cols + length, : 2 * cols]])
        return dot(jnp.concatenate(turned, axis=0).astype(bf), columns)

    row = lax.broadcasted_iota(jnp.int32, (high, 1), 0)
    weight = jnp.where(row < LANES, scale / whole, 2.0 * scale / whole)
    weights = jnp.concatenate([weight] * groups, axis=0)
    shorts = short_specs()

    def combine(s, spec):
        gains = own_ref[s * width : (s + 1) * width, length:] * (1.0 / scale)
        gains = jnp.concatenate([gains] * (cols // 128), axis=1)
        shift = jnp.concatenate(
            [gains[g * LANES : (g + 1) * LANES] for g in range(groups) for _ in range(copies)], axis=0
        )
        short = shorts[s * span : (s + 1) * span] * weights
        lr, li = spec[:, :cols] + shift, spec[:, cols:]
        rr, ri = short[:, :cols], short[:, cols:]
        return lr * rr - li * ri, lr * ri + li * rr

    chunks = [chunk(s) for s in range(sections)]
    specs = forward([chunks[0][:, :width]] + [part[:, width:] for part in chunks])
    signal_spec = specs[:span]
    for s in range(sections):
        mixed = combine(s, specs[(s + 1) * span : (s + 2) * span])
        result = back(times(signal_spec, mixed))
        rounded = result.reshape(rows * width, cols).astype(bf)
        out_ref[s * rows * width : (s + 1) * rows * width] = rounded
        if s + 1 < sections:
            gated = rounded.astype(jnp.float32).reshape(rows, width, cols) * chunks[s + 1][:, :width]
            signal_spec = forward([gated])


def body(activations, short_filters, long_filters, skip_gain):
    sections = short_filters.shape[0]
    tokens, channels = activations.shape[1:]
    devices = lax.axis_size(BOTH)
    seq_devices = lax.axis_size("seq")
    owned = channels // devices
    width = -(-owned // LANES) * LANES
    cols = tokens
    laid = devices * width

    def widen(array):
        split = array.reshape(array.shape[:2] + (devices, owned))
        split = jnp.pad(split, ((0, 0), (0, 0), (0, 0), (0, width - owned)))
        return split.reshape(array.shape[:2] + (laid,))

    def exchanged(array, height):
        chunks = array.reshape(devices, height, cols)
        moved = lax.all_to_all(chunks, BOTH, split_axis=0, concat_axis=0, tiled=True)
        return moved.reshape(devices * height, cols)

    def grant(size):
        return pltpu.CompilerParams(vmem_limit_bytes=int(size))

    acts, filters = activations, long_filters
    if width != owned:
        acts, filters = widen(acts), widen(filters)
    table, turn = tables(seq_devices, cols)
    vmem = pl.BlockSpec(memory_space=pltpu.VMEM)
    hbm = pl.BlockSpec(memory_space=pltpu.HBM)
    area = laid * cols
    span = (seq_devices + 1) * width
    taps = short_filters.shape[1]
    steps = send_steps(width, laid)[1]
    place = lax.axis_index(BOTH).astype(jnp.int32).reshape(1)
    inputs = (acts, filters, short_filters, skip_gain)
    outgoing, own = pl.pallas_call(
        functools.partial(send_kernel, width, owned),
        out_shape=(
            jax.ShapeDtypeStruct((2 * laid, cols), jnp.bfloat16),
            jax.ShapeDtypeStruct((sections * width, taps + 128), jnp.float32),
        ),
        in_specs=[pl.BlockSpec(memory_space=pltpu.SMEM)] + [hbm] * 4,
        out_specs=(vmem, vmem),
        scratch_shapes=[
            pltpu.VMEM((cols, laid), jnp.bfloat16),
            pltpu.VMEM((cols, laid), jnp.float32),
            pltpu.VMEM(short_filters.shape, jnp.bfloat16),
            pltpu.VMEM(skip_gain.shape, jnp.float32),
            pltpu.SemaphoreType.DMA((2 * steps,)),
            pltpu.SemaphoreType.DMA((2,)),
        ],
        compiler_params=grant(4 * MIB + 24 * area),
    )(place, *(pltpu.with_memory_space_constraint(array, pltpu.HBM) for array in inputs))
    arrived = exchanged(outgoing, 2 * width)
    results = pl.pallas_call(
        functools.partial(main_kernel, width, sections),
        out_shape=jax.ShapeDtypeStruct((laid, cols), jnp.bfloat16),
        in_specs=[vmem] * 4,
        out_specs=vmem,
        compiler_params=grant(2 * MIB + 6 * area + 2 * table.size + 64 * span * cols),
    )(arrived, own, turn, table)
    returned = exchanged(results, width)
    final = pl.pallas_call(
        final_kernel,
        out_shape=jax.ShapeDtypeStruct((1, cols, laid), jnp.bfloat16),
        compiler_params=grant(4 * MIB + 16 * area),
    )(returned)
    if width != owned:
        final = final.reshape(1, cols, devices, width)[..., :owned].reshape(1, cols, channels)
    return final


def solution(mesh):
    return jax.shard_map(
        body,
        mesh=mesh,
        in_specs=(P("segment", "seq", None), P(), P("segment", "seq", None), P()),
        out_specs=P("segment", "seq", None),
        check_vma=False,
    )
```

```python
import functools
import math

import jax
import jax.numpy as jnp
import numpy as np
from jax import lax
from jax.experimental import pallas as pl
from jax.experimental.pallas import tpu as pltpu
from jax.sharding import PartitionSpec as P

BOTH = ("segment", "seq")
LANES = 8
MIB = 1024 * 1024


def apart(index, count):
    if count & (count - 1):
        return index
    bits = count.bit_length() - 1
    return sum(((index >> i) & 1) << (bits - 1 - i) for i in range(bits))


def tables(real_rows, cols):
    grid_rows = 2 * real_rows + 1
    length = grid_rows * cols
    freqs = real_rows + 1
    k = np.arange(freqs)
    rows = 2.0 * math.pi * ((k[:, None] * np.arange(real_rows)[None, :]) % grid_rows) / grid_rows
    first = np.stack([np.cos(rows), -np.sin(rows)]).reshape(2 * freqs, real_rows)
    row_part = np.kron(first, np.eye(LANES))
    b = np.arange(cols)
    angle = 2.0 * math.pi * (k[:, None] * b[None, :]) / length
    turn = np.concatenate([np.cos(angle), np.sin(angle)], axis=1)
    turn = np.pad(turn, ((0, -freqs % LANES), (0, 0)))
    grid = 2.0 * math.pi * ((b[:, None] * b[None, :]) % cols) / cols
    c, s = np.cos(grid), np.sin(grid)
    parts = [np.block([[c, -s], [s, c]]), row_part]
    lanes = max(part.shape[1] for part in parts)
    stacked = np.concatenate([np.pad(p, ((0, 0), (0, lanes - p.shape[1]))) for p in parts])
    return jnp.asarray(stacked, jnp.bfloat16), jnp.asarray(turn, jnp.float32)


def dot(a, b):
    return jnp.dot(a, b, preferred_element_type=jnp.float32)


def dot_rows(a, b):
    return lax.dot_general(a, b, (((1,), (1,)), ((), ())), preferred_element_type=jnp.float32)


def repeated(rows, count):
    return jnp.concatenate(
        [jnp.broadcast_to(rows[k : k + 1], (LANES, rows.shape[1])) for k in range(count)], axis=0
    )


def identity(size):
    down = lax.broadcasted_iota(jnp.int32, (size, size), 0)
    across = lax.broadcasted_iota(jnp.int32, (size, size), 1)
    return jnp.where(down == across, 1.0, 0.0).astype(jnp.bfloat16)


def send_steps(width, channels):
    step = math.lcm(width, 128)
    while 2 * step <= 512 and channels % (2 * step) == 0:
        step = 2 * step
    return step, channels // step


def send_kernel(
    width,
    owned,
    seq_devices,
    place_ref,
    act_ref,
    filt_ref,
    taps_ref,
    gain_ref,
    out_ref,
    own_ref,
    act_held,
    filt_held,
    taps_held,
    gain_held,
    in_sem,
    own_sem,
):
    step, count = send_steps(width, act_ref.shape[2])
    sections, length, channels = taps_ref.shape
    mine_first = (
        pltpu.make_async_copy(taps_ref, taps_held, own_sem.at[0]),
        pltpu.make_async_copy(gain_ref, gain_held, own_sem.at[1]),
    )
    for copy in mine_first:
        copy.start()
    arriving = []
    for n in range(count):
        part = pl.ds(n * step, step)
        pair = (
            pltpu.make_async_copy(filt_ref.at[0, :, part], filt_held.at[:, part], in_sem.at[2 * n]),
            pltpu.make_async_copy(act_ref.at[0, :, part], act_held.at[:, part], in_sem.at[2 * n + 1]),
        )
        for copy in pair:
            copy.start()
        arriving.append(pair)
    eye = identity(128)
    mine = lax.broadcasted_iota(jnp.int32, (width, channels), 0)
    them = lax.broadcasted_iota(jnp.int32, (width, channels), 1)
    part_of, in_seq = lax.div(place_ref[0], seq_devices), lax.rem(place_ref[0], seq_devices)
    place = part_of * seq_devices + apart(in_seq, seq_devices)
    pick = jnp.where((them == mine + place * owned) & (mine < owned), 1.0, 0.0)
    for copy in mine_first:
        copy.wait()
    for s in range(sections):
        gain = jnp.sum(pick * gain_held[s : s + 1, :], axis=1, keepdims=True)
        own_ref[s * width : (s + 1) * width, :length] = dot_rows(pick.astype(jnp.bfloat16), taps_held[s])
        own_ref[s * width : (s + 1) * width, length:] = jnp.broadcast_to(gain, (width, 128))
    for n in range(count):
        for copy in arriving[n]:
            copy.wait()
        acts, filts = [], []
        for start in range(n * step, (n + 1) * step, 128):
            part = slice(start, start + 128)
            acts.append(dot_rows(eye, act_held[:, part]))
            filts.append(dot_rows(eye, filt_held[:, part].astype(jnp.bfloat16)))
        act = jnp.concatenate(acts, axis=0)
        filt = jnp.concatenate(filts, axis=0)
        pieces = []
        for d in range(step // width):
            part = slice(d * width, (d + 1) * width)
            pieces += [act[part], filt[part]]
        whole = slice(2 * n * step, 2 * (n + 1) * step)
        out_ref[whole] = jnp.concatenate(pieces, axis=0).astype(jnp.bfloat16)


def final_kernel(in_ref, out_ref):
    channels, tokens = in_ref.shape
    step = math.gcd(channels, 256)
    eye = identity(tokens)
    for start in range(0, channels, step):
        part = slice(start, start + step)
        out_ref[0, :, part] = dot_rows(eye, in_ref[part]).astype(jnp.bfloat16)


def main_kernel(width, sections, in_ref, own_ref, turn_ref, table_ref, out_ref):
    total, cols = in_ref.shape
    rows = total // (2 * width * sections)
    groups = width // LANES
    high = (rows + 1) * LANES
    span = groups * high
    bf = jnp.bfloat16
    copies = rows + 1
    length = own_ref.shape[1] - 128
    scale = 1.0 / math.sqrt(rows * cols)
    whole = (2 * rows + 1) * cols
    turn = repeated(turn_ref[...], copies)
    cosine, sine = turn[:, :cols], turn[:, cols:]
    all_cos = jnp.concatenate([cosine] * groups, axis=0)
    all_sin = jnp.concatenate([sine] * groups, axis=0)
    forward_cols = table_ref[: 2 * cols, : 2 * cols]
    level, minus = table_ref[:cols, :cols], table_ref[:cols, cols : 2 * cols]
    plus = table_ref[cols : 2 * cols, :cols]
    back_cols = jnp.concatenate(
        [jnp.concatenate([level, plus], axis=1), jnp.concatenate([minus, level], axis=1)], axis=0
    )
    forward_rows = table_ref[2 * cols : 2 * cols + 2 * high, : rows * LANES]
    wide_rows = forward_rows.astype(jnp.float32)
    some_rows = jnp.concatenate([wide_rows[LANES:high], wide_rows[high + LANES :]], axis=0)
    back_rows = dot_rows(identity(rows * LANES), some_rows.astype(bf)).astype(bf)

    def chunk(s):
        starts = [(s * rows + apart(a, rows)) * 2 * width for a in range(rows)]
        part = jnp.concatenate([in_ref[at : at + 2 * width] for at in starts], axis=0)
        return part.astype(jnp.float32).reshape(rows, 2 * width, cols)

    def forward(grids):
        turned = []
        for grid in grids:
            for g in range(groups):
                block = grid[:, g * LANES : (g + 1) * LANES].reshape(rows * LANES, cols).astype(bf)
                spread = dot(forward_rows, block)
                real, imag = spread[:high], spread[high:]
                turned.append(
                    jnp.concatenate(
                        [real * cosine + imag * sine, imag * cosine - real * sine], axis=1
                    )
                )
        return dot(jnp.concatenate(turned, axis=0).astype(bf), forward_cols)

    def times(left, right):
        lr, li = left[:, :cols], left[:, cols:]
        rr, ri = right
        return jnp.concatenate([lr * rr - li * ri, lr * ri + li * rr], axis=1).astype(bf)

    def back(product):
        flat = dot(product, back_cols)
        real, imag = flat[:, :cols], flat[:, cols:]
        turned_real = real * all_cos - imag * all_sin
        turned_imag = real * all_sin + imag * all_cos
        pieces = []
        for g in range(groups):
            start = g * high
            part = slice(start + LANES, start + high)
            both = jnp.concatenate([turned_real[part], turned_imag[part]], axis=0).astype(bf)
            piece = dot(back_rows, both).reshape(rows, LANES, cols)
            pieces.append(piece + turned_real[start : start + LANES][None])
        return jnp.concatenate(pieces, axis=1)

    def short_specs():
        turned = []
        for s in range(sections):
            for g in range(groups):
                start = s * width + g * LANES
                taps = jnp.concatenate([own_ref[start : start + LANES, :length]] * copies, axis=0)
                turned.append(
                    jnp.concatenate([taps * cosine[:, :length], -(taps * sine[:, :length])], axis=1)
                )
        columns = jnp.concatenate([table_ref[:length, : 2 * cols], table_ref[cols : cols + length, : 2 * cols]])
        return dot(jnp.concatenate(turned, axis=0).astype(bf), columns)

    row = lax.broadcasted_iota(jnp.int32, (high, 1), 0)
    weight = jnp.where(row < LANES, scale / whole, 2.0 * scale / whole)
    weights = jnp.concatenate([weight] * groups, axis=0)
    shorts = short_specs()

    def combine(s, spec):
        gains = own_ref[s * width : (s + 1) * width, length:] * (1.0 / scale)
        gains = jnp.concatenate([gains] * (cols // 128), axis=1)
        shift = jnp.concatenate(
            [gains[g * LANES : (g + 1) * LANES] for g in range(groups) for _ in range(copies)], axis=0
        )
        short = shorts[s * span : (s + 1) * span] * weights
        lr, li = spec[:, :cols] + shift, spec[:, cols:]
        rr, ri = short[:, :cols], short[:, cols:]
        return lr * rr - li * ri, lr * ri + li * rr

    chunks = [chunk(s) for s in range(sections)]
    specs = forward([chunks[0][:, :width]] + [part[:, width:] for part in chunks])
    signal_spec = specs[:span]
    for s in range(sections):
        mixed = combine(s, specs[(s + 1) * span : (s + 2) * span])
        result = back(times(signal_spec, mixed))
        rounded = result.reshape(rows * width, cols).astype(bf)
        for at in range(0, rows, 2):
            pair = jnp.concatenate([result[apart(at, rows)], result[apart(at + 1, rows)]], axis=0)
            out_ref[(s * rows + at) * width : (s * rows + at + 2) * width] = pair.astype(bf)
        if s + 1 < sections:
            gated = rounded.astype(jnp.float32).reshape(rows, width, cols) * chunks[s + 1][:, :width]
            signal_spec = forward([gated])


def body(activations, short_filters, long_filters, skip_gain):
    sections = short_filters.shape[0]
    tokens, channels = activations.shape[1:]
    devices = lax.axis_size(BOTH)
    seq_devices = lax.axis_size("seq")
    owned = channels // devices
    width = -(-owned // LANES) * LANES
    cols = tokens
    laid = devices * width
    order = [
        s * seq_devices + apart(q, seq_devices)
        for s in range(devices // seq_devices)
        for q in range(seq_devices)
    ]

    def widen(array):
        split = array.reshape(array.shape[:2] + (devices, owned))
        split = jnp.pad(split, ((0, 0), (0, 0), (0, 0), (0, width - owned)))
        return split.reshape(array.shape[:2] + (laid,))

    def exchanged(array, height):
        chunks = array.reshape(devices, height, cols)
        moved = lax.all_to_all(
            chunks, BOTH, split_axis=0, concat_axis=0, tiled=True, axis_index_groups=[order]
        )
        return moved.reshape(devices * height, cols)

    def grant(size):
        return pltpu.CompilerParams(vmem_limit_bytes=int(size))

    acts, filters = activations, long_filters
    if width != owned:
        acts, filters = widen(acts), widen(filters)
    table, turn = tables(seq_devices, cols)
    vmem = pl.BlockSpec(memory_space=pltpu.VMEM)
    hbm = pl.BlockSpec(memory_space=pltpu.HBM)
    area = laid * cols
    span = (seq_devices + 1) * width
    taps = short_filters.shape[1]
    steps = send_steps(width, laid)[1]
    place = lax.axis_index(BOTH).astype(jnp.int32).reshape(1)
    inputs = (acts, filters, short_filters, skip_gain)
    outgoing, own = pl.pallas_call(
        functools.partial(send_kernel, width, owned, seq_devices),
        out_shape=(
            jax.ShapeDtypeStruct((2 * laid, cols), jnp.bfloat16),
            jax.ShapeDtypeStruct((sections * width, taps + 128), jnp.float32),
        ),
        in_specs=[pl.BlockSpec(memory_space=pltpu.SMEM)] + [hbm] * 4,
        out_specs=(vmem, vmem),
        scratch_shapes=[
            pltpu.VMEM((cols, laid), jnp.bfloat16),
            pltpu.VMEM((cols, laid), jnp.float32),
            pltpu.VMEM(short_filters.shape, jnp.bfloat16),
            pltpu.VMEM(skip_gain.shape, jnp.float32),
            pltpu.SemaphoreType.DMA((2 * steps,)),
            pltpu.SemaphoreType.DMA((2,)),
        ],
        compiler_params=grant(4 * MIB + 24 * area),
    )(place, *(pltpu.with_memory_space_constraint(array, pltpu.HBM) for array in inputs))
    arrived = exchanged(outgoing, 2 * width)
    results = pl.pallas_call(
        functools.partial(main_kernel, width, sections),
        out_shape=jax.ShapeDtypeStruct((laid, cols), jnp.bfloat16),
        in_specs=[vmem] * 4,
        out_specs=vmem,
        compiler_params=grant(2 * MIB + 6 * area + 2 * table.size + 64 * span * cols),
    )(arrived, own, turn, table)
    returned = exchanged(results, width)
    final = pl.pallas_call(
        final_kernel,
        out_shape=jax.ShapeDtypeStruct((1, cols, laid), jnp.bfloat16),
        compiler_params=grant(4 * MIB + 16 * area),
    )(returned)
    if width != owned:
        final = final.reshape(1, cols, devices, width)[..., :owned].reshape(1, cols, channels)
    return final


def solution(mesh):
    return jax.shard_map(
        body,
        mesh=mesh,
        in_specs=(P("segment", "seq", None), P(), P("segment", "seq", None), P()),
        out_specs=P("segment", "seq", None),
        check_vma=False,
    )
```

```python
import functools
import math

import jax
import jax.numpy as jnp
import numpy as np
from jax import lax
from jax.experimental import pallas as pl
from jax.experimental.pallas import tpu as pltpu
from jax.sharding import PartitionSpec as P

BOTH = ("segment", "seq")
LANES = 8
MIB = 1024 * 1024


FIELDS = {2: 7, 3: 11, 4: 19, 5: 37, 6: 67, 7: 131, 8: 285, 9: 529, 10: 1033}


def spread_order(devices):
    bits = devices.bit_length() - 1
    if devices != 1 << bits or bits not in FIELDS:
        return tuple(range(devices))
    order, power = [0], 1
    while len(order) < devices:
        order.append(power)
        power <<= 1
        if power & devices:
            power ^= FIELDS[bits]
    return tuple(order)


def tables(real_rows, cols):
    grid_rows = 2 * real_rows + 1
    length = grid_rows * cols
    freqs = real_rows + 1
    k = np.arange(freqs)
    rows = 2.0 * math.pi * ((k[:, None] * np.arange(real_rows)[None, :]) % grid_rows) / grid_rows
    first = np.stack([np.cos(rows), -np.sin(rows)]).reshape(2 * freqs, real_rows)
    row_part = np.kron(first, np.eye(LANES))
    b = np.arange(cols)
    angle = 2.0 * math.pi * (k[:, None] * b[None, :]) / length
    turn = np.concatenate([np.cos(angle), np.sin(angle)], axis=1)
    turn = np.pad(turn, ((0, -freqs % LANES), (0, 0)))
    grid = 2.0 * math.pi * ((b[:, None] * b[None, :]) % cols) / cols
    c, s = np.cos(grid), np.sin(grid)
    parts = [np.block([[c, -s], [s, c]]), row_part]
    lanes = max(part.shape[1] for part in parts)
    stacked = np.concatenate([np.pad(p, ((0, 0), (0, lanes - p.shape[1]))) for p in parts])
    return jnp.asarray(stacked, jnp.bfloat16), jnp.asarray(turn, jnp.float32)


def dot(a, b):
    return jnp.dot(a, b, preferred_element_type=jnp.float32)


def dot_rows(a, b):
    return lax.dot_general(a, b, (((1,), (1,)), ((), ())), preferred_element_type=jnp.float32)


def repeated(rows, count):
    return jnp.concatenate(
        [jnp.broadcast_to(rows[k : k + 1], (LANES, rows.shape[1])) for k in range(count)], axis=0
    )


def identity(size):
    down = lax.broadcasted_iota(jnp.int32, (size, size), 0)
    across = lax.broadcasted_iota(jnp.int32, (size, size), 1)
    return jnp.where(down == across, 1.0, 0.0).astype(jnp.bfloat16)


def send_steps(width, channels):
    step = math.lcm(width, 128)
    while 2 * step <= 512 and channels % (2 * step) == 0:
        step = 2 * step
    return step, channels // step


def send_kernel(
    width,
    owned,
    order,
    place_ref,
    act_ref,
    filt_ref,
    taps_ref,
    gain_ref,
    out_ref,
    own_ref,
    act_held,
    filt_held,
    taps_held,
    gain_held,
    in_sem,
    own_sem,
):
    step, count = send_steps(width, act_ref.shape[2])
    sections, length, channels = taps_ref.shape
    mine_first = (
        pltpu.make_async_copy(taps_ref, taps_held, own_sem.at[0]),
        pltpu.make_async_copy(gain_ref, gain_held, own_sem.at[1]),
    )
    for copy in mine_first:
        copy.start()
    arriving = []
    for n in range(act_ref.shape[2] // 128):
        part = pl.ds(n * 128, 128)
        pair = (
            pltpu.make_async_copy(filt_ref.at[0, :, part], filt_held.at[:, part], in_sem.at[2 * n]),
            pltpu.make_async_copy(act_ref.at[0, :, part], act_held.at[:, part], in_sem.at[2 * n + 1]),
        )
        for copy in pair:
            copy.start()
        arriving.append(pair)
    eye = identity(128)
    mine = lax.broadcasted_iota(jnp.int32, (width, channels), 0)
    them = lax.broadcasted_iota(jnp.int32, (width, channels), 1)
    place = jnp.int32(0)
    for position, rank in enumerate(order):
        place = place + jnp.where(place_ref[0] == rank, position, 0)
    pick = jnp.where((them == mine + place * owned) & (mine < owned), 1.0, 0.0)
    for copy in mine_first:
        copy.wait()
    for s in range(sections):
        gain = jnp.sum(pick * gain_held[s : s + 1, :], axis=1, keepdims=True)
        own_ref[s * width : (s + 1) * width, :length] = dot_rows(pick.astype(jnp.bfloat16), taps_held[s])
        own_ref[s * width : (s + 1) * width, length:] = jnp.broadcast_to(gain, (width, 128))
    for n in range(count):
        acts, filts = [], []
        for start in range(n * step, (n + 1) * step, 128):
            part = slice(start, start + 128)
            for copy in arriving[start // 128]:
                copy.wait()
            acts.append(dot_rows(eye, act_held[:, part]))
            filts.append(dot_rows(eye, filt_held[:, part].astype(jnp.bfloat16)))
        act = jnp.concatenate(acts, axis=0)
        filt = jnp.concatenate(filts, axis=0)
        pieces = []
        for d in range(step // width):
            part = slice(d * width, (d + 1) * width)
            pieces += [act[part], filt[part]]
        whole = slice(2 * n * step, 2 * (n + 1) * step)
        out_ref[whole] = jnp.concatenate(pieces, axis=0).astype(jnp.bfloat16)


def final_kernel(in_ref, out_ref):
    channels, tokens = in_ref.shape
    step = math.gcd(channels, 256)
    eye = identity(tokens)
    for start in range(0, channels, step):
        part = slice(start, start + step)
        out_ref[0, :, part] = dot_rows(eye, in_ref[part]).astype(jnp.bfloat16)


def main_kernel(width, sections, order, in_ref, own_ref, turn_ref, table_ref, out_ref):
    total, cols = in_ref.shape
    rows = total // (2 * width * sections)
    groups = width // LANES
    high = (rows + 1) * LANES
    span = groups * high
    bf = jnp.bfloat16
    copies = rows + 1
    length = own_ref.shape[1] - 128
    scale = 1.0 / math.sqrt(rows * cols)
    whole = (2 * rows + 1) * cols
    turn = repeated(turn_ref[...], copies)
    cosine, sine = turn[:, :cols], turn[:, cols:]
    all_cos = jnp.concatenate([cosine] * groups, axis=0)
    all_sin = jnp.concatenate([sine] * groups, axis=0)
    forward_cols = table_ref[: 2 * cols, : 2 * cols]
    level, minus = table_ref[:cols, :cols], table_ref[:cols, cols : 2 * cols]
    plus = table_ref[cols : 2 * cols, :cols]
    back_cols = jnp.concatenate(
        [jnp.concatenate([level, plus], axis=1), jnp.concatenate([minus, level], axis=1)], axis=0
    )
    forward_rows = table_ref[2 * cols : 2 * cols + 2 * high, : rows * LANES]
    wide_rows = forward_rows.astype(jnp.float32)
    some_rows = jnp.concatenate([wide_rows[LANES:high], wide_rows[high + LANES :]], axis=0)
    back_rows = dot_rows(identity(rows * LANES), some_rows.astype(bf)).astype(bf)

    def chunk(s):
        starts = [order.index(s * rows + a) * 2 * width for a in range(rows)]
        part = jnp.concatenate([in_ref[at : at + 2 * width] for at in starts], axis=0)
        return part.astype(jnp.float32).reshape(rows, 2 * width, cols)

    def forward(grids):
        turned = []
        for grid in grids:
            for g in range(groups):
                block = grid[:, g * LANES : (g + 1) * LANES].reshape(rows * LANES, cols).astype(bf)
                spread = dot(forward_rows, block)
                real, imag = spread[:high], spread[high:]
                turned.append(
                    jnp.concatenate(
                        [real * cosine + imag * sine, imag * cosine - real * sine], axis=1
                    )
                )
        return dot(jnp.concatenate(turned, axis=0).astype(bf), forward_cols)

    def times(left, right):
        lr, li = left[:, :cols], left[:, cols:]
        rr, ri = right
        return jnp.concatenate([lr * rr - li * ri, lr * ri + li * rr], axis=1).astype(bf)

    def back(product):
        flat = dot(product, back_cols)
        real, imag = flat[:, :cols], flat[:, cols:]
        turned_real = real * all_cos - imag * all_sin
        turned_imag = real * all_sin + imag * all_cos
        pieces = []
        for g in range(groups):
            start = g * high
            part = slice(start + LANES, start + high)
            both = jnp.concatenate([turned_real[part], turned_imag[part]], axis=0).astype(bf)
            piece = dot(back_rows, both).reshape(rows, LANES, cols)
            pieces.append(piece + turned_real[start : start + LANES][None])
        return jnp.concatenate(pieces, axis=1)

    def short_specs():
        turned = []
        for s in range(sections):
            for g in range(groups):
                start = s * width + g * LANES
                taps = jnp.concatenate([own_ref[start : start + LANES, :length]] * copies, axis=0)
                turned.append(
                    jnp.concatenate([taps * short_cos, taps * short_sin], axis=1)
                )
        columns = jnp.concatenate([table_ref[:length, : 2 * cols], table_ref[cols : cols + length, : 2 * cols]])
        return dot(jnp.concatenate(turned, axis=0).astype(bf), columns)

    row = lax.broadcasted_iota(jnp.int32, (high, 1), 0)
    weight = jnp.where(row < LANES, scale / whole, 2.0 * scale / whole)
    short_cos, short_sin = cosine[:, :length] * weight, -(sine[:, :length] * weight)
    shorts = short_specs()

    def combine(s, spec):
        gains = own_ref[s * width : (s + 1) * width, length:] * (1.0 / scale)
        gains = jnp.concatenate([gains] * (cols // 128), axis=1)
        shift = jnp.concatenate(
            [gains[g * LANES : (g + 1) * LANES] for g in range(groups) for _ in range(copies)], axis=0
        )
        short = shorts[s * span : (s + 1) * span]
        lr, li = spec[:, :cols] + shift, spec[:, cols:]
        rr, ri = short[:, :cols], short[:, cols:]
        return lr * rr - li * ri, lr * ri + li * rr

    chunks = [chunk(s) for s in range(sections)]
    specs = forward([chunks[0][:, :width]] + [part[:, width:] for part in chunks])
    signal_spec = specs[:span]
    results = []
    for s in range(sections):
        mixed = combine(s, specs[(s + 1) * span : (s + 2) * span])
        result = back(times(signal_spec, mixed))
        results.append(result)
        if s + 1 < sections:
            rounded = result.astype(bf).astype(jnp.float32)
            signal_spec = forward([rounded * chunks[s + 1][:, :width]])
    for at in range(0, len(order), 2):
        pair = [results[rank // rows][rank % rows] for rank in order[at : at + 2]]
        out_ref[at * width : (at + 2) * width] = jnp.concatenate(pair, axis=0).astype(bf)


def body(activations, short_filters, long_filters, skip_gain):
    sections = short_filters.shape[0]
    tokens, channels = activations.shape[1:]
    devices = lax.axis_size(BOTH)
    seq_devices = lax.axis_size("seq")
    owned = channels // devices
    width = -(-owned // LANES) * LANES
    cols = tokens
    laid = devices * width
    order = spread_order(devices)

    def widen(array):
        split = array.reshape(array.shape[:2] + (devices, owned))
        split = jnp.pad(split, ((0, 0), (0, 0), (0, 0), (0, width - owned)))
        return split.reshape(array.shape[:2] + (laid,))

    def exchanged(array, height):
        chunks = array.reshape(devices, height, cols)
        moved = lax.all_to_all(
            chunks, BOTH, split_axis=0, concat_axis=0, tiled=True, axis_index_groups=[list(order)]
        )
        return moved.reshape(devices * height, cols)

    def grant(size):
        return pltpu.CompilerParams(vmem_limit_bytes=int(size))

    acts, filters = activations, long_filters
    if width != owned:
        acts, filters = widen(acts), widen(filters)
    table, turn = tables(seq_devices, cols)
    vmem = pl.BlockSpec(memory_space=pltpu.VMEM)
    hbm = pl.BlockSpec(memory_space=pltpu.HBM)
    area = laid * cols
    span = (seq_devices + 1) * width
    taps = short_filters.shape[1]
    place = lax.axis_index(BOTH).astype(jnp.int32).reshape(1)
    inputs = (acts, filters, short_filters, skip_gain)
    outgoing, own = pl.pallas_call(
        functools.partial(send_kernel, width, owned, order),
        out_shape=(
            jax.ShapeDtypeStruct((2 * laid, cols), jnp.bfloat16),
            jax.ShapeDtypeStruct((sections * width, taps + 128), jnp.float32),
        ),
        in_specs=[pl.BlockSpec(memory_space=pltpu.SMEM)] + [hbm] * 4,
        out_specs=(vmem, vmem),
        scratch_shapes=[
            pltpu.VMEM((cols, laid), jnp.bfloat16),
            pltpu.VMEM((cols, laid), jnp.float32),
            pltpu.VMEM(short_filters.shape, jnp.bfloat16),
            pltpu.VMEM(skip_gain.shape, jnp.float32),
            pltpu.SemaphoreType.DMA((2 * laid // 128,)),
            pltpu.SemaphoreType.DMA((2,)),
        ],
        compiler_params=grant(4 * MIB + 24 * area),
    )(place, *(pltpu.with_memory_space_constraint(array, pltpu.HBM) for array in inputs))
    arrived = exchanged(outgoing, 2 * width)
    results = pl.pallas_call(
        functools.partial(main_kernel, width, sections, order),
        out_shape=jax.ShapeDtypeStruct((laid, cols), jnp.bfloat16),
        in_specs=[vmem] * 4,
        out_specs=vmem,
        compiler_params=grant(2 * MIB + 6 * area + 2 * table.size + 64 * span * cols),
    )(arrived, own, turn, table)
    returned = exchanged(results, width)
    final = pl.pallas_call(
        final_kernel,
        out_shape=jax.ShapeDtypeStruct((1, cols, laid), jnp.bfloat16),
        compiler_params=grant(4 * MIB + 16 * area),
    )(returned)
    if width != owned:
        final = final.reshape(1, cols, devices, width)[..., :owned].reshape(1, cols, channels)
    return final


def solution(mesh):
    return jax.shard_map(
        body,
        mesh=mesh,
        in_specs=(P("segment", "seq", None), P(), P("segment", "seq", None), P()),
        out_specs=P("segment", "seq", None),
        check_vma=False,
    )
```

```python
import functools
import math

import jax
import jax.numpy as jnp
import numpy as np
from jax import lax
from jax.experimental import pallas as pl
from jax.experimental.pallas import tpu as pltpu
from jax.sharding import PartitionSpec as P

BOTH = ("segment", "seq")
LANES = 8
MIB = 1024 * 1024


FIELDS = {2: 7, 3: 11, 4: 19, 5: 37, 6: 67, 7: 131, 8: 285, 9: 529, 10: 1033}


def spread_order(devices):
    bits = devices.bit_length() - 1
    if devices != 1 << bits or bits not in FIELDS:
        return tuple(range(devices))
    order, power = [0], 1
    while len(order) < devices:
        order.append(power)
        power <<= 1
        if power & devices:
            power ^= FIELDS[bits]
    return tuple(order)


def tables(real_rows, cols):
    grid_rows = 2 * real_rows + 1
    length = grid_rows * cols
    freqs = real_rows + 1
    k = np.arange(freqs)
    rows = 2.0 * math.pi * ((k[:, None] * np.arange(real_rows)[None, :]) % grid_rows) / grid_rows
    first = np.stack([np.cos(rows), -np.sin(rows)]).reshape(2 * freqs, real_rows)
    row_part = np.kron(first, np.eye(LANES))
    b = np.arange(cols)
    angle = 2.0 * math.pi * (k[:, None] * b[None, :]) / length
    turn = np.concatenate([np.cos(angle), np.sin(angle)], axis=1)
    turn = np.pad(turn, ((0, -freqs % LANES), (0, 0)))
    grid = 2.0 * math.pi * ((b[:, None] * b[None, :]) % cols) / cols
    c, s = np.cos(grid), np.sin(grid)
    parts = [np.block([[c, -s], [s, c]]), row_part]
    lanes = max(part.shape[1] for part in parts)
    stacked = np.concatenate([np.pad(p, ((0, 0), (0, lanes - p.shape[1]))) for p in parts])
    return jnp.asarray(stacked, jnp.bfloat16), jnp.asarray(turn, jnp.float32)


def dot(a, b):
    return jnp.dot(a, b, preferred_element_type=jnp.float32)


def dot_rows(a, b):
    return lax.dot_general(a, b, (((1,), (1,)), ((), ())), preferred_element_type=jnp.float32)


def repeated(rows, count):
    return jnp.concatenate(
        [jnp.broadcast_to(rows[k : k + 1], (LANES, rows.shape[1])) for k in range(count)], axis=0
    )


def identity(size):
    down = lax.broadcasted_iota(jnp.int32, (size, size), 0)
    across = lax.broadcasted_iota(jnp.int32, (size, size), 1)
    return jnp.where(down == across, 1.0, 0.0).astype(jnp.bfloat16)


def send_kernel(
    width,
    owned,
    order,
    place_ref,
    act_ref,
    filt_ref,
    taps_ref,
    gain_ref,
    out_ref,
    own_ref,
    act_held,
    filt_held,
    taps_held,
    gain_held,
    in_sem,
    own_sem,
):
    sections, length, channels = taps_ref.shape
    mine_first = (
        pltpu.make_async_copy(taps_ref, taps_held, own_sem.at[0]),
        pltpu.make_async_copy(gain_ref, gain_held, own_sem.at[1]),
    )
    for copy in mine_first:
        copy.start()
    arriving = (
        pltpu.make_async_copy(act_ref.at[0], act_held, in_sem.at[0]),
        pltpu.make_async_copy(filt_ref.at[0], filt_held, in_sem.at[1]),
    )
    for copy in arriving:
        copy.start()
    eye = identity(128)
    mine = lax.broadcasted_iota(jnp.int32, (width, channels), 0)
    them = lax.broadcasted_iota(jnp.int32, (width, channels), 1)
    place = jnp.int32(0)
    for position, rank in enumerate(order):
        place = place + jnp.where(place_ref[0] == rank, position, 0)
    pick = jnp.where((them == mine + place * owned) & (mine < owned), 1.0, 0.0)
    for copy in mine_first:
        copy.wait()
    for s in range(sections):
        gain = jnp.sum(pick * gain_held[s : s + 1, :], axis=1, keepdims=True)
        own_ref[s * width : (s + 1) * width, :length] = dot_rows(pick.astype(jnp.bfloat16), taps_held[s])
        own_ref[s * width : (s + 1) * width, length:] = jnp.broadcast_to(gain, (width, 128))
    both = []
    for copy, held in zip(arriving, (act_held, filt_held)):
        copy.wait()
        turned = [
            dot_rows(eye, held[:, start : start + 128].astype(jnp.bfloat16))
            for start in range(0, held.shape[1], 128)
        ]
        both.append(jnp.concatenate(turned, axis=0))
    for d in range(len(order)):
        part = slice(d * width, (d + 1) * width)
        piece = jnp.concatenate([array[part] for array in both], axis=0).astype(jnp.bfloat16)
        out_ref[2 * d * width : 2 * (d + 1) * width] = piece


def final_kernel(in_ref, out_ref):
    channels, tokens = in_ref.shape
    step = math.gcd(channels, 256)
    eye = identity(tokens)
    for start in range(0, channels, step):
        part = slice(start, start + step)
        out_ref[0, :, part] = dot_rows(eye, in_ref[part]).astype(jnp.bfloat16)


def main_kernel(width, sections, order, in_ref, own_ref, turn_ref, table_ref, out_ref):
    total, cols = in_ref.shape
    rows = total // (2 * width * sections)
    groups = width // LANES
    high = (rows + 1) * LANES
    span = groups * high
    bf = jnp.bfloat16
    copies = rows + 1
    length = own_ref.shape[1] - 128
    scale = 1.0 / math.sqrt(rows * cols)
    whole = (2 * rows + 1) * cols
    turn = repeated(turn_ref[...], copies)
    cosine, sine = turn[:, :cols], turn[:, cols:]
    all_cos = jnp.concatenate([cosine] * groups, axis=0)
    all_sin = jnp.concatenate([sine] * groups, axis=0)
    forward_cols = table_ref[: 2 * cols, : 2 * cols]
    level, minus = table_ref[:cols, :cols], table_ref[:cols, cols : 2 * cols]
    plus = table_ref[cols : 2 * cols, :cols]
    back_cols = jnp.concatenate(
        [jnp.concatenate([level, plus], axis=1), jnp.concatenate([minus, level], axis=1)], axis=0
    )
    forward_rows = table_ref[2 * cols : 2 * cols + 2 * high, : rows * LANES]
    wide_rows = forward_rows.astype(jnp.float32)
    some_rows = jnp.concatenate([wide_rows[LANES:high], wide_rows[high + LANES :]], axis=0)
    back_rows = dot_rows(identity(rows * LANES), some_rows.astype(bf)).astype(bf)

    def chunk(s):
        starts = [order.index(s * rows + a) * 2 * width for a in range(rows)]
        part = jnp.concatenate([in_ref[at : at + 2 * width] for at in starts], axis=0)
        return part.astype(jnp.float32).reshape(rows, 2 * width, cols)

    def forward(grids):
        turned = []
        for grid in grids:
            for g in range(groups):
                block = grid[:, g * LANES : (g + 1) * LANES].reshape(rows * LANES, cols).astype(bf)
                spread = dot(forward_rows, block)
                real, imag = spread[:high], spread[high:]
                turned.append(
                    jnp.concatenate(
                        [real * cosine + imag * sine, imag * cosine - real * sine], axis=1
                    )
                )
        return dot(jnp.concatenate(turned, axis=0).astype(bf), forward_cols)

    def times(left, right):
        lr, li = left[:, :cols], left[:, cols:]
        rr, ri = right
        return jnp.concatenate([lr * rr - li * ri, lr * ri + li * rr], axis=1).astype(bf)

    def back(product):
        flat = dot(product, back_cols)
        real, imag = flat[:, :cols], flat[:, cols:]
        turned_real = real * all_cos - imag * all_sin
        turned_imag = real * all_sin + imag * all_cos
        pieces = []
        for g in range(groups):
            start = g * high
            part = slice(start + LANES, start + high)
            both = jnp.concatenate([turned_real[part], turned_imag[part]], axis=0).astype(bf)
            piece = dot(back_rows, both).reshape(rows, LANES, cols)
            pieces.append(piece + turned_real[start : start + LANES][None])
        return jnp.concatenate(pieces, axis=1)

    def short_specs():
        turned = []
        for s in range(sections):
            for g in range(groups):
                start = s * width + g * LANES
                taps = jnp.concatenate([own_ref[start : start + LANES, :length]] * copies, axis=0)
                turned.append(
                    jnp.concatenate([taps * short_cos, taps * short_sin], axis=1)
                )
        columns = jnp.concatenate([table_ref[:length, : 2 * cols], table_ref[cols : cols + length, : 2 * cols]])
        return dot(jnp.concatenate(turned, axis=0).astype(bf), columns)

    row = lax.broadcasted_iota(jnp.int32, (high, 1), 0)
    weight = jnp.where(row < LANES, scale / whole, 2.0 * scale / whole)
    short_cos, short_sin = cosine[:, :length] * weight, -(sine[:, :length] * weight)
    shorts = short_specs()

    def combine(s, spec):
        gains = own_ref[s * width : (s + 1) * width, length:] * (1.0 / scale)
        gains = jnp.concatenate([gains] * (cols // 128), axis=1)
        shift = jnp.concatenate(
            [gains[g * LANES : (g + 1) * LANES] for g in range(groups) for _ in range(copies)], axis=0
        )
        short = shorts[s * span : (s + 1) * span]
        lr, li = spec[:, :cols] + shift, spec[:, cols:]
        rr, ri = short[:, :cols], short[:, cols:]
        return lr * rr - li * ri, lr * ri + li * rr

    chunks = [chunk(s) for s in range(sections)]
    specs = forward([chunks[0][:, :width]] + [part[:, width:] for part in chunks])
    signal_spec = specs[:span]
    results = []
    for s in range(sections):
        mixed = combine(s, specs[(s + 1) * span : (s + 2) * span])
        result = back(times(signal_spec, mixed))
        results.append(result)
        if s + 1 < sections:
            rounded = result.astype(bf).astype(jnp.float32)
            signal_spec = forward([rounded * chunks[s + 1][:, :width]])
    for at in range(0, len(order), 2):
        pair = [results[rank // rows][rank % rows] for rank in order[at : at + 2]]
        out_ref[at * width : (at + 2) * width] = jnp.concatenate(pair, axis=0).astype(bf)


def body(activations, short_filters, long_filters, skip_gain):
    sections = short_filters.shape[0]
    tokens, channels = activations.shape[1:]
    devices = lax.axis_size(BOTH)
    seq_devices = lax.axis_size("seq")
    owned = channels // devices
    width = -(-owned // LANES) * LANES
    cols = tokens
    laid = devices * width
    order = spread_order(devices)

    def widen(array):
        split = array.reshape(array.shape[:2] + (devices, owned))
        split = jnp.pad(split, ((0, 0), (0, 0), (0, 0), (0, width - owned)))
        return split.reshape(array.shape[:2] + (laid,))

    def exchanged(array, height):
        chunks = array.reshape(devices, height, cols)
        moved = lax.all_to_all(
            chunks, BOTH, split_axis=0, concat_axis=0, tiled=True, axis_index_groups=[list(order)]
        )
        return moved.reshape(devices * height, cols)

    def grant(size):
        return pltpu.CompilerParams(vmem_limit_bytes=int(size))

    acts, filters = activations, long_filters
    if width != owned:
        acts, filters = widen(acts), widen(filters)
    table, turn = tables(seq_devices, cols)
    vmem = pl.BlockSpec(memory_space=pltpu.VMEM)
    hbm = pl.BlockSpec(memory_space=pltpu.HBM)
    area = laid * cols
    span = (seq_devices + 1) * width
    taps = short_filters.shape[1]
    place = lax.axis_index(BOTH).astype(jnp.int32).reshape(1)
    inputs = (acts, filters, short_filters, skip_gain)
    outgoing, own = pl.pallas_call(
        functools.partial(send_kernel, width, owned, order),
        out_shape=(
            jax.ShapeDtypeStruct((2 * laid, cols), jnp.bfloat16),
            jax.ShapeDtypeStruct((sections * width, taps + 128), jnp.float32),
        ),
        in_specs=[pl.BlockSpec(memory_space=pltpu.SMEM)] + [hbm] * 4,
        out_specs=(vmem, vmem),
        scratch_shapes=[
            pltpu.VMEM((cols, laid), jnp.bfloat16),
            pltpu.VMEM((cols, laid), jnp.float32),
            pltpu.VMEM(short_filters.shape, jnp.bfloat16),
            pltpu.VMEM(skip_gain.shape, jnp.float32),
            pltpu.SemaphoreType.DMA((2,)),
            pltpu.SemaphoreType.DMA((2,)),
        ],
        compiler_params=grant(4 * MIB + 24 * area),
    )(place, *(pltpu.with_memory_space_constraint(array, pltpu.HBM) for array in inputs))
    arrived = exchanged(outgoing, 2 * width)
    results = pl.pallas_call(
        functools.partial(main_kernel, width, sections, order),
        out_shape=jax.ShapeDtypeStruct((laid, cols), jnp.bfloat16),
        in_specs=[vmem] * 4,
        out_specs=vmem,
        compiler_params=grant(2 * MIB + 6 * area + 2 * table.size + 64 * span * cols),
    )(arrived, own, turn, table)
    returned = exchanged(results, width)
    final = pl.pallas_call(
        final_kernel,
        out_shape=jax.ShapeDtypeStruct((1, cols, laid), jnp.bfloat16),
        compiler_params=grant(4 * MIB + 16 * area),
    )(returned)
    if width != owned:
        final = final.reshape(1, cols, devices, width)[..., :owned].reshape(1, cols, channels)
    return final


def solution(mesh):
    return jax.shard_map(
        body,
        mesh=mesh,
        in_specs=(P("segment", "seq", None), P(), P("segment", "seq", None), P()),
        out_specs=P("segment", "seq", None),
        check_vma=False,
    )
```

```python
import functools
import math

import jax
import jax.numpy as jnp
import numpy as np
from jax import lax
from jax.experimental import pallas as pl
from jax.experimental.pallas import tpu as pltpu
from jax.sharding import PartitionSpec as P

BOTH = ("segment", "seq")
LANES = 8
MIB = 1024 * 1024


FIELDS = {2: 7, 3: 11, 4: 19, 5: 37, 6: 67, 7: 131, 8: 285, 9: 529, 10: 1033}


def spread_order(devices):
    bits = devices.bit_length() - 1
    if devices != 1 << bits or bits not in FIELDS:
        return tuple(range(devices))
    order, power = [0], 1
    while len(order) < devices:
        order.append(power)
        power <<= 1
        if power & devices:
            power ^= FIELDS[bits]
    return tuple(order)


def tables(real_rows, cols):
    grid_rows = 2 * real_rows + 1
    length = grid_rows * cols
    freqs = real_rows + 1
    k = np.arange(freqs)
    rows = 2.0 * math.pi * ((k[:, None] * np.arange(real_rows)[None, :]) % grid_rows) / grid_rows
    first = np.stack([np.cos(rows), -np.sin(rows)]).reshape(2 * freqs, real_rows)
    row_part = np.kron(first, np.eye(LANES))
    b = np.arange(cols)
    angle = 2.0 * math.pi * (k[:, None] * b[None, :]) / length
    turn = np.concatenate([np.cos(angle), np.sin(angle)], axis=1)
    turn = np.pad(turn, ((0, -freqs % LANES), (0, 0)))
    grid = 2.0 * math.pi * ((b[:, None] * b[None, :]) % cols) / cols
    c, s = np.cos(grid), np.sin(grid)
    parts = [np.block([[c, -s], [s, c]]), row_part]
    lanes = max(part.shape[1] for part in parts)
    stacked = np.concatenate([np.pad(p, ((0, 0), (0, lanes - p.shape[1]))) for p in parts])
    return jnp.asarray(stacked, jnp.bfloat16), jnp.asarray(turn, jnp.float32)


def dot(a, b):
    return jnp.dot(a, b, preferred_element_type=jnp.float32)


def dot_rows(a, b):
    return lax.dot_general(a, b, (((1,), (1,)), ((), ())), preferred_element_type=jnp.float32)


def repeated(rows, count):
    return jnp.concatenate(
        [jnp.broadcast_to(rows[k : k + 1], (LANES, rows.shape[1])) for k in range(count)], axis=0
    )


def identity(size):
    down = lax.broadcasted_iota(jnp.int32, (size, size), 0)
    across = lax.broadcasted_iota(jnp.int32, (size, size), 1)
    return jnp.where(down == across, 1.0, 0.0).astype(jnp.bfloat16)


def send_kernel(
    width,
    owned,
    order,
    place_ref,
    act_ref,
    filt_ref,
    taps_ref,
    gain_ref,
    out_ref,
    own_ref,
    act_held,
    filt_held,
    taps_held,
    gain_held,
    in_sem,
    own_sem,
):
    sections, length, channels = taps_ref.shape
    mine_first = (
        pltpu.make_async_copy(taps_ref, taps_held, own_sem.at[0]),
        pltpu.make_async_copy(gain_ref, gain_held, own_sem.at[1]),
    )
    for copy in mine_first:
        copy.start()
    arriving = (
        pltpu.make_async_copy(act_ref.at[0], act_held, in_sem.at[0]),
        pltpu.make_async_copy(filt_ref.at[0], filt_held, in_sem.at[1]),
    )
    for copy in arriving:
        copy.start()
    eye = identity(128)
    mine = lax.broadcasted_iota(jnp.int32, (width, channels), 0)
    them = lax.broadcasted_iota(jnp.int32, (width, channels), 1)
    place = jnp.int32(0)
    for position, rank in enumerate(order):
        place = place + jnp.where(place_ref[0] == rank, position, 0)
    pick = jnp.where((them == mine + place * owned) & (mine < owned), 1.0, 0.0)
    for copy in mine_first:
        copy.wait()
    for s in range(sections):
        gain = jnp.sum(pick * gain_held[s : s + 1, :], axis=1, keepdims=True)
        own_ref[s * width : (s + 1) * width, :length] = dot_rows(pick.astype(jnp.bfloat16), taps_held[s])
        own_ref[s * width : (s + 1) * width, length:] = jnp.broadcast_to(gain, (width, 128))
    both = []
    for copy, held in zip(arriving, (act_held, filt_held)):
        copy.wait()
        turned = [
            dot_rows(eye, held[:, start : start + 128].astype(jnp.bfloat16))
            for start in range(0, held.shape[1], 128)
        ]
        both.append(jnp.concatenate(turned, axis=0))
    for d in range(len(order)):
        part = slice(d * width, (d + 1) * width)
        piece = jnp.concatenate([array[part] for array in both], axis=0).astype(jnp.bfloat16)
        out_ref[2 * d * width : 2 * (d + 1) * width] = piece


def final_kernel(in_ref, out_ref):
    channels, tokens = in_ref.shape
    step = math.gcd(channels, 256)
    eye = identity(tokens)
    for start in range(0, channels, step):
        part = slice(start, start + step)
        out_ref[0, :, part] = dot_rows(eye, in_ref[part]).astype(jnp.bfloat16)


def main_kernel(width, sections, order, in_ref, own_ref, turn_ref, table_ref, out_ref):
    total, cols = in_ref.shape
    rows = total // (2 * width * sections)
    groups = width // LANES
    high = (rows + 1) * LANES
    bf = jnp.bfloat16
    copies = rows + 1
    length = own_ref.shape[1] - 128
    scale = 1.0 / math.sqrt(rows * cols)
    whole = (2 * rows + 1) * cols
    turn = repeated(turn_ref[...], copies)
    cosine, sine = turn[:, :cols], turn[:, cols:]
    forward_cols = table_ref[: 2 * cols, : 2 * cols]
    level, minus = table_ref[:cols, :cols], table_ref[:cols, cols : 2 * cols]
    plus = table_ref[cols : 2 * cols, :cols]
    back_cols = jnp.concatenate(
        [jnp.concatenate([level, plus], axis=1), jnp.concatenate([minus, level], axis=1)], axis=0
    )
    forward_rows = table_ref[2 * cols : 2 * cols + 2 * high, : rows * LANES]
    wide_rows = forward_rows.astype(jnp.float32)
    some_rows = jnp.concatenate([wide_rows[LANES:high], wide_rows[high + LANES :]], axis=0)
    back_rows = dot_rows(identity(rows * LANES), some_rows.astype(bf)).astype(bf)

    def chunk(s):
        starts = [order.index(s * rows + a) * 2 * width for a in range(rows)]
        part = jnp.concatenate([in_ref[at : at + 2 * width] for at in starts], axis=0)
        return part.astype(jnp.float32).reshape(rows, 2 * width, cols)

    def first_half(block):
        spread = dot(forward_rows, block.reshape(rows * LANES, cols).astype(bf))
        real, imag = spread[:high], spread[high:]
        return jnp.concatenate([real * cosine + imag * sine, imag * cosine - real * sine], axis=1)

    def forward(blocks):
        turned = jnp.concatenate([first_half(block) for block in blocks], axis=0)
        return dot(turned.astype(bf), forward_cols)

    def times(left, right):
        lr, li = left[:, :cols], left[:, cols:]
        rr, ri = right
        return jnp.concatenate([lr * rr - li * ri, lr * ri + li * rr], axis=1).astype(bf)

    def back(flat):
        real, imag = flat[:, :cols], flat[:, cols:]
        turned_real = real * cosine - imag * sine
        turned_imag = real * sine + imag * cosine
        both = jnp.concatenate([turned_real[LANES:], turned_imag[LANES:]], axis=0).astype(bf)
        return dot(back_rows, both).reshape(rows, LANES, cols) + turned_real[:LANES][None]

    row = lax.broadcasted_iota(jnp.int32, (high, 1), 0)
    weight = jnp.where(row < LANES, scale / whole, 2.0 * scale / whole)
    short_cos, short_sin = cosine[:, :length] * weight, -(sine[:, :length] * weight)
    short_cols = jnp.concatenate(
        [table_ref[:length, : 2 * cols], table_ref[cols : cols + length, : 2 * cols]]
    )

    def short_half(s, g):
        start = s * width + g * LANES
        taps = jnp.concatenate([own_ref[start : start + LANES, :length]] * copies, axis=0)
        return jnp.concatenate([taps * short_cos, taps * short_sin], axis=1)

    def combine(s, g, short, spec):
        start = s * width + g * LANES
        gains = own_ref[start : start + LANES, length:] * (1.0 / scale)
        gains = jnp.concatenate([gains] * (cols // 128), axis=1)
        lr, li = spec[:, :cols] + jnp.concatenate([gains] * copies, axis=0), spec[:, cols:]
        rr, ri = short[:, :cols], short[:, cols:]
        return lr * rr - li * ri, lr * ri + li * rr

    chunks = [chunk(s) for s in range(sections)]
    over = range(groups)
    own = [slice(g * LANES, (g + 1) * LANES) for g in over]
    long = [slice(width + g * LANES, width + (g + 1) * LANES) for g in over]
    shorts = [
        dot(jnp.concatenate([short_half(s, g) for s in range(sections)], axis=0).astype(bf), short_cols)
        for g in over
    ]
    specs = [forward([chunks[0][:, own[g]]] + [part[:, long[g]] for part in chunks]) for g in over]
    signals = [specs[g][:high] for g in over]
    results = []
    for s in range(sections):
        part, after = slice(s * high, (s + 1) * high), slice((s + 1) * high, (s + 2) * high)
        products = [
            times(signals[g], combine(s, g, shorts[g][part], specs[g][after])) for g in over
        ]
        flats = [dot(product, back_cols) for product in products]
        result = [back(flat) for flat in flats]
        results.append(jnp.concatenate(result, axis=1))
        if s + 1 < sections:
            signals = [
                forward([result[g].astype(bf).astype(jnp.float32) * chunks[s + 1][:, own[g]]]) for g in over
            ]
    for at in range(0, len(order), 2):
        pair = [results[rank // rows][rank % rows] for rank in order[at : at + 2]]
        out_ref[at * width : (at + 2) * width] = jnp.concatenate(pair, axis=0).astype(bf)


def body(activations, short_filters, long_filters, skip_gain):
    sections = short_filters.shape[0]
    tokens, channels = activations.shape[1:]
    devices = lax.axis_size(BOTH)
    seq_devices = lax.axis_size("seq")
    owned = channels // devices
    width = -(-owned // LANES) * LANES
    cols = tokens
    laid = devices * width
    order = spread_order(devices)

    def widen(array):
        split = array.reshape(array.shape[:2] + (devices, owned))
        split = jnp.pad(split, ((0, 0), (0, 0), (0, 0), (0, width - owned)))
        return split.reshape(array.shape[:2] + (laid,))

    def exchanged(array, height):
        chunks = array.reshape(devices, height, cols)
        moved = lax.all_to_all(
            chunks, BOTH, split_axis=0, concat_axis=0, tiled=True, axis_index_groups=[list(order)]
        )
        return moved.reshape(devices * height, cols)

    def grant(size):
        return pltpu.CompilerParams(vmem_limit_bytes=int(size))

    acts, filters = activations, long_filters
    if width != owned:
        acts, filters = widen(acts), widen(filters)
    table, turn = tables(seq_devices, cols)
    vmem = pl.BlockSpec(memory_space=pltpu.VMEM)
    hbm = pl.BlockSpec(memory_space=pltpu.HBM)
    area = laid * cols
    span = (seq_devices + 1) * width
    taps = short_filters.shape[1]
    place = lax.axis_index(BOTH).astype(jnp.int32).reshape(1)
    inputs = (acts, filters, short_filters, skip_gain)
    outgoing, own = pl.pallas_call(
        functools.partial(send_kernel, width, owned, order),
        out_shape=(
            jax.ShapeDtypeStruct((2 * laid, cols), jnp.bfloat16),
            jax.ShapeDtypeStruct((sections * width, taps + 128), jnp.float32),
        ),
        in_specs=[pl.BlockSpec(memory_space=pltpu.SMEM)] + [hbm] * 4,
        out_specs=(vmem, vmem),
        scratch_shapes=[
            pltpu.VMEM((cols, laid), jnp.bfloat16),
            pltpu.VMEM((cols, laid), jnp.float32),
            pltpu.VMEM(short_filters.shape, jnp.bfloat16),
            pltpu.VMEM(skip_gain.shape, jnp.float32),
            pltpu.SemaphoreType.DMA((2,)),
            pltpu.SemaphoreType.DMA((2,)),
        ],
        compiler_params=grant(4 * MIB + 24 * area),
    )(place, *(pltpu.with_memory_space_constraint(array, pltpu.HBM) for array in inputs))
    arrived = exchanged(outgoing, 2 * width)
    results = pl.pallas_call(
        functools.partial(main_kernel, width, sections, order),
        out_shape=jax.ShapeDtypeStruct((laid, cols), jnp.bfloat16),
        in_specs=[vmem] * 4,
        out_specs=vmem,
        compiler_params=grant(2 * MIB + 6 * area + 2 * table.size + 64 * span * cols),
    )(arrived, own, turn, table)
    returned = exchanged(results, width)
    final = pl.pallas_call(
        final_kernel,
        out_shape=jax.ShapeDtypeStruct((1, cols, laid), jnp.bfloat16),
        compiler_params=grant(4 * MIB + 16 * area),
    )(returned)
    if width != owned:
        final = final.reshape(1, cols, devices, width)[..., :owned].reshape(1, cols, channels)
    return final


def solution(mesh):
    return jax.shard_map(
        body,
        mesh=mesh,
        in_specs=(P("segment", "seq", None), P(), P("segment", "seq", None), P()),
        out_specs=P("segment", "seq", None),
        check_vma=False,
    )
```

```python
import functools
import math

import jax
import jax.numpy as jnp
import numpy as np
from jax import lax
from jax.experimental import pallas as pl
from jax.experimental.pallas import tpu as pltpu
from jax.sharding import PartitionSpec as P

BOTH = ("segment", "seq")
LANES = 8
MIB = 1024 * 1024


def spread_order(devices, seq_devices):
    half = seq_devices // 2
    along = [place // 2 + place % 2 * half for place in range(2 * half)]
    along += range(2 * half, seq_devices)
    return tuple(
        start + q for start in range(0, devices, seq_devices) for q in along
    )


def tables(real_rows, cols):
    grid_rows = 2 * real_rows + 1
    length = grid_rows * cols
    freqs = real_rows + 1
    k = np.arange(freqs)
    rows = 2.0 * math.pi * ((k[:, None] * np.arange(real_rows)[None, :]) % grid_rows) / grid_rows
    first = np.stack([np.cos(rows), -np.sin(rows)]).reshape(2 * freqs, real_rows)
    row_part = np.kron(first, np.eye(LANES))
    b = np.arange(cols)
    angle = 2.0 * math.pi * (k[:, None] * b[None, :]) / length
    turn = np.concatenate([np.cos(angle), np.sin(angle)], axis=1)
    turn = np.pad(turn, ((0, -freqs % LANES), (0, 0)))
    grid = 2.0 * math.pi * ((b[:, None] * b[None, :]) % cols) / cols
    c, s = np.cos(grid), np.sin(grid)
    parts = [np.block([[c, -s], [s, c]]), row_part]
    lanes = max(part.shape[1] for part in parts)
    stacked = np.concatenate([np.pad(p, ((0, 0), (0, lanes - p.shape[1]))) for p in parts])
    return jnp.asarray(stacked, jnp.bfloat16), jnp.asarray(turn, jnp.float32)


def dot(a, b):
    return jnp.dot(a, b, preferred_element_type=jnp.float32)


def dot_rows(a, b):
    return lax.dot_general(a, b, (((1,), (1,)), ((), ())), preferred_element_type=jnp.float32)


def repeated(rows, count):
    return jnp.concatenate(
        [jnp.broadcast_to(rows[k : k + 1], (LANES, rows.shape[1])) for k in range(count)], axis=0
    )


def identity(size):
    down = lax.broadcasted_iota(jnp.int32, (size, size), 0)
    across = lax.broadcasted_iota(jnp.int32, (size, size), 1)
    return jnp.where(down == across, 1.0, 0.0).astype(jnp.bfloat16)


def send_kernel(
    width,
    owned,
    order,
    place_ref,
    act_ref,
    filt_ref,
    taps_ref,
    gain_ref,
    out_ref,
    own_ref,
    act_held,
    filt_held,
    taps_held,
    gain_held,
    in_sem,
    own_sem,
):
    sections, length, channels = taps_ref.shape
    mine_first = (
        pltpu.make_async_copy(taps_ref, taps_held, own_sem.at[0]),
        pltpu.make_async_copy(gain_ref, gain_held, own_sem.at[1]),
    )
    for copy in mine_first:
        copy.start()
    arriving = (
        pltpu.make_async_copy(act_ref.at[0], act_held, in_sem.at[0]),
        pltpu.make_async_copy(filt_ref.at[0], filt_held, in_sem.at[1]),
    )
    for copy in arriving:
        copy.start()
    eye = identity(128)
    mine = lax.broadcasted_iota(jnp.int32, (width, channels), 0)
    them = lax.broadcasted_iota(jnp.int32, (width, channels), 1)
    place = jnp.int32(0)
    for position, rank in enumerate(order):
        place = place + jnp.where(place_ref[0] == rank, position, 0)
    pick = jnp.where((them == mine + place * owned) & (mine < owned), 1.0, 0.0)
    for copy in mine_first:
        copy.wait()
    for s in range(sections):
        gain = jnp.sum(pick * gain_held[s : s + 1, :], axis=1, keepdims=True)
        own_ref[s * width : (s + 1) * width, :length] = dot_rows(pick.astype(jnp.bfloat16), taps_held[s])
        own_ref[s * width : (s + 1) * width, length:] = jnp.broadcast_to(gain, (width, 128))
    both = []
    for copy, held in zip(arriving, (act_held, filt_held)):
        copy.wait()
        turned = [
            dot_rows(eye, held[:, start : start + 128].astype(jnp.bfloat16))
            for start in range(0, held.shape[1], 128)
        ]
        both.append(jnp.concatenate(turned, axis=0))
    for d in range(len(order)):
        part = slice(d * width, (d + 1) * width)
        piece = jnp.concatenate([array[part] for array in both], axis=0).astype(jnp.bfloat16)
        out_ref[2 * d * width : 2 * (d + 1) * width] = piece


def final_kernel(in_ref, out_ref):
    channels, tokens = in_ref.shape
    step = math.gcd(channels, 256)
    eye = identity(tokens)
    for start in range(0, channels, step):
        part = slice(start, start + step)
        out_ref[0, :, part] = dot_rows(eye, in_ref[part]).astype(jnp.bfloat16)


def main_kernel(width, sections, order, in_ref, own_ref, turn_ref, table_ref, out_ref):
    total, cols = in_ref.shape
    rows = total // (2 * width * sections)
    groups = width // LANES
    high = (rows + 1) * LANES
    span = groups * high
    bf = jnp.bfloat16
    copies = rows + 1
    length = own_ref.shape[1] - 128
    scale = 1.0 / math.sqrt(rows * cols)
    whole = (2 * rows + 1) * cols
    turn = repeated(turn_ref[...], copies)
    cosine, sine = turn[:, :cols], turn[:, cols:]
    all_cos = jnp.concatenate([cosine] * groups, axis=0)
    all_sin = jnp.concatenate([sine] * groups, axis=0)
    forward_cols = table_ref[: 2 * cols, : 2 * cols]
    level, minus = table_ref[:cols, :cols], table_ref[:cols, cols : 2 * cols]
    plus = table_ref[cols : 2 * cols, :cols]
    back_cols = jnp.concatenate(
        [jnp.concatenate([level, plus], axis=1), jnp.concatenate([minus, level], axis=1)], axis=0
    )
    forward_rows = table_ref[2 * cols : 2 * cols + 2 * high, : rows * LANES]
    wide_rows = forward_rows.astype(jnp.float32)
    some_rows = jnp.concatenate([wide_rows[LANES:high], wide_rows[high + LANES :]], axis=0)
    back_rows = dot_rows(identity(rows * LANES), some_rows.astype(bf)).astype(bf)

    def chunk(s):
        starts = [order.index(s * rows + a) * 2 * width for a in range(rows)]
        part = jnp.concatenate([in_ref[at : at + 2 * width] for at in starts], axis=0)
        return part.astype(jnp.float32).reshape(rows, 2 * width, cols)

    def forward(grids):
        turned = []
        for grid in grids:
            for g in range(groups):
                block = grid[:, g * LANES : (g + 1) * LANES].reshape(rows * LANES, cols).astype(bf)
                spread = dot(forward_rows, block)
                real, imag = spread[:high], spread[high:]
                turned.append(
                    jnp.concatenate(
                        [real * cosine + imag * sine, imag * cosine - real * sine], axis=1
                    )
                )
        return dot(jnp.concatenate(turned, axis=0).astype(bf), forward_cols)

    def times(left, right):
        lr, li = left[:, :cols], left[:, cols:]
        rr, ri = right
        return jnp.concatenate([lr * rr - li * ri, lr * ri + li * rr], axis=1).astype(bf)

    def back(product):
        flat = dot(product, back_cols)
        real, imag = flat[:, :cols], flat[:, cols:]
        turned_real = real * all_cos - imag * all_sin
        turned_imag = real * all_sin + imag * all_cos
        pieces = []
        for g in range(groups):
            start = g * high
            part = slice(start + LANES, start + high)
            both = jnp.concatenate([turned_real[part], turned_imag[part]], axis=0).astype(bf)
            piece = dot(back_rows, both).reshape(rows, LANES, cols)
            pieces.append(piece + turned_real[start : start + LANES][None])
        return jnp.concatenate(pieces, axis=1)

    def short_specs():
        turned = []
        for s in range(sections):
            for g in range(groups):
                start = s * width + g * LANES
                taps = jnp.concatenate([own_ref[start : start + LANES, :length]] * copies, axis=0)
                turned.append(
                    jnp.concatenate([taps * short_cos, taps * short_sin], axis=1)
                )
        columns = jnp.concatenate([table_ref[:length, : 2 * cols], table_ref[cols : cols + length, : 2 * cols]])
        return dot(jnp.concatenate(turned, axis=0).astype(bf), columns)

    row = lax.broadcasted_iota(jnp.int32, (high, 1), 0)
    weight = jnp.where(row < LANES, scale / whole, 2.0 * scale / whole)
    short_cos, short_sin = cosine[:, :length] * weight, -(sine[:, :length] * weight)
    shorts = short_specs()

    def combine(s, spec):
        gains = own_ref[s * width : (s + 1) * width, length:] * (1.0 / scale)
        gains = jnp.concatenate([gains] * (cols // 128), axis=1)
        shift = jnp.concatenate(
            [gains[g * LANES : (g + 1) * LANES] for g in range(groups) for _ in range(copies)], axis=0
        )
        short = shorts[s * span : (s + 1) * span]
        lr, li = spec[:, :cols] + shift, spec[:, cols:]
        rr, ri = short[:, :cols], short[:, cols:]
        return lr * rr - li * ri, lr * ri + li * rr

    chunks = [chunk(s) for s in range(sections)]
    specs = forward([chunks[0][:, :width]] + [part[:, width:] for part in chunks])
    signal_spec = specs[:span]
    results = []
    for s in range(sections):
        mixed = combine(s, specs[(s + 1) * span : (s + 2) * span])
        result = back(times(signal_spec, mixed))
        results.append(result)
        if s + 1 < sections:
            rounded = result.astype(bf).astype(jnp.float32)
            signal_spec = forward([rounded * chunks[s + 1][:, :width]])
    for at in range(0, len(order), 2):
        pair = [results[rank // rows][rank % rows] for rank in order[at : at + 2]]
        out_ref[at * width : (at + 2) * width] = jnp.concatenate(pair, axis=0).astype(bf)


def body(activations, short_filters, long_filters, skip_gain):
    sections = short_filters.shape[0]
    tokens, channels = activations.shape[1:]
    devices = lax.axis_size(BOTH)
    seq_devices = lax.axis_size("seq")
    owned = channels // devices
    width = -(-owned // LANES) * LANES
    cols = tokens
    laid = devices * width
    order = spread_order(devices, seq_devices)

    def widen(array):
        split = array.reshape(array.shape[:2] + (devices, owned))
        split = jnp.pad(split, ((0, 0), (0, 0), (0, 0), (0, width - owned)))
        return split.reshape(array.shape[:2] + (laid,))

    def exchanged(array, height):
        chunks = array.reshape(devices, height, cols)
        moved = lax.all_to_all(
            chunks, BOTH, split_axis=0, concat_axis=0, tiled=True, axis_index_groups=[list(order)]
        )
        return moved.reshape(devices * height, cols)

    def grant(size):
        return pltpu.CompilerParams(vmem_limit_bytes=int(size))

    acts, filters = activations, long_filters
    if width != owned:
        acts, filters = widen(acts), widen(filters)
    table, turn = tables(seq_devices, cols)
    vmem = pl.BlockSpec(memory_space=pltpu.VMEM)
    hbm = pl.BlockSpec(memory_space=pltpu.HBM)
    area = laid * cols
    span = (seq_devices + 1) * width
    taps = short_filters.shape[1]
    place = lax.axis_index(BOTH).astype(jnp.int32).reshape(1)
    inputs = (acts, filters, short_filters, skip_gain)
    outgoing, own = pl.pallas_call(
        functools.partial(send_kernel, width, owned, order),
        out_shape=(
            jax.ShapeDtypeStruct((2 * laid, cols), jnp.bfloat16),
            jax.ShapeDtypeStruct((sections * width, taps + 128), jnp.float32),
        ),
        in_specs=[pl.BlockSpec(memory_space=pltpu.SMEM)] + [hbm] * 4,
        out_specs=(vmem, vmem),
        scratch_shapes=[
            pltpu.VMEM((cols, laid), jnp.bfloat16),
            pltpu.VMEM((cols, laid), jnp.float32),
            pltpu.VMEM(short_filters.shape, jnp.bfloat16),
            pltpu.VMEM(skip_gain.shape, jnp.float32),
            pltpu.SemaphoreType.DMA((2,)),
            pltpu.SemaphoreType.DMA((2,)),
        ],
        compiler_params=grant(4 * MIB + 24 * area),
    )(place, *(pltpu.with_memory_space_constraint(array, pltpu.HBM) for array in inputs))
    arrived = exchanged(outgoing, 2 * width)
    results = pl.pallas_call(
        functools.partial(main_kernel, width, sections, order),
        out_shape=jax.ShapeDtypeStruct((laid, cols), jnp.bfloat16),
        in_specs=[vmem] * 4,
        out_specs=vmem,
        compiler_params=grant(2 * MIB + 6 * area + 2 * table.size + 64 * span * cols),
    )(arrived, own, turn, table)
    returned = exchanged(results, width)
    final = pl.pallas_call(
        final_kernel,
        out_shape=jax.ShapeDtypeStruct((1, cols, laid), jnp.bfloat16),
        compiler_params=grant(4 * MIB + 16 * area),
    )(returned)
    if width != owned:
        final = final.reshape(1, cols, devices, width)[..., :owned].reshape(1, cols, channels)
    return final


def solution(mesh):
    return jax.shard_map(
        body,
        mesh=mesh,
        in_specs=(P("segment", "seq", None), P(), P("segment", "seq", None), P()),
        out_specs=P("segment", "seq", None),
        check_vma=False,
    )
```

```python
import functools
import math

import jax
import jax.numpy as jnp
import numpy as np
from jax import lax
from jax.experimental import pallas as pl
from jax.experimental.pallas import tpu as pltpu
from jax.sharding import PartitionSpec as P

BOTH = ("segment", "seq")
LANES = 8
MIB = 1024 * 1024


def spread_order(devices, seq_devices):
    half = seq_devices // 2
    along = [place // 2 + place % 2 * half for place in range(2 * half)]
    along += range(2 * half, seq_devices)
    return tuple(
        start + q for start in range(0, devices, seq_devices) for q in along
    )


def tables(real_rows, cols, split):
    grid_rows = 2 * real_rows + 1
    length = grid_rows * cols
    freqs = real_rows + 1
    k = np.arange(freqs)
    place = np.arange(real_rows).reshape(-1, split).T.reshape(-1)
    rows = 2.0 * math.pi * ((k[:, None] * place[None, :]) % grid_rows) / grid_rows
    first = np.stack([np.cos(rows), -np.sin(rows)]).reshape(2 * freqs, real_rows)
    row_part = np.kron(first, np.eye(LANES))
    b = np.arange(cols)
    angle = 2.0 * math.pi * (k[:, None] * b[None, :]) / length
    turn = np.concatenate([np.cos(angle), np.sin(angle)], axis=1)
    turn = np.pad(turn, ((0, -freqs % LANES), (0, 0)))
    grid = 2.0 * math.pi * ((b[:, None] * b[None, :]) % cols) / cols
    c, s = np.cos(grid), np.sin(grid)
    parts = [np.block([[c, -s], [s, c]]), row_part]
    lanes = max(part.shape[1] for part in parts)
    stacked = np.concatenate([np.pad(p, ((0, 0), (0, lanes - p.shape[1]))) for p in parts])
    return jnp.asarray(stacked, jnp.bfloat16), jnp.asarray(turn, jnp.float32)


def dot(a, b):
    return jnp.dot(a, b, preferred_element_type=jnp.float32)


def dot_rows(a, b):
    return lax.dot_general(a, b, (((1,), (1,)), ((), ())), preferred_element_type=jnp.float32)


def repeated(rows, count):
    return jnp.concatenate(
        [jnp.broadcast_to(rows[k : k + 1], (LANES, rows.shape[1])) for k in range(count)], axis=0
    )


def identity(size):
    down = lax.broadcasted_iota(jnp.int32, (size, size), 0)
    across = lax.broadcasted_iota(jnp.int32, (size, size), 1)
    return jnp.where(down == across, 1.0, 0.0).astype(jnp.bfloat16)


def send_kernel(
    width,
    owned,
    order,
    place_ref,
    act_ref,
    filt_ref,
    taps_ref,
    gain_ref,
    out_ref,
    own_ref,
    act_held,
    filt_held,
    taps_held,
    gain_held,
    in_sem,
    own_sem,
):
    sections, length, channels = taps_ref.shape
    mine_first = (
        pltpu.make_async_copy(taps_ref, taps_held, own_sem.at[0]),
        pltpu.make_async_copy(gain_ref, gain_held, own_sem.at[1]),
    )
    for copy in mine_first:
        copy.start()
    arriving = (
        pltpu.make_async_copy(act_ref.at[0], act_held, in_sem.at[0]),
        pltpu.make_async_copy(filt_ref.at[0], filt_held, in_sem.at[1]),
    )
    for copy in arriving:
        copy.start()
    eye = identity(128)
    mine = lax.broadcasted_iota(jnp.int32, (width, channels), 0)
    them = lax.broadcasted_iota(jnp.int32, (width, channels), 1)
    place = jnp.int32(0)
    for position, rank in enumerate(order):
        place = place + jnp.where(place_ref[0] == rank, position, 0)
    pick = jnp.where((them == mine + place * owned) & (mine < owned), 1.0, 0.0)
    for copy in mine_first:
        copy.wait()
    for s in range(sections):
        gain = jnp.sum(pick * gain_held[s : s + 1, :], axis=1, keepdims=True)
        own_ref[s * width : (s + 1) * width, :length] = dot_rows(pick.astype(jnp.bfloat16), taps_held[s])
        own_ref[s * width : (s + 1) * width, length:] = jnp.broadcast_to(gain, (width, 128))
    both = []
    for copy, held in zip(arriving, (act_held, filt_held)):
        copy.wait()
        turned = [
            dot_rows(eye, held[:, start : start + 128].astype(jnp.bfloat16))
            for start in range(0, held.shape[1], 128)
        ]
        both.append(jnp.concatenate(turned, axis=0))
    for d in range(len(order)):
        part = slice(d * width, (d + 1) * width)
        piece = jnp.concatenate([array[part] for array in both], axis=0).astype(jnp.bfloat16)
        out_ref[2 * d * width : 2 * (d + 1) * width] = piece


def final_kernel(in_ref, out_ref):
    channels, tokens = in_ref.shape
    step = math.gcd(channels, 256)
    eye = identity(tokens)
    for start in range(0, channels, step):
        part = slice(start, start + step)
        out_ref[0, :, part] = dot_rows(eye, in_ref[part]).astype(jnp.bfloat16)


def main_kernel(width, sections, split, order, in_ref, own_ref, turn_ref, table_ref, out_ref):
    total, tokens = in_ref.shape
    cols = tokens // split
    seq = total // (2 * width * sections)
    rows = seq * split
    groups = width // LANES
    high = (rows + 1) * LANES
    span = groups * high
    bf = jnp.bfloat16
    copies = rows + 1
    length = own_ref.shape[1] - 128
    scale = 1.0 / math.sqrt(rows * cols)
    whole = (2 * rows + 1) * cols
    turn = repeated(turn_ref[...], copies)
    cosine, sine = turn[:, :cols], turn[:, cols:]
    all_cos = jnp.concatenate([cosine] * groups, axis=0)
    all_sin = jnp.concatenate([sine] * groups, axis=0)
    forward_cols = table_ref[: 2 * cols, : 2 * cols]
    level, minus = table_ref[:cols, :cols], table_ref[:cols, cols : 2 * cols]
    plus = table_ref[cols : 2 * cols, :cols]
    back_cols = jnp.concatenate(
        [jnp.concatenate([level, plus], axis=1), jnp.concatenate([minus, level], axis=1)], axis=0
    )
    forward_rows = table_ref[2 * cols : 2 * cols + 2 * high, : rows * LANES]
    wide_rows = forward_rows.astype(jnp.float32)
    some_rows = jnp.concatenate([wide_rows[LANES:high], wide_rows[high + LANES :]], axis=0)
    back_rows = dot_rows(identity(rows * LANES), some_rows.astype(bf)).astype(bf)

    def chunk(s):
        starts = [order.index(s * seq + q) * 2 * width for q in range(seq)]
        part = jnp.concatenate([in_ref[at : at + 2 * width] for at in starts], axis=0)
        return part.astype(jnp.float32).reshape(seq, 2 * width, tokens)

    def forward(grids):
        blocks = []
        for grid in grids:
            for g in range(groups):
                part = grid[:, g * LANES : (g + 1) * LANES]
                parts = [part[:, :, h * cols : (h + 1) * cols] for h in range(split)]
                blocks.append(jnp.concatenate(parts, axis=0).reshape(rows * LANES, cols))
        spread = dot(forward_rows, jnp.concatenate(blocks, axis=1).astype(bf))
        turned = []
        for n in range(len(blocks)):
            lanes = slice(n * cols, (n + 1) * cols)
            real, imag = spread[:high, lanes], spread[high:, lanes]
            turned.append(
                jnp.concatenate([real * cosine + imag * sine, imag * cosine - real * sine], axis=1)
            )
        return dot(jnp.concatenate(turned, axis=0).astype(bf), forward_cols)

    def times(left, right):
        lr, li = left[:, :cols], left[:, cols:]
        rr, ri = right
        return jnp.concatenate([lr * rr - li * ri, lr * ri + li * rr], axis=1).astype(bf)

    def back(product):
        flat = dot(product, back_cols)
        real, imag = flat[:, :cols], flat[:, cols:]
        turned_real = real * all_cos - imag * all_sin
        turned_imag = real * all_sin + imag * all_cos
        joined = []
        for g in range(groups):
            part = slice(g * high + LANES, (g + 1) * high)
            joined.append(jnp.concatenate([turned_real[part], turned_imag[part]], axis=0))
        spread = dot(back_rows, jnp.concatenate(joined, axis=1).astype(bf))
        pieces = []
        for g in range(groups):
            piece = spread[:, g * cols : (g + 1) * cols].reshape(rows, LANES, cols)
            piece = piece + turned_real[g * high : g * high + LANES][None]
            parts = [piece[h * seq : (h + 1) * seq] for h in range(split)]
            pieces.append(jnp.concatenate(parts, axis=2))
        return jnp.concatenate(pieces, axis=1)

    def short_specs():
        turned = []
        for s in range(sections):
            for g in range(groups):
                start = s * width + g * LANES
                taps = jnp.concatenate([own_ref[start : start + LANES, :length]] * copies, axis=0)
                turned.append(
                    jnp.concatenate([taps * short_cos, taps * short_sin], axis=1)
                )
        columns = jnp.concatenate([table_ref[:length, : 2 * cols], table_ref[cols : cols + length, : 2 * cols]])
        return dot(jnp.concatenate(turned, axis=0).astype(bf), columns)

    row = lax.broadcasted_iota(jnp.int32, (high, 1), 0)
    weight = jnp.where(row < LANES, scale / whole, 2.0 * scale / whole)
    short_cos, short_sin = cosine[:, :length] * weight, -(sine[:, :length] * weight)
    shorts = short_specs()

    def combine(s, spec):
        gains = own_ref[s * width : (s + 1) * width, length:] * (1.0 / scale)
        gains = jnp.concatenate([gains] * (cols // 128), axis=1)
        shift = jnp.concatenate(
            [gains[g * LANES : (g + 1) * LANES] for g in range(groups) for _ in range(copies)], axis=0
        )
        short = shorts[s * span : (s + 1) * span]
        lr, li = spec[:, :cols] + shift, spec[:, cols:]
        rr, ri = short[:, :cols], short[:, cols:]
        return lr * rr - li * ri, lr * ri + li * rr

    chunks = [chunk(s) for s in range(sections)]
    specs = forward([chunks[0][:, :width]] + [part[:, width:] for part in chunks])
    signal_spec = specs[:span]
    results = []
    for s in range(sections):
        mixed = combine(s, specs[(s + 1) * span : (s + 2) * span])
        result = back(times(signal_spec, mixed))
        results.append(result)
        if s + 1 < sections:
            rounded = result.astype(bf).astype(jnp.float32)
            signal_spec = forward([rounded * chunks[s + 1][:, :width]])
    for at in range(0, len(order), 2):
        pair = [results[rank // seq][rank % seq] for rank in order[at : at + 2]]
        out_ref[at * width : (at + 2) * width] = jnp.concatenate(pair, axis=0).astype(bf)


def body(activations, short_filters, long_filters, skip_gain):
    sections = short_filters.shape[0]
    tokens, channels = activations.shape[1:]
    devices = lax.axis_size(BOTH)
    seq_devices = lax.axis_size("seq")
    owned = channels // devices
    width = -(-owned // LANES) * LANES
    cols = tokens
    laid = devices * width
    order = spread_order(devices, seq_devices)

    def widen(array):
        split = array.reshape(array.shape[:2] + (devices, owned))
        split = jnp.pad(split, ((0, 0), (0, 0), (0, 0), (0, width - owned)))
        return split.reshape(array.shape[:2] + (laid,))

    def exchanged(array, height):
        chunks = array.reshape(devices, height, cols)
        moved = lax.all_to_all(
            chunks, BOTH, split_axis=0, concat_axis=0, tiled=True, axis_index_groups=[list(order)]
        )
        return moved.reshape(devices * height, cols)

    def grant(size):
        return pltpu.CompilerParams(vmem_limit_bytes=int(size))

    acts, filters = activations, long_filters
    if width != owned:
        acts, filters = widen(acts), widen(filters)
    split = 2 if seq_devices <= 32 and cols % 256 == 0 else 1
    table, turn = tables(seq_devices * split, cols // split, split)
    vmem = pl.BlockSpec(memory_space=pltpu.VMEM)
    hbm = pl.BlockSpec(memory_space=pltpu.HBM)
    area = laid * cols
    span = (seq_devices + 1) * width
    taps = short_filters.shape[1]
    place = lax.axis_index(BOTH).astype(jnp.int32).reshape(1)
    inputs = (acts, filters, short_filters, skip_gain)
    outgoing, own = pl.pallas_call(
        functools.partial(send_kernel, width, owned, order),
        out_shape=(
            jax.ShapeDtypeStruct((2 * laid, cols), jnp.bfloat16),
            jax.ShapeDtypeStruct((sections * width, taps + 128), jnp.float32),
        ),
        in_specs=[pl.BlockSpec(memory_space=pltpu.SMEM)] + [hbm] * 4,
        out_specs=(vmem, vmem),
        scratch_shapes=[
            pltpu.VMEM((cols, laid), jnp.bfloat16),
            pltpu.VMEM((cols, laid), jnp.float32),
            pltpu.VMEM(short_filters.shape, jnp.bfloat16),
            pltpu.VMEM(skip_gain.shape, jnp.float32),
            pltpu.SemaphoreType.DMA((2,)),
            pltpu.SemaphoreType.DMA((2,)),
        ],
        compiler_params=grant(4 * MIB + 24 * area),
    )(place, *(pltpu.with_memory_space_constraint(array, pltpu.HBM) for array in inputs))
    arrived = exchanged(outgoing, 2 * width)
    results = pl.pallas_call(
        functools.partial(main_kernel, width, sections, split, order),
        out_shape=jax.ShapeDtypeStruct((laid, cols), jnp.bfloat16),
        in_specs=[vmem] * 4,
        out_specs=vmem,
        compiler_params=grant(2 * MIB + 6 * area + 2 * table.size + 64 * span * cols),
    )(arrived, own, turn, table)
    returned = exchanged(results, width)
    final = pl.pallas_call(
        final_kernel,
        out_shape=jax.ShapeDtypeStruct((1, cols, laid), jnp.bfloat16),
        compiler_params=grant(4 * MIB + 16 * area),
    )(returned)
    if width != owned:
        final = final.reshape(1, cols, devices, width)[..., :owned].reshape(1, cols, channels)
    return final


def solution(mesh):
    return jax.shard_map(
        body,
        mesh=mesh,
        in_specs=(P("segment", "seq", None), P(), P("segment", "seq", None), P()),
        out_specs=P("segment", "seq", None),
        check_vma=False,
    )
```

```python
import functools
import math

import jax
import jax.numpy as jnp
import numpy as np
from jax import lax
from jax.experimental import pallas as pl
from jax.experimental.pallas import tpu as pltpu
from jax.sharding import PartitionSpec as P

BOTH = ("segment", "seq")
LANES = 8
MIB = 1024 * 1024


def spread_order(devices, seq_devices):
    half = seq_devices // 2
    along = [place // 2 + place % 2 * half for place in range(2 * half)]
    along += range(2 * half, seq_devices)
    return tuple(
        start + q for start in range(0, devices, seq_devices) for q in along
    )


def tables(real_rows, cols, split):
    grid_rows = 2 * real_rows + 1
    length = grid_rows * cols
    freqs = real_rows + 1
    k = np.arange(freqs)
    place = np.arange(real_rows).reshape(-1, split).T.reshape(-1)
    rows = 2.0 * math.pi * ((k[:, None] * place[None, :]) % grid_rows) / grid_rows
    first = np.stack([np.cos(rows), -np.sin(rows)]).reshape(2 * freqs, real_rows)
    row_part = np.kron(first, np.eye(LANES))
    b = np.arange(cols)
    angle = 2.0 * math.pi * (k[:, None] * b[None, :]) / length
    turn = np.concatenate([np.cos(angle), np.sin(angle)], axis=1)
    turn = np.pad(turn, ((0, -freqs % LANES), (0, 0)))
    grid = 2.0 * math.pi * ((b[:, None] * b[None, :]) % cols) / cols
    c, s = np.cos(grid), np.sin(grid)
    parts = [np.block([[c, -s], [s, c]]), row_part]
    lanes = max(part.shape[1] for part in parts)
    stacked = np.concatenate([np.pad(p, ((0, 0), (0, lanes - p.shape[1]))) for p in parts])
    return jnp.asarray(stacked, jnp.bfloat16), jnp.asarray(turn, jnp.float32)


def dot(a, b):
    return jnp.dot(a, b, preferred_element_type=jnp.float32)


def dot_rows(a, b):
    return lax.dot_general(a, b, (((1,), (1,)), ((), ())), preferred_element_type=jnp.float32)


def repeated(rows, count):
    return jnp.concatenate(
        [jnp.broadcast_to(rows[k : k + 1], (LANES, rows.shape[1])) for k in range(count)], axis=0
    )


def identity(size):
    down = lax.broadcasted_iota(jnp.int32, (size, size), 0)
    across = lax.broadcasted_iota(jnp.int32, (size, size), 1)
    return jnp.where(down == across, 1.0, 0.0).astype(jnp.bfloat16)


def send_kernel(
    width,
    owned,
    order,
    place_ref,
    act_ref,
    filt_ref,
    taps_ref,
    gain_ref,
    out_ref,
    own_ref,
    act_held,
    filt_held,
    taps_held,
    gain_held,
    in_sem,
    own_sem,
):
    sections, length, channels = taps_ref.shape
    mine_first = (
        pltpu.make_async_copy(taps_ref, taps_held, own_sem.at[0]),
        pltpu.make_async_copy(gain_ref, gain_held, own_sem.at[1]),
    )
    for copy in mine_first:
        copy.start()
    half = act_ref.shape[1] // 2
    arriving = [
        pltpu.make_async_copy(filt_ref.at[0, :half], filt_held.at[:half], in_sem.at[0]),
        pltpu.make_async_copy(act_ref.at[0], act_held, in_sem.at[1]),
        pltpu.make_async_copy(filt_ref.at[0, half:], filt_held.at[half:], in_sem.at[2]),
    ]
    for copy in arriving:
        copy.start()
    eye = identity(128)
    mine = lax.broadcasted_iota(jnp.int32, (width, channels), 0)
    them = lax.broadcasted_iota(jnp.int32, (width, channels), 1)
    place = jnp.int32(0)
    for position, rank in enumerate(order):
        place = place + jnp.where(place_ref[0] == rank, position, 0)
    pick = jnp.where((them == mine + place * owned) & (mine < owned), 1.0, 0.0)
    for copy in mine_first:
        copy.wait()
    for s in range(sections):
        gain = jnp.sum(pick * gain_held[s : s + 1, :], axis=1, keepdims=True)
        own_ref[s * width : (s + 1) * width, :length] = dot_rows(pick.astype(jnp.bfloat16), taps_held[s])
        own_ref[s * width : (s + 1) * width, length:] = jnp.broadcast_to(gain, (width, 128))
    turned = []
    for copy, held in zip(arriving, (filt_held.at[:half], act_held, filt_held.at[half:])):
        copy.wait()
        columns = [
            dot_rows(eye, held[:, start : start + 128].astype(jnp.bfloat16))
            for start in range(0, held.shape[1], 128)
        ]
        turned.append(jnp.concatenate(columns, axis=0))
    both = (turned[1], jnp.concatenate([turned[0], turned[2]], axis=1))
    for d in range(len(order)):
        part = slice(d * width, (d + 1) * width)
        piece = jnp.concatenate([array[part] for array in both], axis=0).astype(jnp.bfloat16)
        out_ref[2 * d * width : 2 * (d + 1) * width] = piece


def final_kernel(in_ref, out_ref):
    channels, tokens = in_ref.shape
    step = math.gcd(channels, 256)
    eye = identity(tokens)
    for start in range(0, channels, step):
        part = slice(start, start + step)
        out_ref[0, :, part] = dot_rows(eye, in_ref[part]).astype(jnp.bfloat16)


def main_kernel(width, sections, split, order, in_ref, own_ref, turn_ref, table_ref, out_ref):
    total, tokens = in_ref.shape
    cols = tokens // split
    seq = total // (2 * width * sections)
    rows = seq * split
    groups = width // LANES
    high = (rows + 1) * LANES
    bf = jnp.bfloat16
    copies = rows + 1
    length = own_ref.shape[1] - 128
    scale = 1.0 / math.sqrt(rows * cols)
    whole = (2 * rows + 1) * cols
    turn = repeated(turn_ref[...], copies)
    cosine, sine = turn[:, :cols], turn[:, cols:]
    forward_cols = table_ref[: 2 * cols, : 2 * cols]
    level, minus = table_ref[:cols, :cols], table_ref[:cols, cols : 2 * cols]
    plus = table_ref[cols : 2 * cols, :cols]
    back_cols = jnp.concatenate(
        [jnp.concatenate([level, plus], axis=1), jnp.concatenate([minus, level], axis=1)], axis=0
    )
    forward_rows = table_ref[2 * cols : 2 * cols + 2 * high, : rows * LANES]
    wide_rows = forward_rows.astype(jnp.float32)
    some_rows = jnp.concatenate([wide_rows[LANES:high], wide_rows[high + LANES :]], axis=0)
    back_rows = dot_rows(identity(rows * LANES), some_rows.astype(bf)).astype(bf)

    def chunk(s):
        starts = [order.index(s * seq + q) * 2 * width for q in range(seq)]
        part = jnp.concatenate([in_ref[at : at + 2 * width] for at in starts], axis=0)
        return part.astype(jnp.float32).reshape(seq, 2 * width, tokens)

    def forward(grids):
        blocks = []
        for g in over:
            for grid in grids:
                part = grid[:, g * LANES : (g + 1) * LANES]
                parts = [part[:, :, h * cols : (h + 1) * cols] for h in range(split)]
                blocks.append(jnp.concatenate(parts, axis=0).reshape(rows * LANES, cols))
        spread = dot(forward_rows, jnp.concatenate(blocks, axis=1).astype(bf))
        turned = []
        for n in range(len(blocks)):
            lanes = slice(n * cols, (n + 1) * cols)
            real, imag = spread[:high, lanes], spread[high:, lanes]
            turned.append(
                jnp.concatenate([real * cosine + imag * sine, imag * cosine - real * sine], axis=1)
            )
        count = len(grids)
        stacked = [jnp.concatenate(turned[g * count : (g + 1) * count], axis=0) for g in over]
        return [dot(part.astype(bf), forward_cols) for part in stacked]

    def times(left, right):
        lr, li = left[:, :cols], left[:, cols:]
        rr, ri = right
        return jnp.concatenate([lr * rr - li * ri, lr * ri + li * rr], axis=1).astype(bf)

    def back(products):
        joined, firsts = [], []
        for flat in [dot(product, back_cols) for product in products]:
            real, imag = flat[:, :cols], flat[:, cols:]
            turned_real = real * cosine - imag * sine
            turned_imag = real * sine + imag * cosine
            firsts.append(turned_real[:LANES][None])
            joined.append(jnp.concatenate([turned_real[LANES:], turned_imag[LANES:]], axis=0))
        spread = dot(back_rows, jnp.concatenate(joined, axis=1).astype(bf))
        pieces = []
        for g in over:
            piece = spread[:, g * cols : (g + 1) * cols].reshape(rows, LANES, cols) + firsts[g]
            parts = [piece[h * seq : (h + 1) * seq] for h in range(split)]
            pieces.append(jnp.concatenate(parts, axis=2))
        return jnp.concatenate(pieces, axis=1)

    row = lax.broadcasted_iota(jnp.int32, (high, 1), 0)
    weight = jnp.where(row < LANES, scale / whole, 2.0 * scale / whole)
    short_cos, short_sin = cosine[:, :length] * weight, -(sine[:, :length] * weight)
    short_cols = jnp.concatenate(
        [table_ref[:length, : 2 * cols], table_ref[cols : cols + length, : 2 * cols]], axis=0
    )

    def short_half(s, g):
        start = s * width + g * LANES
        taps = jnp.concatenate([own_ref[start : start + LANES, :length]] * copies, axis=0)
        return jnp.concatenate([taps * short_cos, taps * short_sin], axis=1)

    def combine(s, g, short, spec):
        start = s * width + g * LANES
        gains = own_ref[start : start + LANES, length:] * (1.0 / scale)
        gains = jnp.concatenate([gains] * (cols // 128), axis=1)
        lr, li = spec[:, :cols] + jnp.concatenate([gains] * copies, axis=0), spec[:, cols:]
        rr, ri = short[:, :cols], short[:, cols:]
        return lr * rr - li * ri, lr * ri + li * rr

    over = range(groups)
    chunks = [chunk(s) for s in range(sections)]
    specs = forward([chunks[0][:, :width]] + [part[:, width:] for part in chunks])
    signals = [spec[:high] for spec in specs]
    shorts = [
        dot(jnp.concatenate([short_half(s, g) for s in range(sections)], axis=0).astype(bf), short_cols)
        for g in over
    ]
    results = []
    for s in range(sections):
        part, after = slice(s * high, (s + 1) * high), slice((s + 1) * high, (s + 2) * high)
        result = back(
            [times(signals[g], combine(s, g, shorts[g][part], specs[g][after])) for g in over]
        )
        results.append(result)
        if s + 1 < sections:
            rounded = result.astype(bf).astype(jnp.float32)
            signals = forward([rounded * chunks[s + 1][:, :width]])
    for at in range(0, len(order), 2):
        pair = [results[rank // seq][rank % seq] for rank in order[at : at + 2]]
        out_ref[at * width : (at + 2) * width] = jnp.concatenate(pair, axis=0).astype(bf)


def body(activations, short_filters, long_filters, skip_gain):
    sections = short_filters.shape[0]
    tokens, channels = activations.shape[1:]
    devices = lax.axis_size(BOTH)
    seq_devices = lax.axis_size("seq")
    owned = channels // devices
    width = -(-owned // LANES) * LANES
    cols = tokens
    laid = devices * width
    order = spread_order(devices, seq_devices)

    def widen(array):
        split = array.reshape(array.shape[:2] + (devices, owned))
        split = jnp.pad(split, ((0, 0), (0, 0), (0, 0), (0, width - owned)))
        return split.reshape(array.shape[:2] + (laid,))

    def exchanged(array, height):
        chunks = array.reshape(devices, height, cols)
        moved = lax.all_to_all(
            chunks, BOTH, split_axis=0, concat_axis=0, tiled=True, axis_index_groups=[list(order)]
        )
        return moved.reshape(devices * height, cols)

    def grant(size):
        return pltpu.CompilerParams(vmem_limit_bytes=int(size))

    acts, filters = activations, long_filters
    if width != owned:
        acts, filters = widen(acts), widen(filters)
    split = 2 if seq_devices <= 32 and cols % 256 == 0 else 1
    table, turn = tables(seq_devices * split, cols // split, split)
    vmem = pl.BlockSpec(memory_space=pltpu.VMEM)
    hbm = pl.BlockSpec(memory_space=pltpu.HBM)
    area = laid * cols
    span = (seq_devices + 1) * width
    taps = short_filters.shape[1]
    place = lax.axis_index(BOTH).astype(jnp.int32).reshape(1)
    inputs = (acts, filters, short_filters, skip_gain)
    outgoing, own = pl.pallas_call(
        functools.partial(send_kernel, width, owned, order),
        out_shape=(
            jax.ShapeDtypeStruct((2 * laid, cols), jnp.bfloat16),
            jax.ShapeDtypeStruct((sections * width, taps + 128), jnp.float32),
        ),
        in_specs=[pl.BlockSpec(memory_space=pltpu.SMEM)] + [hbm] * 4,
        out_specs=(vmem, vmem),
        scratch_shapes=[
            pltpu.VMEM((cols, laid), jnp.bfloat16),
            pltpu.VMEM((cols, laid), jnp.float32),
            pltpu.VMEM(short_filters.shape, jnp.bfloat16),
            pltpu.VMEM(skip_gain.shape, jnp.float32),
            pltpu.SemaphoreType.DMA((3,)),
            pltpu.SemaphoreType.DMA((2,)),
        ],
        compiler_params=grant(4 * MIB + 24 * area),
    )(place, *(pltpu.with_memory_space_constraint(array, pltpu.HBM) for array in inputs))
    arrived = exchanged(outgoing, 2 * width)
    results = pl.pallas_call(
        functools.partial(main_kernel, width, sections, split, order),
        out_shape=jax.ShapeDtypeStruct((laid, cols), jnp.bfloat16),
        in_specs=[vmem] * 4,
        out_specs=vmem,
        compiler_params=grant(2 * MIB + 6 * area + 2 * table.size + 64 * span * cols),
    )(arrived, own, turn, table)
    returned = exchanged(results, width)
    final = pl.pallas_call(
        final_kernel,
        out_shape=jax.ShapeDtypeStruct((1, cols, laid), jnp.bfloat16),
        compiler_params=grant(4 * MIB + 16 * area),
    )(returned)
    if width != owned:
        final = final.reshape(1, cols, devices, width)[..., :owned].reshape(1, cols, channels)
    return final


def solution(mesh):
    return jax.shard_map(
        body,
        mesh=mesh,
        in_specs=(P("segment", "seq", None), P(), P("segment", "seq", None), P()),
        out_specs=P("segment", "seq", None),
        check_vma=False,
    )
```

```python
import functools
import math

import jax
import jax.numpy as jnp
import numpy as np
from jax import lax
from jax.experimental import pallas as pl
from jax.experimental.pallas import tpu as pltpu
from jax.sharding import PartitionSpec as P

BOTH = ("segment", "seq")
LANES = 8
MIB = 1024 * 1024


def spread_order(devices, seq_devices):
    half = seq_devices // 2
    along = [place // 2 + place % 2 * half for place in range(2 * half)]
    along += range(2 * half, seq_devices)
    return tuple(
        start + q for start in range(0, devices, seq_devices) for q in along
    )


def tables(real_rows, cols, split):
    grid_rows = 2 * real_rows + 1
    length = grid_rows * cols
    freqs = real_rows + 1
    k = np.arange(freqs)
    place = np.arange(real_rows).reshape(-1, split).T.reshape(-1)
    rows = 2.0 * math.pi * ((k[:, None] * place[None, :]) % grid_rows) / grid_rows
    first = np.stack([np.cos(rows), -np.sin(rows)]).reshape(2 * freqs, real_rows)
    row_part = np.kron(first, np.eye(LANES))
    b = np.arange(cols)
    angle = 2.0 * math.pi * (k[:, None] * b[None, :]) / length
    turn = np.concatenate([np.cos(angle), np.sin(angle)], axis=1)
    turn = np.pad(turn, ((0, -freqs % LANES), (0, 0)))
    grid = 2.0 * math.pi * ((b[:, None] * b[None, :]) % cols) / cols
    c, s = np.cos(grid), np.sin(grid)
    parts = [np.block([[c, -s], [s, c]]), row_part]
    lanes = max(part.shape[1] for part in parts)
    stacked = np.concatenate([np.pad(p, ((0, 0), (0, lanes - p.shape[1]))) for p in parts])
    return jnp.asarray(stacked, jnp.bfloat16), jnp.asarray(turn, jnp.float32)


def dot(a, b):
    return jnp.dot(a, b, preferred_element_type=jnp.float32)


def dot_rows(a, b):
    return lax.dot_general(a, b, (((1,), (1,)), ((), ())), preferred_element_type=jnp.float32)


def repeated(rows, count):
    return jnp.concatenate(
        [jnp.broadcast_to(rows[k : k + 1], (LANES, rows.shape[1])) for k in range(count)], axis=0
    )


def identity(size):
    down = lax.broadcasted_iota(jnp.int32, (size, size), 0)
    across = lax.broadcasted_iota(jnp.int32, (size, size), 1)
    return jnp.where(down == across, 1.0, 0.0).astype(jnp.bfloat16)


def send_kernel(
    width,
    owned,
    order,
    place_ref,
    act_ref,
    filt_ref,
    taps_ref,
    gain_ref,
    out_ref,
    own_ref,
    act_held,
    filt_held,
    taps_held,
    gain_held,
    in_sem,
    own_sem,
):
    sections, length, channels = taps_ref.shape
    mine_first = (
        pltpu.make_async_copy(taps_ref, taps_held, own_sem.at[0]),
        pltpu.make_async_copy(gain_ref, gain_held, own_sem.at[1]),
    )
    for copy in mine_first:
        copy.start()
    arriving = (
        pltpu.make_async_copy(act_ref.at[0], act_held, in_sem.at[0]),
        pltpu.make_async_copy(filt_ref.at[0], filt_held, in_sem.at[1]),
    )
    for copy in arriving:
        copy.start()
    size = math.gcd(act_ref.shape[2], 256)
    eye = identity(size)
    mine = lax.broadcasted_iota(jnp.int32, (width, channels), 0)
    them = lax.broadcasted_iota(jnp.int32, (width, channels), 1)
    place = jnp.int32(0)
    for position, rank in enumerate(order):
        place = place + jnp.where(place_ref[0] == rank, position, 0)
    pick = jnp.where((them == mine + place * owned) & (mine < owned), 1.0, 0.0)
    for copy in mine_first:
        copy.wait()
    for s in range(sections):
        gain = jnp.sum(pick * gain_held[s : s + 1, :], axis=1, keepdims=True)
        own_ref[s * width : (s + 1) * width, :length] = dot_rows(pick.astype(jnp.bfloat16), taps_held[s])
        own_ref[s * width : (s + 1) * width, length:] = jnp.broadcast_to(gain, (width, 128))
    def across(copy, held):
        copy.wait()
        columns = [
            dot_rows(eye, held[:, start : start + size].astype(jnp.bfloat16))
            for start in range(0, held.shape[1], size)
        ]
        return jnp.concatenate(columns, axis=0)

    even = width // 16 * 16
    act = across(arriving[0], act_held)
    for d in range(len(order) if even else 0):
        start = d * width
        out_ref[2 * start : 2 * start + even] = act[start : start + even].astype(jnp.bfloat16)
    filt = across(arriving[1], filt_held)
    for d in range(len(order)):
        start, end = d * width, (d + 1) * width
        parts = [act[start + even : end], filt[start + even : end], filt[start : start + even]]
        rest = jnp.concatenate([part for part in parts if part.shape[0]], axis=0)
        out_ref[2 * start + even : 2 * end] = rest.astype(jnp.bfloat16)


def final_kernel(in_ref, out_ref):
    channels, tokens = in_ref.shape
    step = math.gcd(channels, 256)
    eye = identity(tokens)
    for start in range(0, channels, step):
        part = slice(start, start + step)
        out_ref[0, :, part] = dot_rows(eye, in_ref[part]).astype(jnp.bfloat16)


def main_kernel(width, sections, split, order, in_ref, own_ref, turn_ref, table_ref, out_ref):
    total, tokens = in_ref.shape
    cols = tokens // split
    seq = total // (2 * width * sections)
    rows = seq * split
    groups = width // LANES
    high = (rows + 1) * LANES
    span = groups * high
    bf = jnp.bfloat16
    copies = rows + 1
    length = own_ref.shape[1] - 128
    scale = 1.0 / math.sqrt(rows * cols)
    whole = (2 * rows + 1) * cols
    turn = repeated(turn_ref[...], copies)
    cosine, sine = turn[:, :cols], turn[:, cols:]
    all_cos = jnp.concatenate([cosine] * groups, axis=0)
    all_sin = jnp.concatenate([sine] * groups, axis=0)
    forward_cols = table_ref[: 2 * cols, : 2 * cols]
    level, minus = table_ref[:cols, :cols], table_ref[:cols, cols : 2 * cols]
    plus = table_ref[cols : 2 * cols, :cols]
    back_cols = jnp.concatenate(
        [jnp.concatenate([level, plus], axis=1), jnp.concatenate([minus, level], axis=1)], axis=0
    )
    forward_rows = table_ref[2 * cols : 2 * cols + 2 * high, : rows * LANES]
    wide_rows = forward_rows.astype(jnp.float32)
    some_rows = jnp.concatenate([wide_rows[LANES:high], wide_rows[high + LANES :]], axis=0)
    back_rows = dot_rows(identity(rows * LANES), some_rows.astype(bf)).astype(bf)

    def chunk(s):
        starts = [order.index(s * seq + q) * 2 * width for q in range(seq)]
        part = jnp.concatenate([in_ref[at : at + 2 * width] for at in starts], axis=0)
        return part.astype(jnp.float32).reshape(seq, 2 * width, tokens)

    def forward(grids):
        blocks = []
        for grid in grids:
            for g in range(groups):
                part = grid[:, g * LANES : (g + 1) * LANES]
                parts = [part[:, :, h * cols : (h + 1) * cols] for h in range(split)]
                blocks.append(jnp.concatenate(parts, axis=0).reshape(rows * LANES, cols))
        spread = dot(forward_rows, jnp.concatenate(blocks, axis=1).astype(bf))
        turned = []
        for n in range(len(blocks)):
            lanes = slice(n * cols, (n + 1) * cols)
            real, imag = spread[:high, lanes], spread[high:, lanes]
            turned.append(
                jnp.concatenate([real * cosine + imag * sine, imag * cosine - real * sine], axis=1)
            )
        return dot(jnp.concatenate(turned, axis=0).astype(bf), forward_cols)

    def times(left, right):
        lr, li = left[:, :cols], left[:, cols:]
        rr, ri = right
        return jnp.concatenate([lr * rr - li * ri, lr * ri + li * rr], axis=1).astype(bf)

    def back(product):
        flat = dot(product, back_cols)
        real, imag = flat[:, :cols], flat[:, cols:]
        turned_real = real * all_cos - imag * all_sin
        turned_imag = real * all_sin + imag * all_cos
        joined = []
        for g in range(groups):
            part = slice(g * high + LANES, (g + 1) * high)
            joined.append(jnp.concatenate([turned_real[part], turned_imag[part]], axis=0))
        spread = dot(back_rows, jnp.concatenate(joined, axis=1).astype(bf))
        pieces = []
        for g in range(groups):
            piece = spread[:, g * cols : (g + 1) * cols].reshape(rows, LANES, cols)
            piece = piece + turned_real[g * high : g * high + LANES][None]
            parts = [piece[h * seq : (h + 1) * seq] for h in range(split)]
            pieces.append(jnp.concatenate(parts, axis=2))
        return jnp.concatenate(pieces, axis=1)

    def short_specs():
        turned = []
        for s in range(sections):
            for g in range(groups):
                start = s * width + g * LANES
                taps = jnp.concatenate([own_ref[start : start + LANES, :length]] * copies, axis=0)
                turned.append(
                    jnp.concatenate([taps * short_cos, taps * short_sin], axis=1)
                )
        columns = jnp.concatenate([table_ref[:length, : 2 * cols], table_ref[cols : cols + length, : 2 * cols]])
        return dot(jnp.concatenate(turned, axis=0).astype(bf), columns)

    row = lax.broadcasted_iota(jnp.int32, (high, 1), 0)
    weight = jnp.where(row < LANES, scale / whole, 2.0 * scale / whole)
    short_cos, short_sin = cosine[:, :length] * weight, -(sine[:, :length] * weight)
    shorts = short_specs()

    def combine(s, spec):
        gains = own_ref[s * width : (s + 1) * width, length:] * (1.0 / scale)
        gains = jnp.concatenate([gains] * (cols // 128), axis=1)
        shift = jnp.concatenate(
            [gains[g * LANES : (g + 1) * LANES] for g in range(groups) for _ in range(copies)], axis=0
        )
        short = shorts[s * span : (s + 1) * span]
        lr, li = spec[:, :cols] + shift, spec[:, cols:]
        rr, ri = short[:, :cols], short[:, cols:]
        return lr * rr - li * ri, lr * ri + li * rr

    chunks = [chunk(s) for s in range(sections)]
    odd = 2 * width - width // 16 * 16
    longs = [jnp.concatenate([part[:, odd:], part[:, width:odd]], axis=1) for part in chunks]
    if odd == 2 * width:
        longs = [part[:, width:] for part in chunks]
    specs = forward([chunks[0][:, :width]] + longs)
    signal_spec = specs[:span]
    results = []
    for s in range(sections):
        mixed = combine(s, specs[(s + 1) * span : (s + 2) * span])
        result = back(times(signal_spec, mixed))
        results.append(result)
        if s + 1 < sections:
            rounded = result.astype(bf).astype(jnp.float32)
            signal_spec = forward([rounded * chunks[s + 1][:, :width]])
    for at in range(0, len(order), 2):
        pair = [results[rank // seq][rank % seq] for rank in order[at : at + 2]]
        out_ref[at * width : (at + 2) * width] = jnp.concatenate(pair, axis=0).astype(bf)


def body(activations, short_filters, long_filters, skip_gain):
    sections = short_filters.shape[0]
    tokens, channels = activations.shape[1:]
    devices = lax.axis_size(BOTH)
    seq_devices = lax.axis_size("seq")
    owned = channels // devices
    width = -(-owned // LANES) * LANES
    cols = tokens
    laid = devices * width
    order = spread_order(devices, seq_devices)

    def widen(array):
        split = array.reshape(array.shape[:2] + (devices, owned))
        split = jnp.pad(split, ((0, 0), (0, 0), (0, 0), (0, width - owned)))
        return split.reshape(array.shape[:2] + (laid,))

    def exchanged(array, height):
        chunks = array.reshape(devices, height, cols)
        moved = lax.all_to_all(
            chunks, BOTH, split_axis=0, concat_axis=0, tiled=True, axis_index_groups=[list(order)]
        )
        return moved.reshape(devices * height, cols)

    def grant(size):
        return pltpu.CompilerParams(vmem_limit_bytes=int(size))

    acts, filters = activations, long_filters
    if width != owned:
        acts, filters = widen(acts), widen(filters)
    split = 2 if seq_devices <= 32 and cols % 256 == 0 else 1
    table, turn = tables(seq_devices * split, cols // split, split)
    vmem = pl.BlockSpec(memory_space=pltpu.VMEM)
    hbm = pl.BlockSpec(memory_space=pltpu.HBM)
    area = laid * cols
    span = (seq_devices + 1) * width
    taps = short_filters.shape[1]
    place = lax.axis_index(BOTH).astype(jnp.int32).reshape(1)
    inputs = (acts, filters, short_filters, skip_gain)
    outgoing, own = pl.pallas_call(
        functools.partial(send_kernel, width, owned, order),
        out_shape=(
            jax.ShapeDtypeStruct((2 * laid, cols), jnp.bfloat16),
            jax.ShapeDtypeStruct((sections * width, taps + 128), jnp.float32),
        ),
        in_specs=[pl.BlockSpec(memory_space=pltpu.SMEM)] + [hbm] * 4,
        out_specs=(vmem, vmem),
        scratch_shapes=[
            pltpu.VMEM((cols, laid), jnp.bfloat16),
            pltpu.VMEM((cols, laid), jnp.float32),
            pltpu.VMEM(short_filters.shape, jnp.bfloat16),
            pltpu.VMEM(skip_gain.shape, jnp.float32),
            pltpu.SemaphoreType.DMA((2,)),
            pltpu.SemaphoreType.DMA((2,)),
        ],
        compiler_params=grant(4 * MIB + 24 * area),
    )(place, *(pltpu.with_memory_space_constraint(array, pltpu.HBM) for array in inputs))
    arrived = exchanged(outgoing, 2 * width)
    results = pl.pallas_call(
        functools.partial(main_kernel, width, sections, split, order),
        out_shape=jax.ShapeDtypeStruct((laid, cols), jnp.bfloat16),
        in_specs=[vmem] * 4,
        out_specs=vmem,
        compiler_params=grant(2 * MIB + 6 * area + 2 * table.size + 64 * span * cols),
    )(arrived, own, turn, table)
    returned = exchanged(results, width)
    final = pl.pallas_call(
        final_kernel,
        out_shape=jax.ShapeDtypeStruct((1, cols, laid), jnp.bfloat16),
        compiler_params=grant(4 * MIB + 16 * area),
    )(returned)
    if width != owned:
        final = final.reshape(1, cols, devices, width)[..., :owned].reshape(1, cols, channels)
    return final


def solution(mesh):
    return jax.shard_map(
        body,
        mesh=mesh,
        in_specs=(P("segment", "seq", None), P(), P("segment", "seq", None), P()),
        out_specs=P("segment", "seq", None),
        check_vma=False,
    )
```

```python
import functools
import math

import jax
import jax.numpy as jnp
import numpy as np
from jax import lax
from jax.experimental import pallas as pl
from jax.experimental.pallas import tpu as pltpu
from jax.sharding import PartitionSpec as P

BOTH = ("segment", "seq")
LANES = 8
MIB = 1024 * 1024


FIELDS = {2: 7, 3: 11, 4: 19, 5: 37, 6: 67, 7: 131, 8: 285, 9: 529, 10: 1033}


def spread_order(devices):
    bits = devices.bit_length() - 1
    if devices != 1 << bits or bits not in FIELDS:
        return tuple(range(devices))
    order, power = [0], 1
    while len(order) < devices:
        order.append(power)
        power <<= 1
        if power & devices:
            power ^= FIELDS[bits]
    return tuple(order)


def tables(real_rows, cols, split):
    grid_rows = 2 * real_rows + 1
    length = grid_rows * cols
    freqs = real_rows + 1
    k = np.arange(freqs)
    place = np.arange(real_rows).reshape(-1, split).T.reshape(-1)
    rows = 2.0 * math.pi * ((k[:, None] * place[None, :]) % grid_rows) / grid_rows
    first = np.stack([np.cos(rows), -np.sin(rows)]).reshape(2 * freqs, real_rows)
    row_part = np.kron(first, np.eye(LANES))
    b = np.arange(cols)
    angle = 2.0 * math.pi * (k[:, None] * b[None, :]) / length
    turn = np.concatenate([np.cos(angle), np.sin(angle)], axis=1)
    turn = np.pad(turn, ((0, -freqs % LANES), (0, 0)))
    grid = 2.0 * math.pi * ((b[:, None] * b[None, :]) % cols) / cols
    c, s = np.cos(grid), np.sin(grid)
    parts = [np.block([[c, -s], [s, c]]), row_part]
    lanes = max(part.shape[1] for part in parts)
    stacked = np.concatenate([np.pad(p, ((0, 0), (0, lanes - p.shape[1]))) for p in parts])
    return jnp.asarray(stacked, jnp.bfloat16), jnp.asarray(turn, jnp.float32)


def dot(a, b):
    return jnp.dot(a, b, preferred_element_type=jnp.float32)


def dot_rows(a, b):
    return lax.dot_general(a, b, (((1,), (1,)), ((), ())), preferred_element_type=jnp.float32)


def repeated(rows, count):
    return jnp.concatenate(
        [jnp.broadcast_to(rows[k : k + 1], (LANES, rows.shape[1])) for k in range(count)], axis=0
    )


def identity(size):
    down = lax.broadcasted_iota(jnp.int32, (size, size), 0)
    across = lax.broadcasted_iota(jnp.int32, (size, size), 1)
    return jnp.where(down == across, 1.0, 0.0).astype(jnp.bfloat16)


def send_kernel(
    width,
    owned,
    order,
    place_ref,
    act_ref,
    filt_ref,
    taps_ref,
    gain_ref,
    out_ref,
    own_ref,
    act_held,
    filt_held,
    taps_held,
    gain_held,
    in_sem,
    own_sem,
):
    sections, length, channels = taps_ref.shape
    mine_first = (
        pltpu.make_async_copy(taps_ref, taps_held, own_sem.at[0]),
        pltpu.make_async_copy(gain_ref, gain_held, own_sem.at[1]),
    )
    for copy in mine_first:
        copy.start()
    arriving = (
        pltpu.make_async_copy(act_ref.at[0], act_held, in_sem.at[0]),
        pltpu.make_async_copy(filt_ref.at[0], filt_held, in_sem.at[1]),
    )
    for copy in arriving:
        copy.start()
    size = 128
    eye = identity(size)
    mine = lax.broadcasted_iota(jnp.int32, (width, channels), 0)
    them = lax.broadcasted_iota(jnp.int32, (width, channels), 1)
    place = jnp.int32(0)
    for position, rank in enumerate(order):
        place = place + jnp.where(place_ref[0] == rank, position, 0)
    pick = jnp.where((them == mine + place * owned) & (mine < owned), 1.0, 0.0)
    for copy in mine_first:
        copy.wait()
    for s in range(sections):
        gain = jnp.sum(pick * gain_held[s : s + 1, :], axis=1, keepdims=True)
        own_ref[s * width : (s + 1) * width, :length] = dot_rows(pick.astype(jnp.bfloat16), taps_held[s])
        own_ref[s * width : (s + 1) * width, length:] = jnp.broadcast_to(gain, (width, 128))
    def across(copy, held):
        copy.wait()
        columns = [
            dot_rows(eye, held[:, start : start + size].astype(jnp.bfloat16))
            for start in range(0, held.shape[1], size)
        ]
        return jnp.concatenate(columns, axis=0)

    even = width // 16 * 16
    act = across(arriving[0], act_held)
    for d in range(len(order) if even else 0):
        start = d * width
        out_ref[2 * start : 2 * start + even] = act[start : start + even].astype(jnp.bfloat16)
    filt = across(arriving[1], filt_held)
    for d in range(len(order)):
        start, end = d * width, (d + 1) * width
        parts = [act[start + even : end], filt[start + even : end], filt[start : start + even]]
        rest = jnp.concatenate([part for part in parts if part.shape[0]], axis=0)
        out_ref[2 * start + even : 2 * end] = rest.astype(jnp.bfloat16)


def final_kernel(in_ref, out_ref):
    channels, tokens = in_ref.shape
    step = math.gcd(channels, 256)
    eye = identity(tokens)
    for start in range(0, channels, step):
        part = slice(start, start + step)
        out_ref[0, :, part] = dot_rows(eye, in_ref[part]).astype(jnp.bfloat16)


def main_kernel(width, sections, split, order, in_ref, own_ref, turn_ref, table_ref, out_ref):
    total, tokens = in_ref.shape
    cols = tokens // split
    seq = total // (2 * width * sections)
    rows = seq * split
    groups = width // LANES
    high = (rows + 1) * LANES
    span = groups * high
    bf = jnp.bfloat16
    copies = rows + 1
    length = own_ref.shape[1] - 128
    scale = 1.0 / math.sqrt(rows * cols)
    whole = (2 * rows + 1) * cols
    turn = repeated(turn_ref[...], copies)
    cosine, sine = turn[:, :cols], turn[:, cols:]
    all_cos = jnp.concatenate([cosine] * groups, axis=0)
    all_sin = jnp.concatenate([sine] * groups, axis=0)
    forward_cols = table_ref[: 2 * cols, : 2 * cols]
    level, minus = table_ref[:cols, :cols], table_ref[:cols, cols : 2 * cols]
    plus = table_ref[cols : 2 * cols, :cols]
    back_cols = jnp.concatenate(
        [jnp.concatenate([level, plus], axis=1), jnp.concatenate([minus, level], axis=1)], axis=0
    )
    forward_rows = table_ref[2 * cols : 2 * cols + 2 * high, : rows * LANES]
    wide_rows = forward_rows.astype(jnp.float32)
    some_rows = jnp.concatenate([wide_rows[LANES:high], wide_rows[high + LANES :]], axis=0)
    back_rows = dot_rows(identity(rows * LANES), some_rows.astype(bf)).astype(bf)

    def chunk(s):
        starts = [order.index(s * seq + q) * 2 * width for q in range(seq)]
        part = jnp.concatenate([in_ref[at : at + 2 * width] for at in starts], axis=0)
        return part.astype(jnp.float32).reshape(seq, 2 * width, tokens)

    def forward(grids):
        blocks = []
        for grid in grids:
            for g in range(groups):
                part = grid[:, g * LANES : (g + 1) * LANES]
                parts = [part[:, :, h * cols : (h + 1) * cols] for h in range(split)]
                blocks.append(jnp.concatenate(parts, axis=0).reshape(rows * LANES, cols))
        spread = dot(forward_rows, jnp.concatenate(blocks, axis=1).astype(bf))
        turned = []
        for n in range(len(blocks)):
            lanes = slice(n * cols, (n + 1) * cols)
            real, imag = spread[:high, lanes], spread[high:, lanes]
            turned.append(
                jnp.concatenate([real * cosine + imag * sine, imag * cosine - real * sine], axis=1)
            )
        return dot(jnp.concatenate(turned, axis=0).astype(bf), forward_cols)

    def times(left, right):
        lr, li = left[:, :cols], left[:, cols:]
        rr, ri = right
        return jnp.concatenate([lr * rr - li * ri, lr * ri + li * rr], axis=1).astype(bf)

    def back(product):
        flat = dot(product, back_cols)
        real, imag = flat[:, :cols], flat[:, cols:]
        turned_real = real * all_cos - imag * all_sin
        turned_imag = real * all_sin + imag * all_cos
        joined = []
        for g in range(groups):
            part = slice(g * high + LANES, (g + 1) * high)
            joined.append(jnp.concatenate([turned_real[part], turned_imag[part]], axis=0))
        spread = dot(back_rows, jnp.concatenate(joined, axis=1).astype(bf))
        pieces = []
        for g in range(groups):
            piece = spread[:, g * cols : (g + 1) * cols].reshape(rows, LANES, cols)
            piece = piece + turned_real[g * high : g * high + LANES][None]
            parts = [piece[h * seq : (h + 1) * seq] for h in range(split)]
            pieces.append(jnp.concatenate(parts, axis=2))
        return jnp.concatenate(pieces, axis=1)

    def short_specs():
        turned = []
        for s in range(sections):
            for g in range(groups):
                start = s * width + g * LANES
                taps = jnp.concatenate([own_ref[start : start + LANES, :length]] * copies, axis=0)
                turned.append(
                    jnp.concatenate([taps * short_cos, taps * short_sin], axis=1)
                )
        columns = jnp.concatenate([table_ref[:length, : 2 * cols], table_ref[cols : cols + length, : 2 * cols]])
        return dot(jnp.concatenate(turned, axis=0).astype(bf), columns)

    row = lax.broadcasted_iota(jnp.int32, (high, 1), 0)
    weight = jnp.where(row < LANES, scale / whole, 2.0 * scale / whole)
    short_cos, short_sin = cosine[:, :length] * weight, -(sine[:, :length] * weight)
    shorts = short_specs()

    def combine(s, spec):
        gains = own_ref[s * width : (s + 1) * width, length:] * (1.0 / scale)
        gains = jnp.concatenate([gains] * (cols // 128), axis=1)
        shift = jnp.concatenate(
            [gains[g * LANES : (g + 1) * LANES] for g in range(groups) for _ in range(copies)], axis=0
        )
        short = shorts[s * span : (s + 1) * span]
        lr, li = spec[:, :cols] + shift, spec[:, cols:]
        rr, ri = short[:, :cols], short[:, cols:]
        return lr * rr - li * ri, lr * ri + li * rr

    chunks = [chunk(s) for s in range(sections)]
    odd = 2 * width - width // 16 * 16
    longs = [jnp.concatenate([part[:, odd:], part[:, width:odd]], axis=1) for part in chunks]
    if odd == 2 * width:
        longs = [part[:, width:] for part in chunks]
    specs = forward([chunks[0][:, :width]] + longs)
    signal_spec = specs[:span]
    results = []
    for s in range(sections):
        mixed = combine(s, specs[(s + 1) * span : (s + 2) * span])
        result = back(times(signal_spec, mixed))
        results.append(result)
        if s + 1 < sections:
            rounded = result.astype(bf).astype(jnp.float32)
            signal_spec = forward([rounded * chunks[s + 1][:, :width]])
    for at in range(0, len(order), 2):
        pair = [results[rank // seq][rank % seq] for rank in order[at : at + 2]]
        out_ref[at * width : (at + 2) * width] = jnp.concatenate(pair, axis=0).astype(bf)


def body(activations, short_filters, long_filters, skip_gain):
    sections = short_filters.shape[0]
    tokens, channels = activations.shape[1:]
    devices = lax.axis_size(BOTH)
    seq_devices = lax.axis_size("seq")
    owned = channels // devices
    width = -(-owned // LANES) * LANES
    cols = tokens
    laid = devices * width
    order = spread_order(devices)

    def widen(array):
        split = array.reshape(array.shape[:2] + (devices, owned))
        split = jnp.pad(split, ((0, 0), (0, 0), (0, 0), (0, width - owned)))
        return split.reshape(array.shape[:2] + (laid,))

    def exchanged(array, height):
        chunks = array.reshape(devices, height, cols)
        moved = lax.all_to_all(
            chunks, BOTH, split_axis=0, concat_axis=0, tiled=True, axis_index_groups=[list(order)]
        )
        return moved.reshape(devices * height, cols)

    def grant(size):
        return pltpu.CompilerParams(vmem_limit_bytes=int(size))

    acts, filters = activations, long_filters
    if width != owned:
        acts, filters = widen(acts), widen(filters)
    split = 2 if seq_devices <= 32 and cols % 256 == 0 else 1
    table, turn = tables(seq_devices * split, cols // split, split)
    vmem = pl.BlockSpec(memory_space=pltpu.VMEM)
    hbm = pl.BlockSpec(memory_space=pltpu.HBM)
    area = laid * cols
    span = (seq_devices + 1) * width
    taps = short_filters.shape[1]
    place = lax.axis_index(BOTH).astype(jnp.int32).reshape(1)
    inputs = (acts, filters, short_filters, skip_gain)
    outgoing, own = pl.pallas_call(
        functools.partial(send_kernel, width, owned, order),
        out_shape=(
            jax.ShapeDtypeStruct((2 * laid, cols), jnp.bfloat16),
            jax.ShapeDtypeStruct((sections * width, taps + 128), jnp.float32),
        ),
        in_specs=[pl.BlockSpec(memory_space=pltpu.SMEM)] + [hbm] * 4,
        out_specs=(vmem, vmem),
        scratch_shapes=[
            pltpu.VMEM((cols, laid), jnp.bfloat16),
            pltpu.VMEM((cols, laid), jnp.float32),
            pltpu.VMEM(short_filters.shape, jnp.bfloat16),
            pltpu.VMEM(skip_gain.shape, jnp.float32),
            pltpu.SemaphoreType.DMA((2,)),
            pltpu.SemaphoreType.DMA((2,)),
        ],
        compiler_params=grant(4 * MIB + 24 * area),
    )(place, *(pltpu.with_memory_space_constraint(array, pltpu.HBM) for array in inputs))
    arrived = exchanged(outgoing, 2 * width)
    results = pl.pallas_call(
        functools.partial(main_kernel, width, sections, split, order),
        out_shape=jax.ShapeDtypeStruct((laid, cols), jnp.bfloat16),
        in_specs=[vmem] * 4,
        out_specs=vmem,
        compiler_params=grant(2 * MIB + 6 * area + 2 * table.size + 64 * span * cols),
    )(arrived, own, turn, table)
    returned = exchanged(results, width)
    final = pl.pallas_call(
        final_kernel,
        out_shape=jax.ShapeDtypeStruct((1, cols, laid), jnp.bfloat16),
        compiler_params=grant(4 * MIB + 16 * area),
    )(returned)
    if width != owned:
        final = final.reshape(1, cols, devices, width)[..., :owned].reshape(1, cols, channels)
    return final


def solution(mesh):
    return jax.shard_map(
        body,
        mesh=mesh,
        in_specs=(P("segment", "seq", None), P(), P("segment", "seq", None), P()),
        out_specs=P("segment", "seq", None),
        check_vma=False,
    )
```

```python
import functools
import math

import jax
import jax.numpy as jnp
import numpy as np
from jax import lax
from jax.experimental import pallas as pl
from jax.experimental.pallas import tpu as pltpu
from jax.sharding import PartitionSpec as P

BOTH = ("segment", "seq")
LANES = 8
MIB = 1024 * 1024


FIELDS = {2: 7, 3: 11, 4: 19, 5: 37, 6: 67, 7: 131, 8: 285, 9: 529, 10: 1033}


def spread_order(devices):
    bits = devices.bit_length() - 1
    if devices != 1 << bits or bits not in FIELDS:
        return tuple(range(devices))
    order, power = [0], 1
    while len(order) < devices:
        order.append(power)
        power <<= 1
        if power & devices:
            power ^= FIELDS[bits]
    return tuple(order)


def tables(real_rows, cols, split):
    grid_rows = 2 * real_rows + 1
    length = grid_rows * cols
    freqs = real_rows + 1
    k = np.arange(freqs)
    place = np.arange(real_rows).reshape(-1, split).T.reshape(-1)
    rows = 2.0 * math.pi * ((k[:, None] * place[None, :]) % grid_rows) / grid_rows
    first = np.stack([np.cos(rows), -np.sin(rows)]).reshape(2 * freqs, real_rows)
    row_part = np.kron(first, np.eye(LANES))
    b = np.arange(cols)
    angle = 2.0 * math.pi * (k[:, None] * b[None, :]) / length
    turn = np.concatenate([np.cos(angle), np.sin(angle)], axis=1)
    turn = np.pad(turn, ((0, -freqs % LANES), (0, 0)))
    grid = 2.0 * math.pi * ((b[:, None] * b[None, :]) % cols) / cols
    c, s = np.cos(grid), np.sin(grid)
    parts = [np.block([[c, -s], [s, c]]), row_part]
    lanes = max(part.shape[1] for part in parts)
    stacked = np.concatenate([np.pad(p, ((0, 0), (0, lanes - p.shape[1]))) for p in parts])
    back = np.kron(first.reshape(2, freqs, real_rows)[:, 1:].reshape(-1, real_rows).T, np.eye(LANES))
    bf = jnp.bfloat16
    return jnp.asarray(stacked, bf), jnp.asarray(back, bf), jnp.asarray(turn, jnp.float32)


def dot(a, b):
    return jnp.dot(a, b, preferred_element_type=jnp.float32)


def dot_rows(a, b):
    return lax.dot_general(a, b, (((1,), (1,)), ((), ())), preferred_element_type=jnp.float32)


def repeated(rows, count):
    return jnp.concatenate(
        [jnp.broadcast_to(rows[k : k + 1], (LANES, rows.shape[1])) for k in range(count)], axis=0
    )


def identity(size):
    down = lax.broadcasted_iota(jnp.int32, (size, size), 0)
    across = lax.broadcasted_iota(jnp.int32, (size, size), 1)
    return jnp.where(down == across, 1.0, 0.0).astype(jnp.bfloat16)


def send_kernel(
    width,
    owned,
    order,
    place_ref,
    act_ref,
    filt_ref,
    taps_ref,
    gain_ref,
    out_ref,
    own_ref,
    act_held,
    filt_held,
    taps_held,
    gain_held,
    in_sem,
    own_sem,
):
    sections, length, channels = taps_ref.shape
    mine_first = (
        pltpu.make_async_copy(taps_ref, taps_held, own_sem.at[0]),
        pltpu.make_async_copy(gain_ref, gain_held, own_sem.at[1]),
    )
    for copy in mine_first:
        copy.start()
    arriving = (
        pltpu.make_async_copy(act_ref.at[0], act_held, in_sem.at[0]),
        pltpu.make_async_copy(filt_ref.at[0], filt_held, in_sem.at[1]),
    )
    for copy in arriving:
        copy.start()
    size = 128
    eye = identity(size)
    mine = lax.broadcasted_iota(jnp.int32, (width, channels), 0)
    them = lax.broadcasted_iota(jnp.int32, (width, channels), 1)
    place = jnp.int32(0)
    for position, rank in enumerate(order):
        place = place + jnp.where(place_ref[0] == rank, position, 0)
    pick = jnp.where((them == mine + place * owned) & (mine < owned), 1.0, 0.0)
    for copy in mine_first:
        copy.wait()
    for s in range(sections):
        gain = jnp.sum(pick * gain_held[s : s + 1, :], axis=1, keepdims=True)
        own_ref[s * width : (s + 1) * width, :length] = dot_rows(pick.astype(jnp.bfloat16), taps_held[s])
        own_ref[s * width : (s + 1) * width, length:] = jnp.broadcast_to(gain, (width, 128))
    def across(copy, held):
        copy.wait()
        columns = [
            dot_rows(eye, held[:, start : start + size].astype(jnp.bfloat16))
            for start in range(0, held.shape[1], size)
        ]
        return jnp.concatenate(columns, axis=0)

    even = width // 16 * 16
    act = across(arriving[0], act_held)
    for d in range(len(order) if even else 0):
        start = d * width
        out_ref[2 * start : 2 * start + even] = act[start : start + even].astype(jnp.bfloat16)
    filt = across(arriving[1], filt_held)
    for d in range(len(order)):
        start, end = d * width, (d + 1) * width
        parts = [act[start + even : end], filt[start + even : end], filt[start : start + even]]
        rest = jnp.concatenate([part for part in parts if part.shape[0]], axis=0)
        out_ref[2 * start + even : 2 * end] = rest.astype(jnp.bfloat16)


def final_kernel(in_ref, out_ref):
    channels, tokens = in_ref.shape
    step = math.gcd(channels, 256)
    eye = identity(tokens)
    for start in range(0, channels, step):
        part = slice(start, start + step)
        out_ref[0, :, part] = dot_rows(eye, in_ref[part]).astype(jnp.bfloat16)


def main_kernel(width, sections, split, order, in_ref, own_ref, turn_ref, table_ref, back_ref, out_ref):
    total, tokens = in_ref.shape
    cols = tokens // split
    seq = total // (2 * width * sections)
    rows = seq * split
    groups = width // LANES
    high = (rows + 1) * LANES
    span = groups * high
    bf = jnp.bfloat16
    copies = rows + 1
    length = own_ref.shape[1] - 128
    scale = 1.0 / math.sqrt(rows * cols)
    whole = (2 * rows + 1) * cols
    turn = repeated(turn_ref[...], copies)
    cosine, sine = turn[:, :cols], turn[:, cols:]
    all_cos = jnp.concatenate([cosine] * groups, axis=0)
    all_sin = jnp.concatenate([sine] * groups, axis=0)
    forward_cols = table_ref[: 2 * cols, : 2 * cols]
    level, minus = table_ref[:cols, :cols], table_ref[:cols, cols : 2 * cols]
    plus = table_ref[cols : 2 * cols, :cols]
    back_cols = jnp.concatenate(
        [jnp.concatenate([level, plus], axis=1), jnp.concatenate([minus, level], axis=1)], axis=0
    )
    forward_rows = table_ref[2 * cols : 2 * cols + 2 * high, : rows * LANES]
    def chunk(s):
        starts = [order.index(s * seq + q) * 2 * width for q in range(seq)]
        part = jnp.concatenate([in_ref[at : at + 2 * width] for at in starts], axis=0)
        return part.astype(jnp.float32).reshape(seq, 2 * width, tokens)

    def forward(grids, others=()):
        blocks = []
        for grid in grids:
            for g in range(groups):
                part = grid[:, g * LANES : (g + 1) * LANES]
                parts = [part[:, :, h * cols : (h + 1) * cols] for h in range(split)]
                blocks.append(jnp.concatenate(parts, axis=0).reshape(rows * LANES, cols))
        spread = dot(forward_rows, jnp.concatenate(blocks, axis=1).astype(bf))
        turned = []
        for n in range(len(blocks)):
            lanes = slice(n * cols, (n + 1) * cols)
            real, imag = spread[:high, lanes], spread[high:, lanes]
            turned.append(
                jnp.concatenate([real * cosine + imag * sine, imag * cosine - real * sine], axis=1)
            )
        return dot(jnp.concatenate(turned + list(others), axis=0).astype(bf), forward_cols)

    def times(left, right):
        lr, li = left[:, :cols], left[:, cols:]
        rr, ri = right
        return jnp.concatenate([lr * rr - li * ri, lr * ri + li * rr], axis=1).astype(bf)

    def back(product):
        flat = dot(product, back_cols)
        real, imag = flat[:, :cols], flat[:, cols:]
        turned_real = real * all_cos - imag * all_sin
        turned_imag = real * all_sin + imag * all_cos
        joined = []
        for g in range(groups):
            part = slice(g * high + LANES, (g + 1) * high)
            joined.append(jnp.concatenate([turned_real[part], turned_imag[part]], axis=0))
        spread = dot(back_ref[...], jnp.concatenate(joined, axis=1).astype(bf))
        pieces = []
        for g in range(groups):
            piece = spread[:, g * cols : (g + 1) * cols].reshape(rows, LANES, cols)
            piece = piece + turned_real[g * high : g * high + LANES][None]
            parts = [piece[h * seq : (h + 1) * seq] for h in range(split)]
            pieces.append(jnp.concatenate(parts, axis=2))
        return jnp.concatenate(pieces, axis=1)

    def short_blocks():
        none = [jnp.zeros((high, cols - length), jnp.float32)] if cols > length else []
        turned = []
        for s in range(sections):
            for g in range(groups):
                start = s * width + g * LANES
                taps = jnp.concatenate([own_ref[start : start + LANES, :length]] * copies, axis=0)
                parts = [taps * short_cos] + none + [taps * short_sin] + none
                turned.append(jnp.concatenate(parts, axis=1))
        return turned

    row = lax.broadcasted_iota(jnp.int32, (high, 1), 0)
    weight = jnp.where(row < LANES, scale / whole, 2.0 * scale / whole)
    short_cos, short_sin = cosine[:, :length] * weight, -(sine[:, :length] * weight)

    def combine(s, spec):
        gains = own_ref[s * width : (s + 1) * width, length:] * (1.0 / scale)
        gains = jnp.concatenate([gains] * (cols // 128), axis=1)
        shift = jnp.concatenate(
            [gains[g * LANES : (g + 1) * LANES] for g in range(groups) for _ in range(copies)], axis=0
        )
        short = shorts[s * span : (s + 1) * span]
        lr, li = spec[:, :cols] + shift, spec[:, cols:]
        rr, ri = short[:, :cols], short[:, cols:]
        return lr * rr - li * ri, lr * ri + li * rr

    chunks = [chunk(s) for s in range(sections)]
    odd = 2 * width - width // 16 * 16
    longs = [jnp.concatenate([part[:, odd:], part[:, width:odd]], axis=1) for part in chunks]
    if odd == 2 * width:
        longs = [part[:, width:] for part in chunks]
    specs = forward([chunks[0][:, :width]] + longs, short_blocks())
    shorts = specs[(sections + 1) * span :]
    signal_spec = specs[:span]
    results = []
    for s in range(sections):
        mixed = combine(s, specs[(s + 1) * span : (s + 2) * span])
        result = back(times(signal_spec, mixed))
        results.append(result)
        if s + 1 < sections:
            rounded = result.astype(bf).astype(jnp.float32)
            signal_spec = forward([rounded * chunks[s + 1][:, :width]])
    for at in range(0, len(order), 2):
        pair = [results[rank // seq][rank % seq] for rank in order[at : at + 2]]
        out_ref[at * width : (at + 2) * width] = jnp.concatenate(pair, axis=0).astype(bf)


def body(activations, short_filters, long_filters, skip_gain):
    sections = short_filters.shape[0]
    tokens, channels = activations.shape[1:]
    devices = lax.axis_size(BOTH)
    seq_devices = lax.axis_size("seq")
    owned = channels // devices
    width = -(-owned // LANES) * LANES
    cols = tokens
    laid = devices * width
    order = spread_order(devices)

    def widen(array):
        split = array.reshape(array.shape[:2] + (devices, owned))
        split = jnp.pad(split, ((0, 0), (0, 0), (0, 0), (0, width - owned)))
        return split.reshape(array.shape[:2] + (laid,))

    def exchanged(array, height):
        chunks = array.reshape(devices, height, cols)
        moved = lax.all_to_all(
            chunks, BOTH, split_axis=0, concat_axis=0, tiled=True, axis_index_groups=[list(order)]
        )
        return moved.reshape(devices * height, cols)

    def grant(size):
        return pltpu.CompilerParams(vmem_limit_bytes=int(size))

    acts, filters = activations, long_filters
    if width != owned:
        acts, filters = widen(acts), widen(filters)
    split = 2 if seq_devices <= 32 and cols % 256 == 0 else 1
    table, back_table, turn = tables(seq_devices * split, cols // split, split)
    vmem = pl.BlockSpec(memory_space=pltpu.VMEM)
    hbm = pl.BlockSpec(memory_space=pltpu.HBM)
    area = laid * cols
    span = (seq_devices + 1) * width
    taps = short_filters.shape[1]
    place = lax.axis_index(BOTH).astype(jnp.int32).reshape(1)
    inputs = (acts, filters, short_filters, skip_gain)
    outgoing, own = pl.pallas_call(
        functools.partial(send_kernel, width, owned, order),
        out_shape=(
            jax.ShapeDtypeStruct((2 * laid, cols), jnp.bfloat16),
            jax.ShapeDtypeStruct((sections * width, taps + 128), jnp.float32),
        ),
        in_specs=[pl.BlockSpec(memory_space=pltpu.SMEM)] + [hbm] * 4,
        out_specs=(vmem, vmem),
        scratch_shapes=[
            pltpu.VMEM((cols, laid), jnp.bfloat16),
            pltpu.VMEM((cols, laid), jnp.float32),
            pltpu.VMEM(short_filters.shape, jnp.bfloat16),
            pltpu.VMEM(skip_gain.shape, jnp.float32),
            pltpu.SemaphoreType.DMA((2,)),
            pltpu.SemaphoreType.DMA((2,)),
        ],
        compiler_params=grant(4 * MIB + 24 * area),
    )(place, *(pltpu.with_memory_space_constraint(array, pltpu.HBM) for array in inputs))
    arrived = exchanged(outgoing, 2 * width)
    results = pl.pallas_call(
        functools.partial(main_kernel, width, sections, split, order),
        out_shape=jax.ShapeDtypeStruct((laid, cols), jnp.bfloat16),
        in_specs=[vmem] * 5,
        out_specs=vmem,
        compiler_params=grant(2 * MIB + 6 * area + 2 * table.size + 2 * back_table.size + 64 * span * cols),
    )(arrived, own, turn, table, back_table)
    returned = exchanged(results, width)
    final = pl.pallas_call(
        final_kernel,
        out_shape=jax.ShapeDtypeStruct((1, cols, laid), jnp.bfloat16),
        compiler_params=grant(4 * MIB + 16 * area),
    )(returned)
    if width != owned:
        final = final.reshape(1, cols, devices, width)[..., :owned].reshape(1, cols, channels)
    return final


def solution(mesh):
    return jax.shard_map(
        body,
        mesh=mesh,
        in_specs=(P("segment", "seq", None), P(), P("segment", "seq", None), P()),
        out_specs=P("segment", "seq", None),
        check_vma=False,
    )
```

```python
import functools
import math

import jax
import jax.numpy as jnp
import numpy as np
from jax import lax
from jax.experimental import pallas as pl
from jax.experimental.pallas import tpu as pltpu
from jax.sharding import PartitionSpec as P

BOTH = ("segment", "seq")
LANES = 8
MIB = 1024 * 1024


def spread_order(devices, seq_devices):
    half = seq_devices // 2
    along = [place // 2 + place % 2 * half for place in range(2 * half)]
    along += range(2 * half, seq_devices)
    return tuple(
        start + q for start in range(0, devices, seq_devices) for q in along
    )


def tables(real_rows, cols, split):
    grid_rows = 2 * real_rows + 1
    length = grid_rows * cols
    freqs = real_rows + 1
    k = np.arange(freqs)
    place = np.arange(real_rows).reshape(-1, split).T.reshape(-1)
    rows = 2.0 * math.pi * ((k[:, None] * place[None, :]) % grid_rows) / grid_rows
    first = np.stack([np.cos(rows), -np.sin(rows)]).reshape(2 * freqs, real_rows)
    row_part = np.kron(first, np.eye(LANES))
    b = np.arange(cols)
    angle = 2.0 * math.pi * (k[:, None] * b[None, :]) / length
    turn = np.concatenate([np.cos(angle), np.sin(angle)], axis=1)
    turn = np.pad(turn, ((0, -freqs % LANES), (0, 0)))
    grid = 2.0 * math.pi * ((b[:, None] * b[None, :]) % cols) / cols
    c, s = np.cos(grid), np.sin(grid)
    parts = [np.block([[c, -s], [s, c]]), row_part]
    lanes = max(part.shape[1] for part in parts)
    stacked = np.concatenate([np.pad(p, ((0, 0), (0, lanes - p.shape[1]))) for p in parts])
    back = np.kron(first.reshape(2, freqs, real_rows)[:, 1:].reshape(-1, real_rows).T, np.eye(LANES))
    bf = jnp.bfloat16
    return jnp.asarray(stacked, bf), jnp.asarray(back, bf), jnp.asarray(turn, jnp.float32)


def dot(a, b):
    return jnp.dot(a, b, preferred_element_type=jnp.float32)


def dot_rows(a, b):
    return lax.dot_general(a, b, (((1,), (1,)), ((), ())), preferred_element_type=jnp.float32)


def repeated(rows, count):
    return jnp.concatenate(
        [jnp.broadcast_to(rows[k : k + 1], (LANES, rows.shape[1])) for k in range(count)], axis=0
    )


def identity(size):
    down = lax.broadcasted_iota(jnp.int32, (size, size), 0)
    across = lax.broadcasted_iota(jnp.int32, (size, size), 1)
    return jnp.where(down == across, 1.0, 0.0).astype(jnp.bfloat16)


def send_kernel(
    width,
    owned,
    order,
    place_ref,
    act_ref,
    filt_ref,
    taps_ref,
    gain_ref,
    out_ref,
    own_ref,
    act_held,
    filt_held,
    taps_held,
    gain_held,
    in_sem,
    own_sem,
):
    sections, length, channels = taps_ref.shape
    mine_first = (
        pltpu.make_async_copy(taps_ref, taps_held, own_sem.at[0]),
        pltpu.make_async_copy(gain_ref, gain_held, own_sem.at[1]),
    )
    for copy in mine_first:
        copy.start()
    arriving = (
        pltpu.make_async_copy(act_ref.at[0], act_held, in_sem.at[0]),
        pltpu.make_async_copy(filt_ref.at[0], filt_held, in_sem.at[1]),
    )
    for copy in arriving:
        copy.start()
    size = 128
    eye = identity(size)
    mine = lax.broadcasted_iota(jnp.int32, (width, channels), 0)
    them = lax.broadcasted_iota(jnp.int32, (width, channels), 1)
    place = jnp.int32(0)
    for position, rank in enumerate(order):
        place = place + jnp.where(place_ref[0] == rank, position, 0)
    pick = jnp.where((them == mine + place * owned) & (mine < owned), 1.0, 0.0)
    for copy in mine_first:
        copy.wait()
    for s in range(sections):
        gain = jnp.sum(pick * gain_held[s : s + 1, :], axis=1, keepdims=True)
        own_ref[s * width : (s + 1) * width, :length] = dot_rows(pick.astype(jnp.bfloat16), taps_held[s])
        own_ref[s * width : (s + 1) * width, length:] = jnp.broadcast_to(gain, (width, 128))
    def across(copy, held):
        copy.wait()
        columns = [
            dot_rows(eye, held[:, start : start + size].astype(jnp.bfloat16))
            for start in range(0, held.shape[1], size)
        ]
        return jnp.concatenate(columns, axis=0)

    even = width // 16 * 16
    act = across(arriving[0], act_held)
    for d in range(len(order) if even else 0):
        start = d * width
        out_ref[2 * start : 2 * start + even] = act[start : start + even].astype(jnp.bfloat16)
    filt = across(arriving[1], filt_held)
    for d in range(len(order)):
        start, end = d * width, (d + 1) * width
        parts = [act[start + even : end], filt[start + even : end], filt[start : start + even]]
        rest = jnp.concatenate([part for part in parts if part.shape[0]], axis=0)
        out_ref[2 * start + even : 2 * end] = rest.astype(jnp.bfloat16)


def final_kernel(in_ref, out_ref):
    channels, tokens = in_ref.shape
    step = math.gcd(channels, 256)
    eye = identity(tokens)
    for start in range(0, channels, step):
        part = slice(start, start + step)
        out_ref[0, :, part] = dot_rows(eye, in_ref[part]).astype(jnp.bfloat16)


def main_kernel(width, sections, split, order, in_ref, own_ref, turn_ref, table_ref, back_ref, out_ref):
    total, tokens = in_ref.shape
    cols = tokens // split
    seq = total // (2 * width * sections)
    rows = seq * split
    groups = width // LANES
    high = (rows + 1) * LANES
    span = groups * high
    bf = jnp.bfloat16
    copies = rows + 1
    length = own_ref.shape[1] - 128
    scale = 1.0 / math.sqrt(rows * cols)
    whole = (2 * rows + 1) * cols
    turn = repeated(turn_ref[...], copies)
    cosine, sine = turn[:, :cols], turn[:, cols:]
    all_cos = jnp.concatenate([cosine] * groups, axis=0)
    all_sin = jnp.concatenate([sine] * groups, axis=0)
    forward_cols = table_ref[: 2 * cols, : 2 * cols]
    level, minus = table_ref[:cols, :cols], table_ref[:cols, cols : 2 * cols]
    plus = table_ref[cols : 2 * cols, :cols]
    back_cols = jnp.concatenate(
        [jnp.concatenate([level, plus], axis=1), jnp.concatenate([minus, level], axis=1)], axis=0
    )
    forward_rows = table_ref[2 * cols : 2 * cols + 2 * high, : rows * LANES]
    def chunk(s):
        starts = [order.index(s * seq + q) * 2 * width for q in range(seq)]
        part = jnp.concatenate([in_ref[at : at + 2 * width] for at in starts], axis=0)
        return part.astype(jnp.float32).reshape(seq, 2 * width, tokens)

    def forward(grids):
        blocks = []
        for grid in grids:
            for g in range(groups):
                part = grid[:, g * LANES : (g + 1) * LANES]
                parts = [part[:, :, h * cols : (h + 1) * cols] for h in range(split)]
                blocks.append(jnp.concatenate(parts, axis=0).reshape(rows * LANES, cols))
        spread = dot(forward_rows, jnp.concatenate(blocks, axis=1).astype(bf))
        turned = []
        for n in range(len(blocks)):
            lanes = slice(n * cols, (n + 1) * cols)
            real, imag = spread[:high, lanes], spread[high:, lanes]
            turned.append(
                jnp.concatenate([real * cosine + imag * sine, imag * cosine - real * sine], axis=1)
            )
        return dot(jnp.concatenate(turned, axis=0).astype(bf), forward_cols)

    def times(left, right):
        lr, li = left[:, :cols], left[:, cols:]
        rr, ri = right
        return jnp.concatenate([lr * rr - li * ri, lr * ri + li * rr], axis=1).astype(bf)

    def back(product):
        flat = dot(product, back_cols)
        real, imag = flat[:, :cols], flat[:, cols:]
        turned_real = real * all_cos - imag * all_sin
        turned_imag = real * all_sin + imag * all_cos
        joined = []
        for g in range(groups):
            part = slice(g * high + LANES, (g + 1) * high)
            joined.append(jnp.concatenate([turned_real[part], turned_imag[part]], axis=0))
        spread = dot(back_ref[...], jnp.concatenate(joined, axis=1).astype(bf))
        pieces = []
        for g in range(groups):
            piece = spread[:, g * cols : (g + 1) * cols].reshape(rows, LANES, cols)
            piece = piece + turned_real[g * high : g * high + LANES][None]
            parts = [piece[h * seq : (h + 1) * seq] for h in range(split)]
            pieces.append(jnp.concatenate(parts, axis=2))
        return jnp.concatenate(pieces, axis=1)

    def short_specs():
        turned = []
        for s in range(sections):
            for g in range(groups):
                start = s * width + g * LANES
                taps = jnp.concatenate([own_ref[start : start + LANES, :length]] * copies, axis=0)
                turned.append(
                    jnp.concatenate([taps * short_cos, taps * short_sin], axis=1)
                )
        columns = jnp.concatenate([table_ref[:length, : 2 * cols], table_ref[cols : cols + length, : 2 * cols]])
        return dot(jnp.concatenate(turned, axis=0).astype(bf), columns)

    row = lax.broadcasted_iota(jnp.int32, (high, 1), 0)
    weight = jnp.where(row < LANES, scale / whole, 2.0 * scale / whole)
    short_cos, short_sin = cosine[:, :length] * weight, -(sine[:, :length] * weight)
    shorts = short_specs()

    def combine(s, spec):
        gains = own_ref[s * width : (s + 1) * width, length:] * (1.0 / scale)
        gains = jnp.concatenate([gains] * (cols // 128), axis=1)
        shift = jnp.concatenate(
            [gains[g * LANES : (g + 1) * LANES] for g in range(groups) for _ in range(copies)], axis=0
        )
        short = shorts[s * span : (s + 1) * span]
        lr, li = spec[:, :cols] + shift, spec[:, cols:]
        rr, ri = short[:, :cols], short[:, cols:]
        return lr * rr - li * ri, lr * ri + li * rr

    chunks = [chunk(s) for s in range(sections)]
    odd = 2 * width - width // 16 * 16
    longs = [jnp.concatenate([part[:, odd:], part[:, width:odd]], axis=1) for part in chunks]
    if odd == 2 * width:
        longs = [part[:, width:] for part in chunks]
    specs = forward([chunks[0][:, :width]] + longs)
    signal_spec = specs[:span]
    results = []
    for s in range(sections):
        mixed = combine(s, specs[(s + 1) * span : (s + 2) * span])
        result = back(times(signal_spec, mixed))
        results.append(result)
        if s + 1 < sections:
            rounded = result.astype(bf).astype(jnp.float32)
            signal_spec = forward([rounded * chunks[s + 1][:, :width]])
    for at in range(0, len(order), 2):
        pair = [results[rank // seq][rank % seq] for rank in order[at : at + 2]]
        out_ref[at * width : (at + 2) * width] = jnp.concatenate(pair, axis=0).astype(bf)


def body(activations, short_filters, long_filters, skip_gain):
    sections = short_filters.shape[0]
    tokens, channels = activations.shape[1:]
    devices = lax.axis_size(BOTH)
    seq_devices = lax.axis_size("seq")
    owned = channels // devices
    width = -(-owned // LANES) * LANES
    cols = tokens
    laid = devices * width
    order = spread_order(devices, seq_devices)

    def widen(array):
        split = array.reshape(array.shape[:2] + (devices, owned))
        split = jnp.pad(split, ((0, 0), (0, 0), (0, 0), (0, width - owned)))
        return split.reshape(array.shape[:2] + (laid,))

    def exchanged(array, height):
        chunks = array.reshape(devices, height, cols)
        moved = lax.all_to_all(
            chunks, BOTH, split_axis=0, concat_axis=0, tiled=True, axis_index_groups=[list(order)]
        )
        return moved.reshape(devices * height, cols)

    def grant(size):
        return pltpu.CompilerParams(vmem_limit_bytes=int(size))

    acts, filters = activations, long_filters
    if width != owned:
        acts, filters = widen(acts), widen(filters)
    split = 2 if seq_devices <= 32 and cols % 256 == 0 else 1
    table, back_table, turn = tables(seq_devices * split, cols // split, split)
    vmem = pl.BlockSpec(memory_space=pltpu.VMEM)
    hbm = pl.BlockSpec(memory_space=pltpu.HBM)
    area = laid * cols
    span = (seq_devices + 1) * width
    taps = short_filters.shape[1]
    place = lax.axis_index(BOTH).astype(jnp.int32).reshape(1)
    inputs = (acts, filters, short_filters, skip_gain)
    outgoing, own = pl.pallas_call(
        functools.partial(send_kernel, width, owned, order),
        out_shape=(
            jax.ShapeDtypeStruct((2 * laid, cols), jnp.bfloat16),
            jax.ShapeDtypeStruct((sections * width, taps + 128), jnp.float32),
        ),
        in_specs=[pl.BlockSpec(memory_space=pltpu.SMEM)] + [hbm] * 4,
        out_specs=(vmem, vmem),
        scratch_shapes=[
            pltpu.VMEM((cols, laid), jnp.bfloat16),
            pltpu.VMEM((cols, laid), jnp.float32),
            pltpu.VMEM(short_filters.shape, jnp.bfloat16),
            pltpu.VMEM(skip_gain.shape, jnp.float32),
            pltpu.SemaphoreType.DMA((2,)),
            pltpu.SemaphoreType.DMA((2,)),
        ],
        compiler_params=grant(4 * MIB + 24 * area),
    )(place, *(pltpu.with_memory_space_constraint(array, pltpu.HBM) for array in inputs))
    arrived = exchanged(outgoing, 2 * width)
    results = pl.pallas_call(
        functools.partial(main_kernel, width, sections, split, order),
        out_shape=jax.ShapeDtypeStruct((laid, cols), jnp.bfloat16),
        in_specs=[vmem] * 5,
        out_specs=vmem,
        compiler_params=grant(2 * MIB + 6 * area + 2 * table.size + 2 * back_table.size + 64 * span * cols),
    )(arrived, own, turn, table, back_table)
    returned = exchanged(results, width)
    final = pl.pallas_call(
        final_kernel,
        out_shape=jax.ShapeDtypeStruct((1, cols, laid), jnp.bfloat16),
        compiler_params=grant(4 * MIB + 16 * area),
    )(returned)
    if width != owned:
        final = final.reshape(1, cols, devices, width)[..., :owned].reshape(1, cols, channels)
    return final


def solution(mesh):
    return jax.shard_map(
        body,
        mesh=mesh,
        in_specs=(P("segment", "seq", None), P(), P("segment", "seq", None), P()),
        out_specs=P("segment", "seq", None),
        check_vma=False,
    )
```

```python
import functools
import math

import jax
import jax.numpy as jnp
import numpy as np
from jax import lax
from jax.experimental import pallas as pl
from jax.experimental.pallas import tpu as pltpu
from jax.sharding import PartitionSpec as P

BOTH = ("segment", "seq")
LANES = 8
MIB = 1024 * 1024


def spread_order(devices, seq_devices):
    half = seq_devices // 2
    along = [place // 2 + place % 2 * half for place in range(2 * half)]
    along += range(2 * half, seq_devices)
    return tuple(
        start + q for start in range(0, devices, seq_devices) for q in along
    )


def tables(real_rows, cols, split):
    grid_rows = 2 * real_rows + 1
    length = grid_rows * cols
    freqs = real_rows + 1
    k = np.arange(freqs)
    place = np.arange(real_rows).reshape(-1, split).T.reshape(-1)
    rows = 2.0 * math.pi * ((k[:, None] * place[None, :]) % grid_rows) / grid_rows
    first = np.stack([np.cos(rows), -np.sin(rows)]).reshape(2 * freqs, real_rows)
    row_part = np.kron(first, np.eye(LANES))
    b = np.arange(cols)
    angle = 2.0 * math.pi * (k[:, None] * b[None, :]) / length
    turn = np.concatenate([np.cos(angle), np.sin(angle)], axis=1)
    turn = np.pad(turn, ((0, -freqs % LANES), (0, 0)))
    grid = 2.0 * math.pi * ((b[:, None] * b[None, :]) % cols) / cols
    c, s = np.cos(grid), np.sin(grid)
    parts = [np.block([[c, -s], [s, c]]), row_part]
    lanes = max(part.shape[1] for part in parts)
    stacked = np.concatenate([np.pad(p, ((0, 0), (0, lanes - p.shape[1]))) for p in parts])
    back = np.kron(first.reshape(2, freqs, real_rows)[:, 1:].reshape(-1, real_rows).T, np.eye(LANES))
    bf = jnp.bfloat16
    return jnp.asarray(stacked, bf), jnp.asarray(back, bf), jnp.asarray(turn, jnp.float32)


def dot(a, b):
    return jnp.dot(a, b, preferred_element_type=jnp.float32)


def dot_rows(a, b):
    return lax.dot_general(a, b, (((1,), (1,)), ((), ())), preferred_element_type=jnp.float32)


def repeated(rows, count):
    return jnp.concatenate(
        [jnp.broadcast_to(rows[k : k + 1], (LANES, rows.shape[1])) for k in range(count)], axis=0
    )


def identity(size):
    down = lax.broadcasted_iota(jnp.int32, (size, size), 0)
    across = lax.broadcasted_iota(jnp.int32, (size, size), 1)
    return jnp.where(down == across, 1.0, 0.0).astype(jnp.bfloat16)


def send_kernel(
    width,
    owned,
    order,
    place_ref,
    act_ref,
    filt_ref,
    taps_ref,
    gain_ref,
    out_ref,
    own_ref,
    act_held,
    filt_held,
    taps_held,
    gain_held,
    in_sem,
    own_sem,
):
    sections, length, channels = taps_ref.shape
    mine_first = (
        pltpu.make_async_copy(taps_ref, taps_held, own_sem.at[0]),
        pltpu.make_async_copy(gain_ref, gain_held, own_sem.at[1]),
    )
    for copy in mine_first:
        copy.start()
    arriving = (
        pltpu.make_async_copy(act_ref.at[0], act_held, in_sem.at[0]),
        pltpu.make_async_copy(filt_ref.at[0], filt_held, in_sem.at[1]),
    )
    for copy in arriving:
        copy.start()
    size = 128
    eye = identity(size)
    mine = lax.broadcasted_iota(jnp.int32, (width, channels), 0)
    them = lax.broadcasted_iota(jnp.int32, (width, channels), 1)
    place = jnp.int32(0)
    for position, rank in enumerate(order):
        place = place + jnp.where(place_ref[0] == rank, position, 0)
    pick = jnp.where((them == mine + place * owned) & (mine < owned), 1.0, 0.0)
    for copy in mine_first:
        copy.wait()
    for s in range(sections):
        gain = jnp.sum(pick * gain_held[s : s + 1, :], axis=1, keepdims=True)
        own_ref[s * width : (s + 1) * width, :length] = dot_rows(pick.astype(jnp.bfloat16), taps_held[s])
        own_ref[s * width : (s + 1) * width, length:] = jnp.broadcast_to(gain, (width, 128))
    def across(copy, held):
        copy.wait()
        columns = [
            dot_rows(eye, held[:, start : start + size].astype(jnp.bfloat16))
            for start in range(0, held.shape[1], size)
        ]
        return jnp.concatenate(columns, axis=0)

    even = width // 16 * 16
    act = across(arriving[0], act_held)
    for d in range(len(order) if even else 0):
        start = d * width
        out_ref[2 * start : 2 * start + even] = act[start : start + even].astype(jnp.bfloat16)
    filt = across(arriving[1], filt_held)
    for d in range(len(order)):
        start, end = d * width, (d + 1) * width
        parts = [act[start + even : end], filt[start + even : end], filt[start : start + even]]
        rest = jnp.concatenate([part for part in parts if part.shape[0]], axis=0)
        out_ref[2 * start + even : 2 * end] = rest.astype(jnp.bfloat16)


def final_kernel(in_ref, out_ref):
    channels, tokens = in_ref.shape
    step = math.gcd(channels, 256)
    eye = identity(tokens)
    for start in range(0, channels, step):
        part = slice(start, start + step)
        out_ref[0, :, part] = dot_rows(eye, in_ref[part]).astype(jnp.bfloat16)


def main_kernel(width, sections, split, order, in_ref, own_ref, turn_ref, table_ref, back_ref, out_ref):
    total, tokens = in_ref.shape
    cols = tokens // split
    seq = total // (2 * width * sections)
    rows = seq * split
    groups = width // LANES
    high = (rows + 1) * LANES
    span = groups * high
    bf = jnp.bfloat16
    copies = rows + 1
    length = own_ref.shape[1] - 128
    scale = 1.0 / math.sqrt(rows * cols)
    whole = (2 * rows + 1) * cols
    turn = repeated(turn_ref[...], copies)
    cosine, sine = turn[:, :cols], turn[:, cols:]
    all_cos = jnp.concatenate([cosine] * groups, axis=0)
    all_sin = jnp.concatenate([sine] * groups, axis=0)
    forward_cols = table_ref[: 2 * cols, : 2 * cols]
    level, minus = table_ref[:cols, :cols], table_ref[:cols, cols : 2 * cols]
    plus = table_ref[cols : 2 * cols, :cols]
    back_cols = jnp.concatenate(
        [jnp.concatenate([level, plus], axis=1), jnp.concatenate([minus, level], axis=1)], axis=0
    )
    forward_rows = table_ref[2 * cols : 2 * cols + 2 * high, : rows * LANES]
    def chunk(s):
        starts = [order.index(s * seq + q) * 2 * width for q in range(seq)]
        part = jnp.concatenate([in_ref[at : at + 2 * width] for at in starts], axis=0)
        return part.astype(jnp.float32).reshape(seq, 2 * width, tokens)

    def forward(grids):
        blocks = []
        for grid in grids:
            for g in range(groups):
                part = grid[:, g * LANES : (g + 1) * LANES]
                parts = [part[:, :, h * cols : (h + 1) * cols] for h in range(split)]
                blocks.append(jnp.concatenate(parts, axis=0).reshape(rows * LANES, cols))
        spread = dot(forward_rows, jnp.concatenate(blocks, axis=1).astype(bf))
        turned = []
        for n in range(len(blocks)):
            lanes = slice(n * cols, (n + 1) * cols)
            real, imag = spread[:high, lanes], spread[high:, lanes]
            turned.append(
                jnp.concatenate([real * cosine + imag * sine, imag * cosine - real * sine], axis=1)
            )
        return dot(jnp.concatenate(turned, axis=0).astype(bf), forward_cols)

    def times(left, right):
        lr, li = left[:, :cols], left[:, cols:]
        rr, ri = right
        return jnp.concatenate([lr * rr - li * ri, lr * ri + li * rr], axis=1).astype(bf)

    def back(product):
        flat = dot(product, back_cols)
        real, imag = flat[:, :cols], flat[:, cols:]
        turned_real = real * all_cos - imag * all_sin
        turned_imag = real * all_sin + imag * all_cos
        joined = []
        for g in range(groups):
            part = slice(g * high + LANES, (g + 1) * high)
            joined.append(jnp.concatenate([turned_real[part], turned_imag[part]], axis=0))
        spread = dot(back_ref[...], jnp.concatenate(joined, axis=1).astype(bf))
        pieces = []
        for g in range(groups):
            piece = spread[:, g * cols : (g + 1) * cols].reshape(rows, LANES, cols)
            piece = piece + turned_real[g * high : g * high + LANES][None]
            parts = [piece[h * seq : (h + 1) * seq] for h in range(split)]
            pieces.append(jnp.concatenate(parts, axis=2))
        return jnp.concatenate(pieces, axis=1)

    def short_spec(s):
        turned = []
        for g in range(groups):
            start = s * width + g * LANES
            taps = jnp.concatenate([own_ref[start : start + LANES, :length]] * copies, axis=0)
            turned.append(jnp.concatenate([taps * short_cos, taps * short_sin], axis=1))
        columns = jnp.concatenate([table_ref[:length, : 2 * cols], table_ref[cols : cols + length, : 2 * cols]])
        return dot(jnp.concatenate(turned, axis=0).astype(bf), columns)

    row = lax.broadcasted_iota(jnp.int32, (high, 1), 0)
    weight = jnp.where(row < LANES, scale / whole, 2.0 * scale / whole)
    short_cos, short_sin = cosine[:, :length] * weight, -(sine[:, :length] * weight)

    def combine(s, short, spec):
        gains = own_ref[s * width : (s + 1) * width, length:] * (1.0 / scale)
        gains = jnp.concatenate([gains] * (cols // 128), axis=1)
        shift = jnp.concatenate(
            [gains[g * LANES : (g + 1) * LANES] for g in range(groups) for _ in range(copies)], axis=0
        )
        lr, li = spec[:, :cols] + shift, spec[:, cols:]
        rr, ri = short[:, :cols], short[:, cols:]
        return lr * rr - li * ri, lr * ri + li * rr

    chunks = [chunk(s) for s in range(sections)]
    odd = 2 * width - width // 16 * 16
    longs = [jnp.concatenate([part[:, odd:], part[:, width:odd]], axis=1) for part in chunks]
    if odd == 2 * width:
        longs = [part[:, width:] for part in chunks]
    specs = forward([chunks[0][:, :width], longs[0]])
    signal_spec = specs[:span]
    filters = combine(0, short_spec(0), specs[span:])
    results = []
    for s in range(sections):
        product = times(signal_spec, filters)
        if s + 1 < sections:
            filters = combine(s + 1, short_spec(s + 1), forward([longs[s + 1]]))
        result = back(product)
        results.append(result)
        if s + 1 < sections:
            rounded = result.astype(bf).astype(jnp.float32)
            signal_spec = forward([rounded * chunks[s + 1][:, :width]])
    for at in range(0, len(order), 2):
        pair = [results[rank // seq][rank % seq] for rank in order[at : at + 2]]
        out_ref[at * width : (at + 2) * width] = jnp.concatenate(pair, axis=0).astype(bf)


def body(activations, short_filters, long_filters, skip_gain):
    sections = short_filters.shape[0]
    tokens, channels = activations.shape[1:]
    devices = lax.axis_size(BOTH)
    seq_devices = lax.axis_size("seq")
    owned = channels // devices
    width = -(-owned // LANES) * LANES
    cols = tokens
    laid = devices * width
    order = spread_order(devices, seq_devices)

    def widen(array):
        split = array.reshape(array.shape[:2] + (devices, owned))
        split = jnp.pad(split, ((0, 0), (0, 0), (0, 0), (0, width - owned)))
        return split.reshape(array.shape[:2] + (laid,))

    def exchanged(array, height):
        chunks = array.reshape(devices, height, cols)
        moved = lax.all_to_all(
            chunks, BOTH, split_axis=0, concat_axis=0, tiled=True, axis_index_groups=[list(order)]
        )
        return moved.reshape(devices * height, cols)

    def grant(size):
        return pltpu.CompilerParams(vmem_limit_bytes=int(size))

    acts, filters = activations, long_filters
    if width != owned:
        acts, filters = widen(acts), widen(filters)
    split = 2 if seq_devices <= 32 and cols % 256 == 0 else 1
    table, back_table, turn = tables(seq_devices * split, cols // split, split)
    vmem = pl.BlockSpec(memory_space=pltpu.VMEM)
    hbm = pl.BlockSpec(memory_space=pltpu.HBM)
    area = laid * cols
    span = (seq_devices + 1) * width
    taps = short_filters.shape[1]
    place = lax.axis_index(BOTH).astype(jnp.int32).reshape(1)
    inputs = (acts, filters, short_filters, skip_gain)
    outgoing, own = pl.pallas_call(
        functools.partial(send_kernel, width, owned, order),
        out_shape=(
            jax.ShapeDtypeStruct((2 * laid, cols), jnp.bfloat16),
            jax.ShapeDtypeStruct((sections * width, taps + 128), jnp.float32),
        ),
        in_specs=[pl.BlockSpec(memory_space=pltpu.SMEM)] + [hbm] * 4,
        out_specs=(vmem, vmem),
        scratch_shapes=[
            pltpu.VMEM((cols, laid), jnp.bfloat16),
            pltpu.VMEM((cols, laid), jnp.float32),
            pltpu.VMEM(short_filters.shape, jnp.bfloat16),
            pltpu.VMEM(skip_gain.shape, jnp.float32),
            pltpu.SemaphoreType.DMA((2,)),
            pltpu.SemaphoreType.DMA((2,)),
        ],
        compiler_params=grant(4 * MIB + 24 * area),
    )(place, *(pltpu.with_memory_space_constraint(array, pltpu.HBM) for array in inputs))
    arrived = exchanged(outgoing, 2 * width)
    results = pl.pallas_call(
        functools.partial(main_kernel, width, sections, split, order),
        out_shape=jax.ShapeDtypeStruct((laid, cols), jnp.bfloat16),
        in_specs=[vmem] * 5,
        out_specs=vmem,
        compiler_params=grant(2 * MIB + 6 * area + 2 * table.size + 2 * back_table.size + 64 * span * cols),
    )(arrived, own, turn, table, back_table)
    returned = exchanged(results, width)
    final = pl.pallas_call(
        final_kernel,
        out_shape=jax.ShapeDtypeStruct((1, cols, laid), jnp.bfloat16),
        compiler_params=grant(4 * MIB + 16 * area),
    )(returned)
    if width != owned:
        final = final.reshape(1, cols, devices, width)[..., :owned].reshape(1, cols, channels)
    return final


def solution(mesh):
    return jax.shard_map(
        body,
        mesh=mesh,
        in_specs=(P("segment", "seq", None), P(), P("segment", "seq", None), P()),
        out_specs=P("segment", "seq", None),
        check_vma=False,
    )
```

```python
import functools
import math

import jax
import jax.numpy as jnp
import numpy as np
from jax import lax
from jax.experimental import pallas as pl
from jax.experimental.pallas import tpu as pltpu
from jax.sharding import PartitionSpec as P

BOTH = ("segment", "seq")
LANES = 8
MIB = 1024 * 1024


def spread_order(devices, seq_devices):
    half = seq_devices // 2
    along = [place // 2 + place % 2 * half for place in range(2 * half)]
    along += range(2 * half, seq_devices)
    return tuple(
        start + q for start in range(0, devices, seq_devices) for q in along
    )


def tables(real_rows, cols, split):
    grid_rows = 2 * real_rows + 1
    length = grid_rows * cols
    freqs = real_rows + 1
    k = np.arange(freqs)
    place = np.arange(real_rows).reshape(-1, split).T.reshape(-1)
    rows = 2.0 * math.pi * ((k[:, None] * place[None, :]) % grid_rows) / grid_rows
    first = np.stack([np.cos(rows), -np.sin(rows)]).reshape(2 * freqs, real_rows)
    row_part = np.kron(first, np.eye(LANES))
    b = np.arange(cols)
    angle = 2.0 * math.pi * (k[:, None] * b[None, :]) / length
    turn = np.concatenate([np.cos(angle), np.sin(angle)], axis=1)
    turn = np.pad(turn, ((0, -freqs % LANES), (0, 0)))
    grid = 2.0 * math.pi * ((b[:, None] * b[None, :]) % cols) / cols
    c, s = np.cos(grid), np.sin(grid)
    parts = [np.block([[c, -s], [s, c]]), row_part]
    lanes = max(part.shape[1] for part in parts)
    stacked = np.concatenate([np.pad(p, ((0, 0), (0, lanes - p.shape[1]))) for p in parts])
    back = np.kron(first.reshape(2, freqs, real_rows)[:, 1:].reshape(-1, real_rows).T, np.eye(LANES))
    bf = jnp.bfloat16
    return jnp.asarray(stacked, bf), jnp.asarray(back, bf), jnp.asarray(turn, jnp.float32)


def dot(a, b):
    return jnp.dot(a, b, preferred_element_type=jnp.float32)


def dot_rows(a, b):
    return lax.dot_general(a, b, (((1,), (1,)), ((), ())), preferred_element_type=jnp.float32)


def repeated(rows, count):
    return jnp.concatenate(
        [jnp.broadcast_to(rows[k : k + 1], (LANES, rows.shape[1])) for k in range(count)], axis=0
    )


def identity(size):
    down = lax.broadcasted_iota(jnp.int32, (size, size), 0)
    across = lax.broadcasted_iota(jnp.int32, (size, size), 1)
    return jnp.where(down == across, 1.0, 0.0).astype(jnp.bfloat16)


def send_kernel(
    width,
    owned,
    order,
    place_ref,
    act_ref,
    filt_ref,
    taps_ref,
    gain_ref,
    out_ref,
    own_ref,
    act_held,
    filt_held,
    taps_held,
    gain_held,
    in_sem,
    own_sem,
):
    sections, length, channels = taps_ref.shape
    mine_first = (
        pltpu.make_async_copy(taps_ref, taps_held, own_sem.at[0]),
        pltpu.make_async_copy(gain_ref, gain_held, own_sem.at[1]),
    )
    for copy in mine_first:
        copy.start()
    arriving = (
        pltpu.make_async_copy(act_ref.at[0], act_held, in_sem.at[0]),
        pltpu.make_async_copy(filt_ref.at[0], filt_held, in_sem.at[1]),
    )
    for copy in arriving:
        copy.start()
    size = 128
    eye = identity(size)
    mine = lax.broadcasted_iota(jnp.int32, (width, channels), 0)
    them = lax.broadcasted_iota(jnp.int32, (width, channels), 1)
    place = jnp.int32(0)
    for position, rank in enumerate(order):
        place = place + jnp.where(place_ref[0] == rank, position, 0)
    pick = jnp.where((them == mine + place * owned) & (mine < owned), 1.0, 0.0)
    for copy in mine_first:
        copy.wait()
    for s in range(sections):
        gain = jnp.sum(pick * gain_held[s : s + 1, :], axis=1, keepdims=True)
        own_ref[s * width : (s + 1) * width, :length] = dot_rows(pick.astype(jnp.bfloat16), taps_held[s])
        own_ref[s * width : (s + 1) * width, length:] = jnp.broadcast_to(gain, (width, 128))
    def across(copy, held):
        copy.wait()
        columns = [
            dot_rows(eye, held[:, start : start + size].astype(jnp.bfloat16))
            for start in range(0, held.shape[1], size)
        ]
        return jnp.concatenate(columns, axis=0)

    even = width // 16 * 16
    act = across(arriving[0], act_held)
    for d in range(len(order) if even else 0):
        start = d * width
        out_ref[2 * start : 2 * start + even] = act[start : start + even].astype(jnp.bfloat16)
    filt = across(arriving[1], filt_held)
    for d in range(len(order)):
        start, end = d * width, (d + 1) * width
        parts = [act[start + even : end], filt[start + even : end], filt[start : start + even]]
        rest = jnp.concatenate([part for part in parts if part.shape[0]], axis=0)
        out_ref[2 * start + even : 2 * end] = rest.astype(jnp.bfloat16)


def final_kernel(in_ref, out_ref):
    channels, tokens = in_ref.shape
    step = math.gcd(channels, 256)
    eye = identity(tokens)
    for start in range(0, channels, step):
        part = slice(start, start + step)
        out_ref[0, :, part] = dot_rows(eye, in_ref[part]).astype(jnp.bfloat16)


def main_kernel(width, sections, split, order, in_ref, own_ref, turn_ref, table_ref, back_ref, out_ref):
    total, tokens = in_ref.shape
    cols = tokens // split
    seq = total // (2 * width * sections)
    rows = seq * split
    groups = width // LANES
    high = (rows + 1) * LANES
    span = groups * high
    bf = jnp.bfloat16
    copies = rows + 1
    length = own_ref.shape[1] - 128
    scale = 1.0 / math.sqrt(rows * cols)
    whole = (2 * rows + 1) * cols
    turn = repeated(turn_ref[...], copies)
    cosine, sine = turn[:, :cols], turn[:, cols:]
    all_cos = jnp.concatenate([cosine] * groups, axis=0)
    all_sin = jnp.concatenate([sine] * groups, axis=0)
    forward_cols = table_ref[: 2 * cols, : 2 * cols]
    level, minus = table_ref[:cols, :cols], table_ref[:cols, cols : 2 * cols]
    plus = table_ref[cols : 2 * cols, :cols]
    back_cols = jnp.concatenate(
        [jnp.concatenate([level, plus], axis=1), jnp.concatenate([minus, level], axis=1)], axis=0
    )
    forward_rows = table_ref[2 * cols : 2 * cols + 2 * high, : rows * LANES]
    def chunk(s):
        starts = [order.index(s * seq + q) * 2 * width for q in range(seq)]
        part = jnp.concatenate([in_ref[at : at + 2 * width] for at in starts], axis=0)
        return part.astype(jnp.float32).reshape(seq, 2 * width, tokens)

    def forward(grids):
        blocks = []
        for grid in grids:
            for g in range(groups):
                part = grid[:, g * LANES : (g + 1) * LANES]
                parts = [part[:, :, h * cols : (h + 1) * cols] for h in range(split)]
                blocks.append(jnp.concatenate(parts, axis=0).reshape(rows * LANES, cols))
        spread = dot(forward_rows, jnp.concatenate(blocks, axis=1).astype(bf))
        turned = []
        for n in range(len(blocks)):
            lanes = slice(n * cols, (n + 1) * cols)
            real, imag = spread[:high, lanes], spread[high:, lanes]
            turned.append(
                jnp.concatenate([real * cosine + imag * sine, imag * cosine - real * sine], axis=1)
            )
        return dot(jnp.concatenate(turned, axis=0).astype(bf), forward_cols)

    def times(left, right):
        lr, li = left[:, :cols], left[:, cols:]
        rr, ri = right
        return jnp.concatenate([lr * rr - li * ri, lr * ri + li * rr], axis=1).astype(bf)

    def back(product):
        flat = dot(product, back_cols)
        real, imag = flat[:, :cols], flat[:, cols:]
        turned_real = real * all_cos - imag * all_sin
        turned_imag = real * all_sin + imag * all_cos
        joined = []
        for g in range(groups):
            part = slice(g * high + LANES, (g + 1) * high)
            joined.append(jnp.concatenate([turned_real[part], turned_imag[part]], axis=0))
        spread = dot(back_ref[...], jnp.concatenate(joined, axis=1).astype(bf))
        pieces = []
        for g in range(groups):
            piece = spread[:, g * cols : (g + 1) * cols].reshape(rows, LANES, cols)
            piece = piece + turned_real[g * high : g * high + LANES][None]
            parts = [piece[h * seq : (h + 1) * seq] for h in range(split)]
            pieces.append(jnp.concatenate(parts, axis=2))
        return jnp.concatenate(pieces, axis=1)

    def short_spec(s):
        turned = []
        for g in range(groups):
            start = s * width + g * LANES
            taps = jnp.concatenate([own_ref[start : start + LANES, :length]] * copies, axis=0)
            turned.append(jnp.concatenate([taps * short_cos, taps * short_sin], axis=1))
        columns = jnp.concatenate([table_ref[:length, : 2 * cols], table_ref[cols : cols + length, : 2 * cols]])
        return dot(jnp.concatenate(turned, axis=0).astype(bf), columns)

    row = lax.broadcasted_iota(jnp.int32, (high, 1), 0)
    weight = jnp.where(row < LANES, scale / whole, 2.0 * scale / whole)
    short_cos, short_sin = cosine[:, :length] * weight, -(sine[:, :length] * weight)

    def combine(s, short, spec):
        gains = own_ref[s * width : (s + 1) * width, length:] * (1.0 / scale)
        gains = jnp.concatenate([gains] * (cols // 128), axis=1)
        shift = jnp.concatenate(
            [gains[g * LANES : (g + 1) * LANES] for g in range(groups) for _ in range(copies)], axis=0
        )
        lr, li = spec[:, :cols] + shift, spec[:, cols:]
        rr, ri = short[:, :cols], short[:, cols:]
        return lr * rr - li * ri, lr * ri + li * rr

    chunks = [chunk(s) for s in range(sections)]
    odd = 2 * width - width // 16 * 16
    longs = [jnp.concatenate([part[:, odd:], part[:, width:odd]], axis=1) for part in chunks]
    if odd == 2 * width:
        longs = [part[:, width:] for part in chunks]
    specs = forward([chunks[0][:, :width], longs[0]])
    signal_spec = specs[:span]
    filters = combine(0, short_spec(0), specs[span:])
    results = []
    for s in range(sections):
        product = times(signal_spec, filters)
        if s + 1 < sections:
            filters = combine(s + 1, short_spec(s + 1), forward([longs[s + 1]]))
        result = back(product)
        results.append(result)
        for at in range(0, len(order), 2):
            pair = order[at : at + 2]
            if max(pair) // seq == s:
                rows_out = jnp.concatenate([results[rank // seq][rank % seq] for rank in pair], axis=0)
                out_ref[at * width : (at + 2) * width] = rows_out.astype(bf)
        if s + 1 < sections:
            rounded = result.astype(bf).astype(jnp.float32)
            signal_spec = forward([rounded * chunks[s + 1][:, :width]])


def body(activations, short_filters, long_filters, skip_gain):
    sections = short_filters.shape[0]
    tokens, channels = activations.shape[1:]
    devices = lax.axis_size(BOTH)
    seq_devices = lax.axis_size("seq")
    owned = channels // devices
    width = -(-owned // LANES) * LANES
    cols = tokens
    laid = devices * width
    order = spread_order(devices, seq_devices)

    def widen(array):
        split = array.reshape(array.shape[:2] + (devices, owned))
        split = jnp.pad(split, ((0, 0), (0, 0), (0, 0), (0, width - owned)))
        return split.reshape(array.shape[:2] + (laid,))

    def exchanged(array, height):
        chunks = array.reshape(devices, height, cols)
        moved = lax.all_to_all(
            chunks, BOTH, split_axis=0, concat_axis=0, tiled=True, axis_index_groups=[list(order)]
        )
        return moved.reshape(devices * height, cols)

    def grant(size):
        return pltpu.CompilerParams(vmem_limit_bytes=int(size))

    acts, filters = activations, long_filters
    if width != owned:
        acts, filters = widen(acts), widen(filters)
    split = 2 if seq_devices <= 32 and cols % 256 == 0 else 1
    table, back_table, turn = tables(seq_devices * split, cols // split, split)
    vmem = pl.BlockSpec(memory_space=pltpu.VMEM)
    hbm = pl.BlockSpec(memory_space=pltpu.HBM)
    area = laid * cols
    span = (seq_devices + 1) * width
    taps = short_filters.shape[1]
    place = lax.axis_index(BOTH).astype(jnp.int32).reshape(1)
    inputs = (acts, filters, short_filters, skip_gain)
    outgoing, own = pl.pallas_call(
        functools.partial(send_kernel, width, owned, order),
        out_shape=(
            jax.ShapeDtypeStruct((2 * laid, cols), jnp.bfloat16),
            jax.ShapeDtypeStruct((sections * width, taps + 128), jnp.float32),
        ),
        in_specs=[pl.BlockSpec(memory_space=pltpu.SMEM)] + [hbm] * 4,
        out_specs=(vmem, vmem),
        scratch_shapes=[
            pltpu.VMEM((cols, laid), jnp.bfloat16),
            pltpu.VMEM((cols, laid), jnp.float32),
            pltpu.VMEM(short_filters.shape, jnp.bfloat16),
            pltpu.VMEM(skip_gain.shape, jnp.float32),
            pltpu.SemaphoreType.DMA((2,)),
            pltpu.SemaphoreType.DMA((2,)),
        ],
        compiler_params=grant(4 * MIB + 24 * area),
    )(place, *(pltpu.with_memory_space_constraint(array, pltpu.HBM) for array in inputs))
    arrived = exchanged(outgoing, 2 * width)
    results = pl.pallas_call(
        functools.partial(main_kernel, width, sections, split, order),
        out_shape=jax.ShapeDtypeStruct((laid, cols), jnp.bfloat16),
        in_specs=[vmem] * 5,
        out_specs=vmem,
        compiler_params=grant(2 * MIB + 6 * area + 2 * table.size + 2 * back_table.size + 64 * span * cols),
    )(arrived, own, turn, table, back_table)
    returned = exchanged(results, width)
    final = pl.pallas_call(
        final_kernel,
        out_shape=jax.ShapeDtypeStruct((1, cols, laid), jnp.bfloat16),
        compiler_params=grant(4 * MIB + 16 * area),
    )(returned)
    if width != owned:
        final = final.reshape(1, cols, devices, width)[..., :owned].reshape(1, cols, channels)
    return final


def solution(mesh):
    return jax.shard_map(
        body,
        mesh=mesh,
        in_specs=(P("segment", "seq", None), P(), P("segment", "seq", None), P()),
        out_specs=P("segment", "seq", None),
        check_vma=False,
    )
```

```python
import functools
import math

import jax
import jax.numpy as jnp
import numpy as np
from jax import lax
from jax.experimental import pallas as pl
from jax.experimental.pallas import tpu as pltpu
from jax.sharding import PartitionSpec as P

BOTH = ("segment", "seq")
LANES = 8
MIB = 1024 * 1024


def spread_order(devices, seq_devices):
    half = seq_devices // 2
    along = [place // 2 + place % 2 * half for place in range(2 * half)]
    along += range(2 * half, seq_devices)
    return tuple(
        start + q for start in range(0, devices, seq_devices) for q in along
    )


def tables(real_rows, cols, split):
    grid_rows = 2 * real_rows + 1
    length = grid_rows * cols
    freqs = real_rows + 1
    k = np.arange(freqs)
    place = np.arange(real_rows).reshape(-1, split).T.reshape(-1)
    rows = 2.0 * math.pi * ((k[:, None] * place[None, :]) % grid_rows) / grid_rows
    first = np.stack([np.cos(rows), -np.sin(rows)]).reshape(2 * freqs, real_rows)
    row_part = np.kron(first, np.eye(LANES))
    b = np.arange(cols)
    angle = 2.0 * math.pi * (k[:, None] * b[None, :]) / length
    turn = np.concatenate([np.cos(angle), np.sin(angle)], axis=1)
    turn = np.pad(turn, ((0, -freqs % LANES), (0, 0)))
    grid = 2.0 * math.pi * ((b[:, None] * b[None, :]) % cols) / cols
    c, s = np.cos(grid), np.sin(grid)
    parts = [np.block([[c, -s], [s, c]]), row_part]
    lanes = max(part.shape[1] for part in parts)
    stacked = np.concatenate([np.pad(p, ((0, 0), (0, lanes - p.shape[1]))) for p in parts])
    back = np.kron(first.reshape(2, freqs, real_rows)[:, 1:].reshape(-1, real_rows).T, np.eye(LANES))
    bf = jnp.bfloat16
    return jnp.asarray(stacked, bf), jnp.asarray(back, bf), jnp.asarray(turn, jnp.float32)


def dot(a, b):
    return jnp.dot(a, b, preferred_element_type=jnp.float32)


def dot_rows(a, b):
    return lax.dot_general(a, b, (((1,), (1,)), ((), ())), preferred_element_type=jnp.float32)


def repeated(rows, count):
    return jnp.concatenate(
        [jnp.broadcast_to(rows[k : k + 1], (LANES, rows.shape[1])) for k in range(count)], axis=0
    )


def identity(size):
    down = lax.broadcasted_iota(jnp.int32, (size, size), 0)
    across = lax.broadcasted_iota(jnp.int32, (size, size), 1)
    return jnp.where(down == across, 1.0, 0.0).astype(jnp.bfloat16)


def send_kernel(
    width,
    owned,
    order,
    place_ref,
    act_ref,
    filt_ref,
    taps_ref,
    gain_ref,
    out_ref,
    own_ref,
    act_held,
    filt_held,
    taps_held,
    gain_held,
    in_sem,
    own_sem,
):
    sections, length, channels = taps_ref.shape
    own_copies = (
        pltpu.make_async_copy(taps_ref, taps_held, own_sem.at[0]),
        pltpu.make_async_copy(gain_ref, gain_held, own_sem.at[1]),
    )
    arriving = (
        pltpu.make_async_copy(act_ref.at[0], act_held, in_sem.at[0]),
        pltpu.make_async_copy(filt_ref.at[0], filt_held, in_sem.at[1]),
    )
    for copy in (arriving[0], *own_copies, arriving[1]):
        copy.start()
    size = 128
    eye = identity(size)
    mine = lax.broadcasted_iota(jnp.int32, (width, channels), 0)
    them = lax.broadcasted_iota(jnp.int32, (width, channels), 1)
    place = jnp.int32(0)
    for position, rank in enumerate(order):
        place = place + jnp.where(place_ref[0] == rank, position, 0)
    pick = jnp.where((them == mine + place * owned) & (mine < owned), 1.0, 0.0)
    def across(copy, held):
        copy.wait()
        columns = [
            dot_rows(eye, held[:, start : start + size].astype(jnp.bfloat16))
            for start in range(0, held.shape[1], size)
        ]
        return jnp.concatenate(columns, axis=0)

    even = width // 16 * 16
    act = across(arriving[0], act_held)
    for d in range(len(order) if even else 0):
        start = d * width
        out_ref[2 * start : 2 * start + even] = act[start : start + even].astype(jnp.bfloat16)
    for copy in own_copies:
        copy.wait()
    for s in range(sections):
        gain = jnp.sum(pick * gain_held[s : s + 1, :], axis=1, keepdims=True)
        own_ref[s * width : (s + 1) * width, :length] = dot_rows(pick.astype(jnp.bfloat16), taps_held[s])
        own_ref[s * width : (s + 1) * width, length:] = jnp.broadcast_to(gain, (width, 128))
    filt = across(arriving[1], filt_held)
    for d in range(len(order)):
        start, end = d * width, (d + 1) * width
        parts = [act[start + even : end], filt[start + even : end], filt[start : start + even]]
        rest = jnp.concatenate([part for part in parts if part.shape[0]], axis=0)
        out_ref[2 * start + even : 2 * end] = rest.astype(jnp.bfloat16)


def final_kernel(in_ref, out_ref):
    channels, tokens = in_ref.shape
    step = math.gcd(channels, 256)
    eye = identity(tokens)
    for start in range(0, channels, step):
        part = slice(start, start + step)
        out_ref[0, :, part] = dot_rows(eye, in_ref[part]).astype(jnp.bfloat16)


def main_kernel(width, sections, split, order, in_ref, own_ref, turn_ref, table_ref, back_ref, out_ref):
    total, tokens = in_ref.shape
    cols = tokens // split
    seq = total // (2 * width * sections)
    rows = seq * split
    groups = width // LANES
    high = (rows + 1) * LANES
    span = groups * high
    bf = jnp.bfloat16
    copies = rows + 1
    length = own_ref.shape[1] - 128
    scale = 1.0 / math.sqrt(rows * cols)
    whole = (2 * rows + 1) * cols
    turn = repeated(turn_ref[...], copies)
    cosine, sine = turn[:, :cols], turn[:, cols:]
    all_cos = jnp.concatenate([cosine] * groups, axis=0)
    all_sin = jnp.concatenate([sine] * groups, axis=0)
    forward_cols = table_ref[: 2 * cols, : 2 * cols]
    level, minus = table_ref[:cols, :cols], table_ref[:cols, cols : 2 * cols]
    plus = table_ref[cols : 2 * cols, :cols]
    back_cols = jnp.concatenate(
        [jnp.concatenate([level, plus], axis=1), jnp.concatenate([minus, level], axis=1)], axis=0
    )
    forward_rows = table_ref[2 * cols : 2 * cols + 2 * high, : rows * LANES]
    def chunk(s):
        starts = [order.index(s * seq + q) * 2 * width for q in range(seq)]
        part = jnp.concatenate([in_ref[at : at + 2 * width] for at in starts], axis=0)
        return part.astype(jnp.float32).reshape(seq, 2 * width, tokens)

    def forward(grids):
        blocks = []
        for grid in grids:
            for g in range(groups):
                part = grid[:, g * LANES : (g + 1) * LANES]
                parts = [part[:, :, h * cols : (h + 1) * cols] for h in range(split)]
                blocks.append(jnp.concatenate(parts, axis=0).reshape(rows * LANES, cols))
        spread = dot(forward_rows, jnp.concatenate(blocks, axis=1).astype(bf))
        turned = []
        for n in range(len(blocks)):
            lanes = slice(n * cols, (n + 1) * cols)
            real, imag = spread[:high, lanes], spread[high:, lanes]
            turned.append(
                jnp.concatenate([real * cosine + imag * sine, imag * cosine - real * sine], axis=1)
            )
        return dot(jnp.concatenate(turned, axis=0).astype(bf), forward_cols)

    def times(left, right):
        lr, li = left[:, :cols], left[:, cols:]
        rr, ri = right
        return jnp.concatenate([lr * rr - li * ri, lr * ri + li * rr], axis=1).astype(bf)

    def back(product):
        flat = dot(product, back_cols)
        real, imag = flat[:, :cols], flat[:, cols:]
        turned_real = real * all_cos - imag * all_sin
        turned_imag = real * all_sin + imag * all_cos
        joined = []
        for g in range(groups):
            part = slice(g * high + LANES, (g + 1) * high)
            joined.append(jnp.concatenate([turned_real[part], turned_imag[part]], axis=0))
        spread = dot(back_ref[...], jnp.concatenate(joined, axis=1).astype(bf))
        pieces = []
        for g in range(groups):
            piece = spread[:, g * cols : (g + 1) * cols].reshape(rows, LANES, cols)
            piece = piece + turned_real[g * high : g * high + LANES][None]
            parts = [piece[h * seq : (h + 1) * seq] for h in range(split)]
            pieces.append(jnp.concatenate(parts, axis=2))
        return jnp.concatenate(pieces, axis=1)

    def short_spec(s):
        turned = []
        for g in range(groups):
            start = s * width + g * LANES
            taps = jnp.concatenate([own_ref[start : start + LANES, :length]] * copies, axis=0)
            turned.append(jnp.concatenate([taps * short_cos, taps * short_sin], axis=1))
        columns = jnp.concatenate([table_ref[:length, : 2 * cols], table_ref[cols : cols + length, : 2 * cols]])
        return dot(jnp.concatenate(turned, axis=0).astype(bf), columns)

    row = lax.broadcasted_iota(jnp.int32, (high, 1), 0)
    weight = jnp.where(row < LANES, scale / whole, 2.0 * scale / whole)
    short_cos, short_sin = cosine[:, :length] * weight, -(sine[:, :length] * weight)

    def combine(s, short, spec):
        gains = own_ref[s * width : (s + 1) * width, length:] * (1.0 / scale)
        gains = jnp.concatenate([gains] * (cols // 128), axis=1)
        shift = jnp.concatenate(
            [gains[g * LANES : (g + 1) * LANES] for g in range(groups) for _ in range(copies)], axis=0
        )
        lr, li = spec[:, :cols] + shift, spec[:, cols:]
        rr, ri = short[:, :cols], short[:, cols:]
        return lr * rr - li * ri, lr * ri + li * rr

    chunks = [chunk(s) for s in range(sections)]
    odd = 2 * width - width // 16 * 16
    longs = [jnp.concatenate([part[:, odd:], part[:, width:odd]], axis=1) for part in chunks]
    if odd == 2 * width:
        longs = [part[:, width:] for part in chunks]
    specs = forward([chunks[0][:, :width], longs[0]])
    signal_spec = specs[:span]
    filters = combine(0, short_spec(0), specs[span:])
    results = []
    for s in range(sections):
        product = times(signal_spec, filters)
        if s + 1 < sections:
            filters = combine(s + 1, short_spec(s + 1), forward([longs[s + 1]]))
        result = back(product)
        results.append(result)
        if s + 1 < sections:
            rounded = result.astype(bf).astype(jnp.float32)
            signal_spec = forward([rounded * chunks[s + 1][:, :width]])
    for at in range(0, len(order), 2):
        pair = [results[rank // seq][rank % seq] for rank in order[at : at + 2]]
        out_ref[at * width : (at + 2) * width] = jnp.concatenate(pair, axis=0).astype(bf)


def body(activations, short_filters, long_filters, skip_gain):
    sections = short_filters.shape[0]
    tokens, channels = activations.shape[1:]
    devices = lax.axis_size(BOTH)
    seq_devices = lax.axis_size("seq")
    owned = channels // devices
    width = -(-owned // LANES) * LANES
    cols = tokens
    laid = devices * width
    order = spread_order(devices, seq_devices)

    def widen(array):
        split = array.reshape(array.shape[:2] + (devices, owned))
        split = jnp.pad(split, ((0, 0), (0, 0), (0, 0), (0, width - owned)))
        return split.reshape(array.shape[:2] + (laid,))

    def exchanged(array, height):
        chunks = array.reshape(devices, height, cols)
        moved = lax.all_to_all(
            chunks, BOTH, split_axis=0, concat_axis=0, tiled=True, axis_index_groups=[list(order)]
        )
        return moved.reshape(devices * height, cols)

    def grant(size):
        return pltpu.CompilerParams(vmem_limit_bytes=int(size))

    acts, filters = activations, long_filters
    if width != owned:
        acts, filters = widen(acts), widen(filters)
    split = 2 if seq_devices <= 32 and cols % 256 == 0 else 1
    table, back_table, turn = tables(seq_devices * split, cols // split, split)
    vmem = pl.BlockSpec(memory_space=pltpu.VMEM)
    hbm = pl.BlockSpec(memory_space=pltpu.HBM)
    area = laid * cols
    span = (seq_devices + 1) * width
    taps = short_filters.shape[1]
    place = lax.axis_index(BOTH).astype(jnp.int32).reshape(1)
    inputs = (acts, filters, short_filters, skip_gain)
    outgoing, own = pl.pallas_call(
        functools.partial(send_kernel, width, owned, order),
        out_shape=(
            jax.ShapeDtypeStruct((2 * laid, cols), jnp.bfloat16),
            jax.ShapeDtypeStruct((sections * width, taps + 128), jnp.float32),
        ),
        in_specs=[pl.BlockSpec(memory_space=pltpu.SMEM)] + [hbm] * 4,
        out_specs=(vmem, vmem),
        scratch_shapes=[
            pltpu.VMEM((cols, laid), jnp.bfloat16),
            pltpu.VMEM((cols, laid), jnp.float32),
            pltpu.VMEM(short_filters.shape, jnp.bfloat16),
            pltpu.VMEM(skip_gain.shape, jnp.float32),
            pltpu.SemaphoreType.DMA((2,)),
            pltpu.SemaphoreType.DMA((2,)),
        ],
        compiler_params=grant(4 * MIB + 24 * area),
    )(place, *(pltpu.with_memory_space_constraint(array, pltpu.HBM) for array in inputs))
    arrived = exchanged(outgoing, 2 * width)
    results = pl.pallas_call(
        functools.partial(main_kernel, width, sections, split, order),
        out_shape=jax.ShapeDtypeStruct((laid, cols), jnp.bfloat16),
        in_specs=[vmem] * 5,
        out_specs=vmem,
        compiler_params=grant(2 * MIB + 6 * area + 2 * table.size + 2 * back_table.size + 64 * span * cols),
    )(arrived, own, turn, table, back_table)
    returned = exchanged(results, width)
    final = pl.pallas_call(
        final_kernel,
        out_shape=jax.ShapeDtypeStruct((1, cols, laid), jnp.bfloat16),
        compiler_params=grant(4 * MIB + 16 * area),
    )(returned)
    if width != owned:
        final = final.reshape(1, cols, devices, width)[..., :owned].reshape(1, cols, channels)
    return final


def solution(mesh):
    return jax.shard_map(
        body,
        mesh=mesh,
        in_specs=(P("segment", "seq", None), P(), P("segment", "seq", None), P()),
        out_specs=P("segment", "seq", None),
        check_vma=False,
    )
```

```python
import functools
import math

import jax
import jax.numpy as jnp
import numpy as np
from jax import lax
from jax.experimental import pallas as pl
from jax.experimental.pallas import tpu as pltpu
from jax.sharding import PartitionSpec as P

BOTH = ("segment", "seq")
LANES = 8
MIB = 1024 * 1024


def spread_order(devices, seq_devices):
    half = seq_devices // 2
    along = [place // 2 + place % 2 * half for place in range(2 * half)]
    along += range(2 * half, seq_devices)
    return tuple(
        start + q for start in range(0, devices, seq_devices) for q in along
    )


def tables(real_rows, cols, split):
    grid_rows = 2 * real_rows + 1
    length = grid_rows * cols
    freqs = real_rows + 1
    k = np.arange(freqs)
    place = np.arange(real_rows).reshape(-1, split).T.reshape(-1)
    rows = 2.0 * math.pi * ((k[:, None] * place[None, :]) % grid_rows) / grid_rows
    first = np.stack([np.cos(rows), -np.sin(rows)]).reshape(2 * freqs, real_rows)
    row_part = np.kron(first, np.eye(LANES))
    b = np.arange(cols)
    angle = 2.0 * math.pi * (k[:, None] * b[None, :]) / length
    turn = np.concatenate([np.cos(angle), np.sin(angle)], axis=1)
    turn = np.pad(turn, ((0, -freqs % LANES), (0, 0)))
    grid = 2.0 * math.pi * ((b[:, None] * b[None, :]) % cols) / cols
    c, s = np.cos(grid), np.sin(grid)
    parts = [np.block([[c, -s], [s, c]]), row_part]
    lanes = max(part.shape[1] for part in parts)
    stacked = np.concatenate([np.pad(p, ((0, 0), (0, lanes - p.shape[1]))) for p in parts])
    back = np.kron(first.reshape(2, freqs, real_rows)[:, 1:].reshape(-1, real_rows).T, np.eye(LANES))
    bf = jnp.bfloat16
    return jnp.asarray(stacked, bf), jnp.asarray(back, bf), jnp.asarray(turn, jnp.float32)


def dot(a, b):
    return jnp.dot(a, b, preferred_element_type=jnp.float32)


def dot_rows(a, b):
    return lax.dot_general(a, b, (((1,), (1,)), ((), ())), preferred_element_type=jnp.float32)


def repeated(rows, count):
    return jnp.concatenate(
        [jnp.broadcast_to(rows[k : k + 1], (LANES, rows.shape[1])) for k in range(count)], axis=0
    )


def identity(size):
    down = lax.broadcasted_iota(jnp.int32, (size, size), 0)
    across = lax.broadcasted_iota(jnp.int32, (size, size), 1)
    return jnp.where(down == across, 1.0, 0.0).astype(jnp.bfloat16)


def send_kernel(
    width,
    owned,
    order,
    place_ref,
    act_ref,
    filt_ref,
    taps_ref,
    gain_ref,
    out_ref,
    own_ref,
    act_held,
    filt_held,
    taps_held,
    gain_held,
    in_sem,
    own_sem,
):
    sections, length, channels = taps_ref.shape
    mine_first = (
        pltpu.make_async_copy(taps_ref, taps_held, own_sem.at[0]),
        pltpu.make_async_copy(gain_ref, gain_held, own_sem.at[1]),
    )
    for copy in mine_first:
        copy.start()
    arriving = (
        pltpu.make_async_copy(act_ref.at[0], act_held, in_sem.at[0]),
        pltpu.make_async_copy(filt_ref.at[0], filt_held, in_sem.at[1]),
    )
    for copy in arriving:
        copy.start()
    size = 128
    eye = identity(size)
    mine = lax.broadcasted_iota(jnp.int32, (width, channels), 0)
    them = lax.broadcasted_iota(jnp.int32, (width, channels), 1)
    place = jnp.int32(0)
    for position, rank in enumerate(order):
        place = place + jnp.where(place_ref[0] == rank, position, 0)
    pick = jnp.where((them == mine + place * owned) & (mine < owned), 1.0, 0.0)
    for copy in mine_first:
        copy.wait()
    for s in range(sections):
        gain = jnp.sum(pick * gain_held[s : s + 1, :], axis=1, keepdims=True)
        own_ref[s * width : (s + 1) * width, :length] = dot_rows(pick.astype(jnp.bfloat16), taps_held[s])
        own_ref[s * width : (s + 1) * width, length:] = jnp.broadcast_to(gain, (width, 128))
    def across(copy, held):
        copy.wait()
        columns = []
        for start in range(0, held.shape[1], size):
            block = held[:, start : start + size]
            if start // size % 2 and block.dtype == jnp.float32:
                columns.append(block.T)
            else:
                columns.append(dot_rows(eye, block.astype(jnp.bfloat16)))
        return jnp.concatenate(columns, axis=0)

    even = width // 16 * 16
    act = across(arriving[0], act_held)
    for d in range(len(order) if even else 0):
        start = d * width
        out_ref[2 * start : 2 * start + even] = act[start : start + even].astype(jnp.bfloat16)
    filt = across(arriving[1], filt_held)
    for d in range(len(order)):
        start, end = d * width, (d + 1) * width
        parts = [act[start + even : end], filt[start + even : end], filt[start : start + even]]
        rest = jnp.concatenate([part for part in parts if part.shape[0]], axis=0)
        out_ref[2 * start + even : 2 * end] = rest.astype(jnp.bfloat16)


def final_kernel(in_ref, out_ref):
    channels, tokens = in_ref.shape
    step = math.gcd(channels, 256)
    eye = identity(tokens)
    for start in range(0, channels, step):
        part = slice(start, start + step)
        out_ref[0, :, part] = dot_rows(eye, in_ref[part]).astype(jnp.bfloat16)


def main_kernel(width, sections, split, order, in_ref, own_ref, turn_ref, table_ref, back_ref, out_ref):
    total, tokens = in_ref.shape
    cols = tokens // split
    seq = total // (2 * width * sections)
    rows = seq * split
    groups = width // LANES
    high = (rows + 1) * LANES
    span = groups * high
    bf = jnp.bfloat16
    copies = rows + 1
    length = own_ref.shape[1] - 128
    scale = 1.0 / math.sqrt(rows * cols)
    whole = (2 * rows + 1) * cols
    turn = repeated(turn_ref[...], copies)
    cosine, sine = turn[:, :cols], turn[:, cols:]
    all_cos = jnp.concatenate([cosine] * groups, axis=0)
    all_sin = jnp.concatenate([sine] * groups, axis=0)
    forward_cols = table_ref[: 2 * cols, : 2 * cols]
    level, minus = table_ref[:cols, :cols], table_ref[:cols, cols : 2 * cols]
    plus = table_ref[cols : 2 * cols, :cols]
    back_cols = jnp.concatenate(
        [jnp.concatenate([level, plus], axis=1), jnp.concatenate([minus, level], axis=1)], axis=0
    )
    forward_rows = table_ref[2 * cols : 2 * cols + 2 * high, : rows * LANES]
    def chunk(s):
        starts = [order.index(s * seq + q) * 2 * width for q in range(seq)]
        part = jnp.concatenate([in_ref[at : at + 2 * width] for at in starts], axis=0)
        return part.astype(jnp.float32).reshape(seq, 2 * width, tokens)

    def forward(grids):
        blocks = []
        for grid in grids:
            for g in range(groups):
                part = grid[:, g * LANES : (g + 1) * LANES]
                parts = [part[:, :, h * cols : (h + 1) * cols] for h in range(split)]
                blocks.append(jnp.concatenate(parts, axis=0).reshape(rows * LANES, cols))
        spread = dot(forward_rows, jnp.concatenate(blocks, axis=1).astype(bf))
        turned = []
        for n in range(len(blocks)):
            lanes = slice(n * cols, (n + 1) * cols)
            real, imag = spread[:high, lanes], spread[high:, lanes]
            turned.append(
                jnp.concatenate([real * cosine + imag * sine, imag * cosine - real * sine], axis=1)
            )
        return dot(jnp.concatenate(turned, axis=0).astype(bf), forward_cols)

    def times(left, right):
        lr, li = left[:, :cols], left[:, cols:]
        rr, ri = right
        return jnp.concatenate([lr * rr - li * ri, lr * ri + li * rr], axis=1).astype(bf)

    def back(product):
        flat = dot(product, back_cols)
        real, imag = flat[:, :cols], flat[:, cols:]
        turned_real = real * all_cos - imag * all_sin
        turned_imag = real * all_sin + imag * all_cos
        joined = []
        for g in range(groups):
            part = slice(g * high + LANES, (g + 1) * high)
            joined.append(jnp.concatenate([turned_real[part], turned_imag[part]], axis=0))
        spread = dot(back_ref[...], jnp.concatenate(joined, axis=1).astype(bf))
        pieces = []
        for g in range(groups):
            piece = spread[:, g * cols : (g + 1) * cols].reshape(rows, LANES, cols)
            piece = piece + turned_real[g * high : g * high + LANES][None]
            parts = [piece[h * seq : (h + 1) * seq] for h in range(split)]
            pieces.append(jnp.concatenate(parts, axis=2))
        return jnp.concatenate(pieces, axis=1)

    def short_spec(s):
        turned = []
        for g in range(groups):
            start = s * width + g * LANES
            taps = jnp.concatenate([own_ref[start : start + LANES, :length]] * copies, axis=0)
            turned.append(jnp.concatenate([taps * short_cos, taps * short_sin], axis=1))
        columns = jnp.concatenate([table_ref[:length, : 2 * cols], table_ref[cols : cols + length, : 2 * cols]])
        return dot(jnp.concatenate(turned, axis=0).astype(bf), columns)

    row = lax.broadcasted_iota(jnp.int32, (high, 1), 0)
    weight = jnp.where(row < LANES, scale / whole, 2.0 * scale / whole)
    short_cos, short_sin = cosine[:, :length] * weight, -(sine[:, :length] * weight)

    def combine(s, short, spec):
        gains = own_ref[s * width : (s + 1) * width, length:] * (1.0 / scale)
        gains = jnp.concatenate([gains] * (cols // 128), axis=1)
        shift = jnp.concatenate(
            [gains[g * LANES : (g + 1) * LANES] for g in range(groups) for _ in range(copies)], axis=0
        )
        lr, li = spec[:, :cols] + shift, spec[:, cols:]
        rr, ri = short[:, :cols], short[:, cols:]
        return lr * rr - li * ri, lr * ri + li * rr

    chunks = [chunk(s) for s in range(sections)]
    odd = 2 * width - width // 16 * 16
    longs = [jnp.concatenate([part[:, odd:], part[:, width:odd]], axis=1) for part in chunks]
    if odd == 2 * width:
        longs = [part[:, width:] for part in chunks]
    specs = forward([chunks[0][:, :width], longs[0]])
    signal_spec = specs[:span]
    filters = combine(0, short_spec(0), specs[span:])
    results = []
    for s in range(sections):
        product = times(signal_spec, filters)
        if s + 1 < sections:
            filters = combine(s + 1, short_spec(s + 1), forward([longs[s + 1]]))
        result = back(product)
        results.append(result)
        if s + 1 < sections:
            rounded = result.astype(bf).astype(jnp.float32)
            signal_spec = forward([rounded * chunks[s + 1][:, :width]])
    for at in range(0, len(order), 2):
        pair = [results[rank // seq][rank % seq] for rank in order[at : at + 2]]
        out_ref[at * width : (at + 2) * width] = jnp.concatenate(pair, axis=0).astype(bf)


def body(activations, short_filters, long_filters, skip_gain):
    sections = short_filters.shape[0]
    tokens, channels = activations.shape[1:]
    devices = lax.axis_size(BOTH)
    seq_devices = lax.axis_size("seq")
    owned = channels // devices
    width = -(-owned // LANES) * LANES
    cols = tokens
    laid = devices * width
    order = spread_order(devices, seq_devices)

    def widen(array):
        split = array.reshape(array.shape[:2] + (devices, owned))
        split = jnp.pad(split, ((0, 0), (0, 0), (0, 0), (0, width - owned)))
        return split.reshape(array.shape[:2] + (laid,))

    def exchanged(array, height):
        chunks = array.reshape(devices, height, cols)
        moved = lax.all_to_all(
            chunks, BOTH, split_axis=0, concat_axis=0, tiled=True, axis_index_groups=[list(order)]
        )
        return moved.reshape(devices * height, cols)

    def grant(size):
        return pltpu.CompilerParams(vmem_limit_bytes=int(size))

    acts, filters = activations, long_filters
    if width != owned:
        acts, filters = widen(acts), widen(filters)
    split = 2 if seq_devices <= 32 and cols % 256 == 0 else 1
    table, back_table, turn = tables(seq_devices * split, cols // split, split)
    vmem = pl.BlockSpec(memory_space=pltpu.VMEM)
    hbm = pl.BlockSpec(memory_space=pltpu.HBM)
    area = laid * cols
    span = (seq_devices + 1) * width
    taps = short_filters.shape[1]
    place = lax.axis_index(BOTH).astype(jnp.int32).reshape(1)
    inputs = (acts, filters, short_filters, skip_gain)
    outgoing, own = pl.pallas_call(
        functools.partial(send_kernel, width, owned, order),
        out_shape=(
            jax.ShapeDtypeStruct((2 * laid, cols), jnp.bfloat16),
            jax.ShapeDtypeStruct((sections * width, taps + 128), jnp.float32),
        ),
        in_specs=[pl.BlockSpec(memory_space=pltpu.SMEM)] + [hbm] * 4,
        out_specs=(vmem, vmem),
        scratch_shapes=[
            pltpu.VMEM((cols, laid), jnp.bfloat16),
            pltpu.VMEM((cols, laid), jnp.float32),
            pltpu.VMEM(short_filters.shape, jnp.bfloat16),
            pltpu.VMEM(skip_gain.shape, jnp.float32),
            pltpu.SemaphoreType.DMA((2,)),
            pltpu.SemaphoreType.DMA((2,)),
        ],
        compiler_params=grant(4 * MIB + 24 * area),
    )(place, *(pltpu.with_memory_space_constraint(array, pltpu.HBM) for array in inputs))
    arrived = exchanged(outgoing, 2 * width)
    results = pl.pallas_call(
        functools.partial(main_kernel, width, sections, split, order),
        out_shape=jax.ShapeDtypeStruct((laid, cols), jnp.bfloat16),
        in_specs=[vmem] * 5,
        out_specs=vmem,
        compiler_params=grant(2 * MIB + 6 * area + 2 * table.size + 2 * back_table.size + 64 * span * cols),
    )(arrived, own, turn, table, back_table)
    returned = exchanged(results, width)
    final = pl.pallas_call(
        final_kernel,
        out_shape=jax.ShapeDtypeStruct((1, cols, laid), jnp.bfloat16),
        compiler_params=grant(4 * MIB + 16 * area),
    )(returned)
    if width != owned:
        final = final.reshape(1, cols, devices, width)[..., :owned].reshape(1, cols, channels)
    return final


def solution(mesh):
    return jax.shard_map(
        body,
        mesh=mesh,
        in_specs=(P("segment", "seq", None), P(), P("segment", "seq", None), P()),
        out_specs=P("segment", "seq", None),
        check_vma=False,
    )
```

```python
import functools
import math

import jax
import jax.numpy as jnp
import numpy as np
from jax import lax
from jax.experimental import pallas as pl
from jax.experimental.pallas import tpu as pltpu
from jax.sharding import PartitionSpec as P

BOTH = ("segment", "seq")
LANES = 8
MIB = 1024 * 1024


def spread_order(devices, seq_devices):
    half = seq_devices // 2
    along = [place // 2 + place % 2 * half for place in range(2 * half)]
    along += range(2 * half, seq_devices)
    return tuple(
        start + q for start in range(0, devices, seq_devices) for q in along
    )


def tables(real_rows, cols, split):
    grid_rows = 2 * real_rows + 1
    length = grid_rows * cols
    freqs = real_rows + 1
    k = np.arange(freqs)
    place = np.arange(real_rows).reshape(-1, split).T.reshape(-1)
    rows = 2.0 * math.pi * ((k[:, None] * place[None, :]) % grid_rows) / grid_rows
    first = np.stack([np.cos(rows), -np.sin(rows)]).reshape(2 * freqs, real_rows)
    row_part = np.kron(first, np.eye(LANES))
    b = np.arange(cols)
    angle = 2.0 * math.pi * (k[:, None] * b[None, :]) / length
    turn = np.concatenate([np.cos(angle), np.sin(angle)], axis=1)
    turn = np.pad(turn, ((0, -freqs % LANES), (0, 0)))
    grid = 2.0 * math.pi * ((b[:, None] * b[None, :]) % cols) / cols
    c, s = np.cos(grid), np.sin(grid)
    parts = [np.block([[c, -s], [s, c]]), row_part]
    lanes = max(part.shape[1] for part in parts)
    stacked = np.concatenate([np.pad(p, ((0, 0), (0, lanes - p.shape[1]))) for p in parts])
    back = np.kron(first.reshape(2, freqs, real_rows)[:, 1:].reshape(-1, real_rows).T, np.eye(LANES))
    bf = jnp.bfloat16
    return jnp.asarray(stacked, bf), jnp.asarray(back, bf), jnp.asarray(turn, jnp.float32)


def dot(a, b):
    return jnp.dot(a, b, preferred_element_type=jnp.float32)


def dot_rows(a, b):
    return lax.dot_general(a, b, (((1,), (1,)), ((), ())), preferred_element_type=jnp.float32)


def repeated(rows, count):
    return jnp.concatenate(
        [jnp.broadcast_to(rows[k : k + 1], (LANES, rows.shape[1])) for k in range(count)], axis=0
    )


def identity(size):
    down = lax.broadcasted_iota(jnp.int32, (size, size), 0)
    across = lax.broadcasted_iota(jnp.int32, (size, size), 1)
    return jnp.where(down == across, 1.0, 0.0).astype(jnp.bfloat16)


def send_kernel(
    width,
    owned,
    order,
    place_ref,
    act_ref,
    filt_ref,
    taps_ref,
    gain_ref,
    out_ref,
    own_ref,
    act_held,
    filt_held,
    taps_held,
    gain_held,
    in_sem,
    own_sem,
):
    sections, length, channels = taps_ref.shape
    mine_first = (
        pltpu.make_async_copy(taps_ref, taps_held, own_sem.at[0]),
        pltpu.make_async_copy(gain_ref, gain_held, own_sem.at[1]),
    )
    for copy in mine_first:
        copy.start()
    arriving = (
        pltpu.make_async_copy(act_ref.at[0], act_held, in_sem.at[0]),
        pltpu.make_async_copy(filt_ref.at[0], filt_held, in_sem.at[1]),
    )
    for copy in arriving:
        copy.start()
    size = 128
    eye = identity(size)
    mine = lax.broadcasted_iota(jnp.int32, (width, channels), 0)
    them = lax.broadcasted_iota(jnp.int32, (width, channels), 1)
    place = jnp.int32(0)
    for position, rank in enumerate(order):
        place = place + jnp.where(place_ref[0] == rank, position, 0)
    pick = jnp.where((them == mine + place * owned) & (mine < owned), 1.0, 0.0)
    for copy in mine_first:
        copy.wait()
    for s in range(sections):
        gain = jnp.sum(pick * gain_held[s : s + 1, :], axis=1, keepdims=True)
        own_ref[s * width : (s + 1) * width, :length] = dot_rows(pick.astype(jnp.bfloat16), taps_held[s])
        own_ref[s * width : (s + 1) * width, length:] = jnp.broadcast_to(gain, (width, 128))
    def across(copy, held):
        copy.wait()
        columns = []
        for start in range(0, held.shape[1], size):
            block = held[:, start : start + size]
            if start // size % 2 and block.dtype == jnp.float32:
                columns.append(block.T)
            else:
                columns.append(dot_rows(eye, block.astype(jnp.bfloat16)))
        return jnp.concatenate(columns, axis=0)

    even = width // 16 * 16
    act = across(arriving[0], act_held)
    for d in range(len(order) if even else 0):
        start = d * width
        out_ref[2 * start : 2 * start + even] = act[start : start + even].astype(jnp.bfloat16)
    filt = across(arriving[1], filt_held)
    for d in range(len(order)):
        start, end = d * width, (d + 1) * width
        parts = [act[start + even : end], filt[start + even : end], filt[start : start + even]]
        rest = jnp.concatenate([part for part in parts if part.shape[0]], axis=0)
        out_ref[2 * start + even : 2 * end] = rest.astype(jnp.bfloat16)


def final_kernel(in_ref, out_ref, held, sem):
    channels, tokens = in_ref.shape
    step = math.gcd(channels, 256)
    half = tokens // 2
    eye = identity(tokens)
    copies = []
    for n in range(2):
        rows = slice(n * half, (n + 1) * half)
        for start in range(0, channels, step):
            part = slice(start, start + step)
            held[rows, part] = dot_rows(eye[rows], in_ref[part]).astype(jnp.bfloat16)
        copies.append(pltpu.make_async_copy(held.at[rows], out_ref.at[0, rows], sem.at[n]))
        copies[n].start()
    for copy in copies:
        copy.wait()


def main_kernel(width, sections, split, order, in_ref, own_ref, turn_ref, table_ref, back_ref, out_ref):
    total, tokens = in_ref.shape
    cols = tokens // split
    seq = total // (2 * width * sections)
    rows = seq * split
    groups = width // LANES
    high = (rows + 1) * LANES
    span = groups * high
    bf = jnp.bfloat16
    copies = rows + 1
    length = own_ref.shape[1] - 128
    scale = 1.0 / math.sqrt(rows * cols)
    whole = (2 * rows + 1) * cols
    turn = repeated(turn_ref[...], copies)
    cosine, sine = turn[:, :cols], turn[:, cols:]
    all_cos = jnp.concatenate([cosine] * groups, axis=0)
    all_sin = jnp.concatenate([sine] * groups, axis=0)
    forward_cols = table_ref[: 2 * cols, : 2 * cols]
    level, minus = table_ref[:cols, :cols], table_ref[:cols, cols : 2 * cols]
    plus = table_ref[cols : 2 * cols, :cols]
    back_cols = jnp.concatenate(
        [jnp.concatenate([level, plus], axis=1), jnp.concatenate([minus, level], axis=1)], axis=0
    )
    forward_rows = table_ref[2 * cols : 2 * cols + 2 * high, : rows * LANES]
    def chunk(s):
        starts = [order.index(s * seq + q) * 2 * width for q in range(seq)]
        part = jnp.concatenate([in_ref[at : at + 2 * width] for at in starts], axis=0)
        return part.astype(jnp.float32).reshape(seq, 2 * width, tokens)

    def forward(grids):
        blocks = []
        for grid in grids:
            for g in range(groups):
                part = grid[:, g * LANES : (g + 1) * LANES]
                parts = [part[:, :, h * cols : (h + 1) * cols] for h in range(split)]
                blocks.append(jnp.concatenate(parts, axis=0).reshape(rows * LANES, cols))
        spread = dot(forward_rows, jnp.concatenate(blocks, axis=1).astype(bf))
        turned = []
        for n in range(len(blocks)):
            lanes = slice(n * cols, (n + 1) * cols)
            real, imag = spread[:high, lanes], spread[high:, lanes]
            turned.append(
                jnp.concatenate([real * cosine + imag * sine, imag * cosine - real * sine], axis=1)
            )
        return dot(jnp.concatenate(turned, axis=0).astype(bf), forward_cols)

    def times(left, right):
        lr, li = left[:, :cols], left[:, cols:]
        rr, ri = right
        return jnp.concatenate([lr * rr - li * ri, lr * ri + li * rr], axis=1).astype(bf)

    def back(product):
        flat = dot(product, back_cols)
        real, imag = flat[:, :cols], flat[:, cols:]
        turned_real = real * all_cos - imag * all_sin
        turned_imag = real * all_sin + imag * all_cos
        joined = []
        for g in range(groups):
            part = slice(g * high + LANES, (g + 1) * high)
            joined.append(jnp.concatenate([turned_real[part], turned_imag[part]], axis=0))
        spread = dot(back_ref[...], jnp.concatenate(joined, axis=1).astype(bf))
        pieces = []
        for g in range(groups):
            piece = spread[:, g * cols : (g + 1) * cols].reshape(rows, LANES, cols)
            piece = piece + turned_real[g * high : g * high + LANES][None]
            parts = [piece[h * seq : (h + 1) * seq] for h in range(split)]
            pieces.append(jnp.concatenate(parts, axis=2))
        return jnp.concatenate(pieces, axis=1)

    def short_spec(s):
        turned = []
        for g in range(groups):
            start = s * width + g * LANES
            taps = jnp.concatenate([own_ref[start : start + LANES, :length]] * copies, axis=0)
            turned.append(jnp.concatenate([taps * short_cos, taps * short_sin], axis=1))
        columns = jnp.concatenate([table_ref[:length, : 2 * cols], table_ref[cols : cols + length, : 2 * cols]])
        return dot(jnp.concatenate(turned, axis=0).astype(bf), columns)

    row = lax.broadcasted_iota(jnp.int32, (high, 1), 0)
    weight = jnp.where(row < LANES, scale / whole, 2.0 * scale / whole)
    short_cos, short_sin = cosine[:, :length] * weight, -(sine[:, :length] * weight)

    def combine(s, short, spec):
        gains = own_ref[s * width : (s + 1) * width, length:] * (1.0 / scale)
        gains = jnp.concatenate([gains] * (cols // 128), axis=1)
        shift = jnp.concatenate(
            [gains[g * LANES : (g + 1) * LANES] for g in range(groups) for _ in range(copies)], axis=0
        )
        lr, li = spec[:, :cols] + shift, spec[:, cols:]
        rr, ri = short[:, :cols], short[:, cols:]
        return lr * rr - li * ri, lr * ri + li * rr

    chunks = [chunk(s) for s in range(sections)]
    odd = 2 * width - width // 16 * 16
    longs = [jnp.concatenate([part[:, odd:], part[:, width:odd]], axis=1) for part in chunks]
    if odd == 2 * width:
        longs = [part[:, width:] for part in chunks]
    specs = forward([chunks[0][:, :width], longs[0]])
    signal_spec = specs[:span]
    filters = combine(0, short_spec(0), specs[span:])
    results = []
    for s in range(sections):
        product = times(signal_spec, filters)
        if s + 1 < sections:
            filters = combine(s + 1, short_spec(s + 1), forward([longs[s + 1]]))
        result = back(product)
        results.append(result)
        if s + 1 < sections:
            rounded = result.astype(bf).astype(jnp.float32)
            signal_spec = forward([rounded * chunks[s + 1][:, :width]])
    for at in range(0, len(order), 2):
        pair = [results[rank // seq][rank % seq] for rank in order[at : at + 2]]
        out_ref[at * width : (at + 2) * width] = jnp.concatenate(pair, axis=0).astype(bf)


def body(activations, short_filters, long_filters, skip_gain):
    sections = short_filters.shape[0]
    tokens, channels = activations.shape[1:]
    devices = lax.axis_size(BOTH)
    seq_devices = lax.axis_size("seq")
    owned = channels // devices
    width = -(-owned // LANES) * LANES
    cols = tokens
    laid = devices * width
    order = spread_order(devices, seq_devices)

    def widen(array):
        split = array.reshape(array.shape[:2] + (devices, owned))
        split = jnp.pad(split, ((0, 0), (0, 0), (0, 0), (0, width - owned)))
        return split.reshape(array.shape[:2] + (laid,))

    def exchanged(array, height):
        chunks = array.reshape(devices, height, cols)
        moved = lax.all_to_all(
            chunks, BOTH, split_axis=0, concat_axis=0, tiled=True, axis_index_groups=[list(order)]
        )
        return moved.reshape(devices * height, cols)

    def grant(size):
        return pltpu.CompilerParams(vmem_limit_bytes=int(size))

    acts, filters = activations, long_filters
    if width != owned:
        acts, filters = widen(acts), widen(filters)
    split = 2 if seq_devices <= 32 and cols % 256 == 0 else 1
    table, back_table, turn = tables(seq_devices * split, cols // split, split)
    vmem = pl.BlockSpec(memory_space=pltpu.VMEM)
    hbm = pl.BlockSpec(memory_space=pltpu.HBM)
    area = laid * cols
    span = (seq_devices + 1) * width
    taps = short_filters.shape[1]
    place = lax.axis_index(BOTH).astype(jnp.int32).reshape(1)
    inputs = (acts, filters, short_filters, skip_gain)
    outgoing, own = pl.pallas_call(
        functools.partial(send_kernel, width, owned, order),
        out_shape=(
            jax.ShapeDtypeStruct((2 * laid, cols), jnp.bfloat16),
            jax.ShapeDtypeStruct((sections * width, taps + 128), jnp.float32),
        ),
        in_specs=[pl.BlockSpec(memory_space=pltpu.SMEM)] + [hbm] * 4,
        out_specs=(vmem, vmem),
        scratch_shapes=[
            pltpu.VMEM((cols, laid), jnp.bfloat16),
            pltpu.VMEM((cols, laid), jnp.float32),
            pltpu.VMEM(short_filters.shape, jnp.bfloat16),
            pltpu.VMEM(skip_gain.shape, jnp.float32),
            pltpu.SemaphoreType.DMA((2,)),
            pltpu.SemaphoreType.DMA((2,)),
        ],
        compiler_params=grant(4 * MIB + 24 * area),
    )(place, *(pltpu.with_memory_space_constraint(array, pltpu.HBM) for array in inputs))
    arrived = exchanged(outgoing, 2 * width)
    results = pl.pallas_call(
        functools.partial(main_kernel, width, sections, split, order),
        out_shape=jax.ShapeDtypeStruct((laid, cols), jnp.bfloat16),
        in_specs=[vmem] * 5,
        out_specs=vmem,
        compiler_params=grant(2 * MIB + 6 * area + 2 * table.size + 2 * back_table.size + 64 * span * cols),
    )(arrived, own, turn, table, back_table)
    returned = exchanged(results, width)
    final = pl.pallas_call(
        final_kernel,
        out_shape=jax.ShapeDtypeStruct((1, cols, laid), jnp.bfloat16),
        in_specs=[vmem],
        out_specs=hbm,
        scratch_shapes=[pltpu.VMEM((cols, laid), jnp.bfloat16), pltpu.SemaphoreType.DMA((2,))],
        compiler_params=grant(4 * MIB + 16 * area),
    )(returned)
    if width != owned:
        final = final.reshape(1, cols, devices, width)[..., :owned].reshape(1, cols, channels)
    return final


def solution(mesh):
    return jax.shard_map(
        body,
        mesh=mesh,
        in_specs=(P("segment", "seq", None), P(), P("segment", "seq", None), P()),
        out_specs=P("segment", "seq", None),
        check_vma=False,
    )
```

```python
import functools
import math

import jax
import jax.numpy as jnp
import numpy as np
from jax import lax
from jax.experimental import pallas as pl
from jax.experimental.pallas import tpu as pltpu
from jax.sharding import PartitionSpec as P

BOTH = ("segment", "seq")
LANES = 8
MIB = 1024 * 1024


FIELDS = {2: 7, 3: 11, 4: 19, 5: 37, 6: 67, 7: 131, 8: 285, 9: 529, 10: 1033}


def spread_order(devices):
    bits = devices.bit_length() - 1
    if devices != 1 << bits or bits not in FIELDS:
        return tuple(range(devices))
    order, power = [0], 1
    while len(order) < devices:
        order.append(power)
        power <<= 1
        if power & devices:
            power ^= FIELDS[bits]
    return tuple(order)


def tables(real_rows, cols, split):
    grid_rows = 2 * real_rows + 1
    length = grid_rows * cols
    freqs = real_rows + 1
    k = np.arange(freqs)
    place = np.arange(real_rows).reshape(-1, split).T.reshape(-1)
    rows = 2.0 * math.pi * ((k[:, None] * place[None, :]) % grid_rows) / grid_rows
    first = np.stack([np.cos(rows), -np.sin(rows)]).reshape(2 * freqs, real_rows)
    row_part = np.kron(first, np.eye(LANES))
    b = np.arange(cols)
    angle = 2.0 * math.pi * (k[:, None] * b[None, :]) / length
    turn = np.concatenate([np.cos(angle), np.sin(angle)], axis=1)
    turn = np.pad(turn, ((0, -freqs % LANES), (0, 0)))
    grid = 2.0 * math.pi * ((b[:, None] * b[None, :]) % cols) / cols
    c, s = np.cos(grid), np.sin(grid)
    parts = [np.block([[c, -s], [s, c]]), row_part]
    lanes = max(part.shape[1] for part in parts)
    stacked = np.concatenate([np.pad(p, ((0, 0), (0, lanes - p.shape[1]))) for p in parts])
    back = np.kron(first.reshape(2, freqs, real_rows)[:, 1:].reshape(-1, real_rows).T, np.eye(LANES))
    bf = jnp.bfloat16
    return jnp.asarray(stacked, bf), jnp.asarray(back, bf), jnp.asarray(turn, jnp.float32)


def dot(a, b):
    return jnp.dot(a, b, preferred_element_type=jnp.float32)


def dot_rows(a, b):
    return lax.dot_general(a, b, (((1,), (1,)), ((), ())), preferred_element_type=jnp.float32)


def repeated(rows, count):
    return jnp.concatenate(
        [jnp.broadcast_to(rows[k : k + 1], (LANES, rows.shape[1])) for k in range(count)], axis=0
    )


def identity(size):
    down = lax.broadcasted_iota(jnp.int32, (size, size), 0)
    across = lax.broadcasted_iota(jnp.int32, (size, size), 1)
    return jnp.where(down == across, 1.0, 0.0).astype(jnp.bfloat16)


def send_kernel(
    width,
    owned,
    order,
    place_ref,
    act_ref,
    filt_ref,
    taps_ref,
    gain_ref,
    out_ref,
    own_ref,
    act_held,
    filt_held,
    taps_held,
    gain_held,
    in_sem,
    own_sem,
):
    sections, length, channels = taps_ref.shape
    mine_first = (
        pltpu.make_async_copy(taps_ref, taps_held, own_sem.at[0]),
        pltpu.make_async_copy(gain_ref, gain_held, own_sem.at[1]),
    )
    for copy in mine_first:
        copy.start()
    arriving = (
        pltpu.make_async_copy(act_ref.at[0], act_held, in_sem.at[0]),
        pltpu.make_async_copy(filt_ref.at[0], filt_held, in_sem.at[1]),
    )
    for copy in arriving:
        copy.start()
    size = 128
    eye = identity(size)
    mine = lax.broadcasted_iota(jnp.int32, (width, channels), 0)
    them = lax.broadcasted_iota(jnp.int32, (width, channels), 1)
    place = jnp.int32(0)
    for position, rank in enumerate(order):
        place = place + jnp.where(place_ref[0] == rank, position, 0)
    pick = jnp.where((them == mine + place * owned) & (mine < owned), 1.0, 0.0)
    for copy in mine_first:
        copy.wait()
    for s in range(sections):
        gain = jnp.sum(pick * gain_held[s : s + 1, :], axis=1, keepdims=True)
        own_ref[s * width : (s + 1) * width, :length] = dot_rows(pick.astype(jnp.bfloat16), taps_held[s])
        own_ref[s * width : (s + 1) * width, length:] = jnp.broadcast_to(gain, (width, 128))
    def across(copy, held):
        copy.wait()
        columns = []
        for start in range(0, held.shape[1], size):
            block = held[:, start : start + size]
            if start // size % 2 and block.dtype == jnp.float32:
                columns.append(block.T)
            else:
                columns.append(dot_rows(eye, block.astype(jnp.bfloat16)))
        return jnp.concatenate(columns, axis=0)

    even = width // 16 * 16
    act = across(arriving[0], act_held)
    for d in range(len(order) if even else 0):
        start = d * width
        out_ref[2 * start : 2 * start + even] = act[start : start + even].astype(jnp.bfloat16)
    filt = across(arriving[1], filt_held)
    for d in range(len(order)):
        start, end = d * width, (d + 1) * width
        parts = [act[start + even : end], filt[start + even : end], filt[start : start + even]]
        rest = jnp.concatenate([part for part in parts if part.shape[0]], axis=0)
        out_ref[2 * start + even : 2 * end] = rest.astype(jnp.bfloat16)


def final_kernel(in_ref, out_ref):
    channels, tokens = in_ref.shape
    step = math.gcd(channels, 256)
    eye = identity(tokens)
    for start in range(0, channels, step):
        part = slice(start, start + step)
        out_ref[0, :, part] = dot_rows(eye, in_ref[part]).astype(jnp.bfloat16)


def main_kernel(width, sections, split, order, in_ref, own_ref, turn_ref, table_ref, back_ref, out_ref):
    total, tokens = in_ref.shape
    cols = tokens // split
    seq = total // (2 * width * sections)
    rows = seq * split
    groups = width // LANES
    high = (rows + 1) * LANES
    span = groups * high
    bf = jnp.bfloat16
    copies = rows + 1
    length = own_ref.shape[1] - 128
    scale = 1.0 / math.sqrt(rows * cols)
    whole = (2 * rows + 1) * cols
    turn = repeated(turn_ref[...], copies)
    cosine, sine = turn[:, :cols], turn[:, cols:]
    all_cos = jnp.concatenate([cosine] * groups, axis=0)
    all_sin = jnp.concatenate([sine] * groups, axis=0)
    forward_cols = table_ref[: 2 * cols, : 2 * cols]
    level, minus = table_ref[:cols, :cols], table_ref[:cols, cols : 2 * cols]
    plus = table_ref[cols : 2 * cols, :cols]
    back_cols = jnp.concatenate(
        [jnp.concatenate([level, plus], axis=1), jnp.concatenate([minus, level], axis=1)], axis=0
    )
    forward_rows = table_ref[2 * cols : 2 * cols + 2 * high, : rows * LANES]
    def chunk(s):
        starts = [order.index(s * seq + q) * 2 * width for q in range(seq)]
        part = jnp.concatenate([in_ref[at : at + 2 * width] for at in starts], axis=0)
        return part.astype(jnp.float32).reshape(seq, 2 * width, tokens)

    def forward(grids):
        blocks = []
        for grid in grids:
            for g in range(groups):
                part = grid[:, g * LANES : (g + 1) * LANES]
                parts = [part[:, :, h * cols : (h + 1) * cols] for h in range(split)]
                blocks.append(jnp.concatenate(parts, axis=0).reshape(rows * LANES, cols))
        spread = dot(forward_rows, jnp.concatenate(blocks, axis=1).astype(bf))
        turned = []
        for n in range(len(blocks)):
            lanes = slice(n * cols, (n + 1) * cols)
            real, imag = spread[:high, lanes], spread[high:, lanes]
            turned.append(
                jnp.concatenate([real * cosine + imag * sine, imag * cosine - real * sine], axis=1)
            )
        return dot(jnp.concatenate(turned, axis=0).astype(bf), forward_cols)

    def times(left, right):
        lr, li = left[:, :cols], left[:, cols:]
        rr, ri = right
        return jnp.concatenate([lr * rr - li * ri, lr * ri + li * rr], axis=1).astype(bf)

    def back(product):
        flat = dot(product, back_cols)
        real, imag = flat[:, :cols], flat[:, cols:]
        turned_real = real * all_cos - imag * all_sin
        turned_imag = real * all_sin + imag * all_cos
        joined = []
        for g in range(groups):
            part = slice(g * high + LANES, (g + 1) * high)
            joined.append(jnp.concatenate([turned_real[part], turned_imag[part]], axis=0))
        spread = dot(back_ref[...], jnp.concatenate(joined, axis=1).astype(bf))
        pieces = []
        for g in range(groups):
            piece = spread[:, g * cols : (g + 1) * cols].reshape(rows, LANES, cols)
            piece = piece + turned_real[g * high : g * high + LANES][None]
            parts = [piece[h * seq : (h + 1) * seq] for h in range(split)]
            pieces.append(jnp.concatenate(parts, axis=2))
        return jnp.concatenate(pieces, axis=1)

    def short_spec(s):
        turned = []
        for g in range(groups):
            start = s * width + g * LANES
            taps = jnp.concatenate([own_ref[start : start + LANES, :length]] * copies, axis=0)
            turned.append(jnp.concatenate([taps * short_cos, taps * short_sin], axis=1))
        columns = jnp.concatenate([table_ref[:length, : 2 * cols], table_ref[cols : cols + length, : 2 * cols]])
        return dot(jnp.concatenate(turned, axis=0).astype(bf), columns)

    row = lax.broadcasted_iota(jnp.int32, (high, 1), 0)
    weight = jnp.where(row < LANES, scale / whole, 2.0 * scale / whole)
    short_cos, short_sin = cosine[:, :length] * weight, -(sine[:, :length] * weight)

    def combine(s, short, spec):
        gains = own_ref[s * width : (s + 1) * width, length:] * (1.0 / scale)
        gains = jnp.concatenate([gains] * (cols // 128), axis=1)
        shift = jnp.concatenate(
            [gains[g * LANES : (g + 1) * LANES] for g in range(groups) for _ in range(copies)], axis=0
        )
        lr, li = spec[:, :cols] + shift, spec[:, cols:]
        rr, ri = short[:, :cols], short[:, cols:]
        return lr * rr - li * ri, lr * ri + li * rr

    chunks = [chunk(s) for s in range(sections)]
    odd = 2 * width - width // 16 * 16
    longs = [jnp.concatenate([part[:, odd:], part[:, width:odd]], axis=1) for part in chunks]
    if odd == 2 * width:
        longs = [part[:, width:] for part in chunks]
    specs = forward([chunks[0][:, :width], longs[0]])
    signal_spec = specs[:span]
    filters = combine(0, short_spec(0), specs[span:])
    results = []
    for s in range(sections):
        product = times(signal_spec, filters)
        if s + 1 < sections:
            filters = combine(s + 1, short_spec(s + 1), forward([longs[s + 1]]))
        result = back(product)
        results.append(result)
        if s + 1 < sections:
            rounded = result.astype(bf).astype(jnp.float32)
            signal_spec = forward([rounded * chunks[s + 1][:, :width]])
    for at in range(0, len(order), 2):
        pair = [results[rank // seq][rank % seq] for rank in order[at : at + 2]]
        out_ref[at * width : (at + 2) * width] = jnp.concatenate(pair, axis=0).astype(bf)


def body(activations, short_filters, long_filters, skip_gain):
    sections = short_filters.shape[0]
    tokens, channels = activations.shape[1:]
    devices = lax.axis_size(BOTH)
    seq_devices = lax.axis_size("seq")
    owned = channels // devices
    width = -(-owned // LANES) * LANES
    cols = tokens
    laid = devices * width
    order = spread_order(devices)

    def widen(array):
        split = array.reshape(array.shape[:2] + (devices, owned))
        split = jnp.pad(split, ((0, 0), (0, 0), (0, 0), (0, width - owned)))
        return split.reshape(array.shape[:2] + (laid,))

    def exchanged(array, height):
        chunks = array.reshape(devices, height, cols)
        moved = lax.all_to_all(
            chunks, BOTH, split_axis=0, concat_axis=0, tiled=True, axis_index_groups=[list(order)]
        )
        return moved.reshape(devices * height, cols)

    def grant(size):
        return pltpu.CompilerParams(vmem_limit_bytes=int(size))

    acts, filters = activations, long_filters
    if width != owned:
        acts, filters = widen(acts), widen(filters)
    split = 2 if seq_devices <= 32 and cols % 256 == 0 else 1
    table, back_table, turn = tables(seq_devices * split, cols // split, split)
    vmem = pl.BlockSpec(memory_space=pltpu.VMEM)
    hbm = pl.BlockSpec(memory_space=pltpu.HBM)
    area = laid * cols
    span = (seq_devices + 1) * width
    taps = short_filters.shape[1]
    place = lax.axis_index(BOTH).astype(jnp.int32).reshape(1)
    inputs = (acts, filters, short_filters, skip_gain)
    outgoing, own = pl.pallas_call(
        functools.partial(send_kernel, width, owned, order),
        out_shape=(
            jax.ShapeDtypeStruct((2 * laid, cols), jnp.bfloat16),
            jax.ShapeDtypeStruct((sections * width, taps + 128), jnp.float32),
        ),
        in_specs=[pl.BlockSpec(memory_space=pltpu.SMEM)] + [hbm] * 4,
        out_specs=(vmem, vmem),
        scratch_shapes=[
            pltpu.VMEM((cols, laid), jnp.bfloat16),
            pltpu.VMEM((cols, laid), jnp.float32),
            pltpu.VMEM(short_filters.shape, jnp.bfloat16),
            pltpu.VMEM(skip_gain.shape, jnp.float32),
            pltpu.SemaphoreType.DMA((2,)),
            pltpu.SemaphoreType.DMA((2,)),
        ],
        compiler_params=grant(4 * MIB + 24 * area),
    )(place, *(pltpu.with_memory_space_constraint(array, pltpu.HBM) for array in inputs))
    arrived = exchanged(outgoing, 2 * width)
    results = pl.pallas_call(
        functools.partial(main_kernel, width, sections, split, order),
        out_shape=jax.ShapeDtypeStruct((laid, cols), jnp.bfloat16),
        in_specs=[vmem] * 5,
        out_specs=vmem,
        compiler_params=grant(2 * MIB + 6 * area + 2 * table.size + 2 * back_table.size + 64 * span * cols),
    )(arrived, own, turn, table, back_table)
    returned = exchanged(results, width)
    final = pl.pallas_call(
        final_kernel,
        out_shape=jax.ShapeDtypeStruct((1, cols, laid), jnp.bfloat16),
        compiler_params=grant(4 * MIB + 16 * area),
    )(returned)
    if width != owned:
        final = final.reshape(1, cols, devices, width)[..., :owned].reshape(1, cols, channels)
    return final


def solution(mesh):
    return jax.shard_map(
        body,
        mesh=mesh,
        in_specs=(P("segment", "seq", None), P(), P("segment", "seq", None), P()),
        out_specs=P("segment", "seq", None),
        check_vma=False,
    )
```
